32 devices in a mesh: dp: 8 (over z, core), tensor: 4 (over y, x).
Axes of the slice: x: 2, y: 2, z: 4, core: 2. Of those that a mesh axis runs over, the one named last changes fastest.
Arguments:
- tokens: bfloat16 [6144, 3072], P('dp'), may hold values from -6 to 6
- assign: int32 [6144, 2], P('dp'), may hold values from 0 to 7, as said below
- combine: float32 [6144, 2], P('dp'), may hold values from 0.1 to 1
- cotangent: bfloat16 [6144, 3072], P('dp'), may hold values from -6 to 6
- w_gate: bfloat16 [3072, 8192], P('dp', 'tensor'), may hold values from -0.109375 to 0.109375
- w_up: bfloat16 [3072, 8192], P('dp', 'tensor'), may hold values from -0.109375 to 0.109375
- w_down_t: bfloat16 [3072, 8192], P('dp', 'tensor'), may hold values from -0.0625 to 0.0625
Outputs:
- mixed: bfloat16 [6144, 3072], P('dp', 'tensor')
- input_grad: bfloat16 [6144, 3072], P('dp', 'tensor')
- weight_grad: float32 [6144], P('dp')
- gate_weight_grad: bfloat16 [3072, 8192], P('dp', 'tensor')
- up_weight_grad: bfloat16 [3072, 8192], P('dp', 'tensor')
- down_weight_grad: bfloat16 [3072, 8192], P('dp', 'tensor')
The draws below stay inside these ranges and needn't reach their ends.
Inputs may be any that keep to these rules, and one draw needn't show every extreme that they name: `assign`: each token names 2 different experts. Of the 768 tokens of one index of dp at most 384 name expert 0, and in every draw the tokens of some index of dp name it exactly 384 times.
All inputs are finite; a program needn't handle non-finite values.
Results may differ from the reference program's by a relative error of at most 0.028.
Values may be sent and summed in bfloat16 or wider, within the bound.
No kernel may reach another device: no remote copies, remote signals or barrier semaphores. Data moves between devices by JAX's collectives and lax.ppermute only.
A program may use at most 192 MiB of HBM per device.

```python
import jax
import jax.numpy as jnp
from jax import lax

D = 3072
HIDDEN_SIZE = 8192
EXPERTS = 8
TOPK = 2
TOK_DEV = 768
ROWS_CAP = 384
TOKENS = 6144
N_DP = 8
N_TENSOR = 4


def draw_assign(key, part):
    device_total = TOKENS // TOK_DEV
    row_limit = TOK_DEV // 2
    keys = jax.random.split(key, 6)
    routed_counts = jax.random.randint(keys[0], (device_total,), TOK_DEV // 16, row_limit + 1)
    busiest = jax.random.randint(keys[1], (), 0, device_total)
    routed_counts = jnp.where(jnp.arange(device_total) == busiest, row_limit, routed_counts)
    scores = jax.random.randint(keys[2], (device_total, TOK_DEV), 0, 1 << 16) * TOK_DEV
    scores = scores + jnp.arange(TOK_DEV, dtype=jnp.int32)[None, :]
    order = jnp.argsort(scores, axis=1, stable=True)
    ranks = jnp.argsort(order, axis=1, stable=True)
    routed = ranks < routed_counts[:, None]
    other = jax.random.randint(keys[3], (device_total, TOK_DEV), 1, EXPERTS)
    offset = jax.random.randint(keys[4], (device_total, TOK_DEV), 1, EXPERTS - 1)
    second = 1 + (other - 1 + offset) % (EXPERTS - 1)
    slot = jax.random.randint(keys[5], (device_total, TOK_DEV), 0, 2)
    first_col = jnp.where(routed, jnp.where(slot == 0, 0, other), other)
    second_col = jnp.where(routed, jnp.where(slot == 0, other, 0), second)
    return jnp.stack([first_col, second_col], axis=-1).reshape(TOKENS, TOPK).astype(jnp.int32)


def with_spikes(result, own_key, source, target, parts, factor):
    def block_of(position):
        return (jnp.arange(result.shape[position]) // (result.shape[position] // parts)).reshape((-1,) + (1,) * (result.ndim - 1 - position))

    near = jax.random.permutation(own_key, parts)[block_of(target)]
    other_side = (block_of(target) + parts // 2) % parts
    return jnp.where((block_of(source) == near) | (block_of(source) == other_side), factor * result, result)


def block_scale(own_key, shape, shards, least, high):
    level, own = 1.0, jax.random.fold_in(own_key, 6)
    for position, blocks in shards:
        steps = jnp.exp(jax.random.uniform(jax.random.fold_in(own, position), (blocks,), jnp.float32, least / len(shards), high / len(shards)))
        level = level * jnp.repeat(steps, shape[position] // blocks).reshape([-1 if axis == position else 1 for axis in range(len(shape))])
    return level


def centred(stream_key, extent, width, most, cuts=(), kind=jnp.bfloat16):
    values = width * jax.random.normal(stream_key, extent, jnp.float32)
    if cuts:
        values = values * block_scale(stream_key, extent, cuts, -0.22, 0.18)
    return jnp.clip(values, -most, most).astype(kind)


def gaussian_with(own_key, dims, scale, bound, cuts, heavy, kind=jnp.bfloat16):
    entries = scale * jax.random.normal(own_key, dims, jnp.float32)
    if cuts:
        entries = entries * block_scale(own_key, dims, cuts, -0.22, 0.18)
    return jnp.clip(with_spikes(entries, jax.random.fold_in(own_key, 3), *heavy), -bound, bound).astype(kind)


def setup_inputs(seed: int = 0) -> dict:
    arg_keys = jax.random.split(jax.random.key(seed), 8)
    return {
        "tokens": gaussian_with(arg_keys[0], (TOKENS, D), 1.0, 6.0, ((0, 8),), (0, 1, 8, 2.0)),
        "assign": draw_assign(jax.random.fold_in(arg_keys[7], 71), 0),
        "combine": jnp.clip(0.1 + 0.9 * jax.random.uniform(arg_keys[2], (TOKENS, TOPK), jnp.float32) ** block_scale(arg_keys[2], (TOKENS, TOPK), ((0, 8),), -0.2, 0.2), 0.1, 1.0),
        "cotangent": gaussian_with(arg_keys[3], (TOKENS, D), 1.0, 6.0, ((0, 8),), (0, 1, 8, 2.0)),
        "w_gate": centred(arg_keys[4], (D, HIDDEN_SIZE), D ** -0.5, 0.109375, ((0, 8), (1, 4))),
        "w_up": centred(arg_keys[5], (D, HIDDEN_SIZE), D ** -0.5, 0.109375, ((0, 8), (1, 4))),
        "w_down_t": centred(arg_keys[6], (D, HIDDEN_SIZE), HIDDEN_SIZE ** -0.5, 0.0625, ((0, 8), (1, 4))),
    }


def select_rows(assign_block, combine_block, row_limit):
    token_total = assign_block.shape[0]
    expert_hit = assign_block == 0
    routed = jnp.any(expert_hit, axis=1)
    weight = jnp.sum(jnp.where(expert_hit, combine_block, jnp.zeros((), combine_block.dtype)), axis=1)
    place = jnp.cumsum(routed.astype(jnp.int32)) - 1
    match = routed[None, :] & (place[None, :] == jnp.arange(row_limit, dtype=jnp.int32)[:, None])
    positions = jnp.arange(token_total, dtype=jnp.int32)
    row_index = jnp.sum(jnp.where(match, positions[None, :], 0), axis=1).astype(jnp.int32)
    valid = jnp.any(match, axis=1)
    row_weight = jnp.where(valid, weight[row_index], jnp.zeros((), weight.dtype))
    return row_index, valid, row_weight


def grouped_sum(pairs, groups):
    total = None
    for left, right in pairs:
        left_groups = left.astype(jnp.float32).reshape(left.shape[0], groups, -1)
        right_groups = right.astype(jnp.float32).reshape(right.shape[0], groups, -1)
        term = jnp.einsum("rgf,dgf->grd", left_groups, right_groups)
        total = term if total is None else total + term
    rounded = lax.optimization_barrier(total.astype(jnp.bfloat16))
    return jnp.sum(rounded.astype(jnp.float32), axis=0)


def place_rows(rows, valid, row_index, token_total):
    shape = (token_total,) + rows.shape[1:]
    mask = valid.reshape(valid.shape + (1,) * (rows.ndim - 1))
    values = jnp.where(mask, rows.astype(jnp.float32), jnp.zeros((), jnp.float32))
    return jnp.zeros(shape, jnp.float32).at[row_index].add(values)


def reference(tokens, assign, combine, cotangent, w_gate, w_up, w_down_t):
    def device_step(carry, block):
        tok_block, assign_block, combine_block, grad_block = block
        row_index, valid, row_weight = select_rows(assign_block, combine_block, ROWS_CAP)
        keep = valid[:, None]
        rows_in = jnp.where(keep, tok_block[row_index], jnp.zeros((), tok_block.dtype))
        rows_grad = jnp.where(keep, grad_block[row_index], jnp.zeros((), grad_block.dtype))
        gate_pre = jnp.dot(rows_in, w_gate, preferred_element_type=jnp.float32)
        up_pre = jnp.dot(rows_in, w_up, preferred_element_type=jnp.float32)
        sigmoid_gate = jax.nn.sigmoid(gate_pre)
        hidden = (gate_pre * sigmoid_gate * up_pre).astype(jnp.bfloat16)
        expert_sum = grouped_sum(((hidden, w_down_t),), N_TENSOR)
        mixed_rows = (row_weight[:, None] * expert_sum).astype(jnp.bfloat16)
        weight_rows = jnp.sum(rows_grad.astype(jnp.float32) * expert_sum, axis=1)
        out_grad = (row_weight[:, None] * rows_grad.astype(jnp.float32)).astype(jnp.bfloat16)
        hidden_grad = jnp.dot(out_grad, w_down_t, preferred_element_type=jnp.float32)
        gate_grad = (hidden_grad * up_pre * sigmoid_gate * (1.0 + gate_pre * (1.0 - sigmoid_gate))).astype(jnp.bfloat16)
        up_grad = (hidden_grad * gate_pre * sigmoid_gate).astype(jnp.bfloat16)
        input_rows = grouped_sum(((gate_grad, w_gate), (up_grad, w_up)), N_TENSOR).astype(jnp.bfloat16)
        token_total = tok_block.shape[0]
        mixed_block = place_rows(mixed_rows, valid, row_index, token_total).astype(jnp.bfloat16)
        input_block = place_rows(input_rows, valid, row_index, token_total).astype(jnp.bfloat16)
        weight_block = place_rows(weight_rows, valid, row_index, token_total)
        term = jnp.concatenate([
            jnp.dot(rows_in.T, gate_grad, preferred_element_type=jnp.float32),
            jnp.dot(rows_in.T, up_grad, preferred_element_type=jnp.float32),
            jnp.dot(out_grad.T, hidden, preferred_element_type=jnp.float32)], axis=1)
        rounded = lax.optimization_barrier(term.astype(jnp.bfloat16))
        return carry + rounded.astype(jnp.float32), (mixed_block, input_block, weight_block)

    blocks = (tokens.reshape(N_DP, TOK_DEV, D), assign.reshape(N_DP, TOK_DEV, TOPK),
              combine.reshape(N_DP, TOK_DEV, TOPK), cotangent.reshape(N_DP, TOK_DEV, D))
    init = jnp.zeros((D, 3 * HIDDEN_SIZE), jnp.float32)
    grads, outputs = lax.scan(device_step, init, blocks)
    mixed = outputs[0].reshape(TOKENS, D)
    input_grad = outputs[1].reshape(TOKENS, D)
    weight_grad = outputs[2].reshape(TOKENS)
    grads = grads.astype(jnp.bfloat16)
    return (mixed, input_grad, weight_grad, grads[:, :HIDDEN_SIZE], grads[:, HIDDEN_SIZE:2 * HIDDEN_SIZE], grads[:, 2 * HIDDEN_SIZE:])
```

```python
import jax
import jax.numpy as jnp
from jax import lax
from jax.sharding import PartitionSpec as P

BF16 = jnp.bfloat16
F32 = jnp.float32


def dot(left, right, dims):
    return lax.dot_general(left, right, (dims, ((), ())), preferred_element_type=F32)


def mm(left, right):
    return dot(left, right, ((1,), (0,)))


def mm_last(left, right):
    return dot(left, right, ((1,), (1,)))


def mm_first(left, right):
    return dot(left, right, ((0,), (0,)))


def swap(value, axis, distance):
    size = lax.axis_size(axis)
    return lax.ppermute(value, axis, [(i, i ^ distance) for i in range(size)])


def select_rows(assign_block, combine_block, row_limit):
    expert_hit = assign_block == 0
    routed = jnp.any(expert_hit, axis=1)
    weight = jnp.sum(
        jnp.where(expert_hit, combine_block, jnp.zeros((), combine_block.dtype)), axis=1
    )
    place = jnp.cumsum(routed.astype(jnp.int32)) - 1
    match = routed[None, :] & (place[None, :] == jnp.arange(row_limit, dtype=jnp.int32)[:, None])
    row_weight = jnp.sum(jnp.where(match, weight[None, :], 0.0), axis=1)
    return (match, row_weight)


def pick(flag, first, second):
    return jnp.where(flag, first, second)


def halves(value, upper, axis):
    width = value.shape[axis] // 2
    start = upper * width
    mine = lax.dynamic_slice_in_dim(value, start, width, axis)
    other = lax.dynamic_slice_in_dim(value, width - start, width, axis)
    return mine, other


def join(mine, other, upper, axis):
    return pick(
        upper == 0,
        jnp.concatenate([mine, other], axis=axis),
        jnp.concatenate([other, mine], axis=axis),
    )


def gather_tensor(value):
    size = lax.axis_size("tensor")
    me = lax.axis_index("tensor")
    rows, width = value.shape
    full = jnp.zeros((rows, width * size), value.dtype)
    full = lax.dynamic_update_slice_in_dim(full, value, me * width, 1)
    for k in range(1, size):
        full = lax.dynamic_update_slice_in_dim(full, swap(value, "tensor", k), (me ^ k) * width, 1)
    return full


def scatter_tensor(value, bits):
    size = lax.axis_size("tensor")
    me = lax.axis_index("tensor")
    rows, depth = value.shape
    width = depth // size
    def part(k):
        return lax.dynamic_slice_in_dim(value, (me ^ k) * width, width, 1)

    parts = {k: part(k) for k in range(size)}
    for bit in bits:
        gone = [k for k in parts if k & bit]
        kept = [k for k in parts if not k & bit]
        sent = jnp.concatenate([parts[k].astype(BF16) for k in gone], axis=1)
        got = swap(sent, "tensor", bit)
        parts = {
            k: parts[k].astype(F32) + got[:, i * width : (i + 1) * width].astype(F32)
            for i, k in enumerate(kept)
        }
    return parts[0]


def local(tokens, assign, combine, cotangent, w_gate, w_up, w_down_t):
    token_total, depth = tokens.shape
    row_limit = token_total // 2
    n_dp = lax.axis_size("dp")
    n_tensor = lax.axis_size("tensor")
    half = n_dp // 2
    upper = lax.axis_index("dp") // half
    me_t = lax.axis_index("tensor")
    width = depth // n_tensor
    groups = [list(range(half)), list(range(half, n_dp))]
    bits = [1 << i for i in range(n_tensor.bit_length() - 1)]

    def gather_half(value):
        return lax.all_gather(value, "dp", axis=0, tiled=True, axis_index_groups=groups)

    def scatter_half(value):
        return lax.psum_scatter(
            value, "dp", scatter_dimension=0, tiled=True, axis_index_groups=groups
        )

    match, row_weight = select_rows(assign, combine, row_limit)
    hot = match.astype(BF16)
    rows_in = mm(hot, tokens).astype(BF16)
    rows_grad = mm(hot, cotangent).astype(BF16)
    out_grad = (row_weight[:, None] * rows_grad.astype(F32)).astype(BF16)

    def partner_rows(rows):
        mine = lax.dynamic_slice_in_dim(rows, me_t * width, width, 1)
        return gather_tensor(swap(mine, "dp", half))

    both_in = jnp.concatenate([rows_in, partner_rows(rows_in)], axis=0)
    both_out = jnp.concatenate([out_grad, partner_rows(out_grad)], axis=0)
    in_own, in_far = halves(both_in, upper, 1)
    out_own, out_far = halves(both_out, upper, 1)

    def panel(block):
        mine, other = halves(block, upper, 1)
        return gather_half(mine), gather_half(swap(other, "dp", half))

    gate_own, gate_far = panel(w_gate)
    up_own, up_far = panel(w_up)
    down_own, down_far = panel(w_down_t)

    gate_pre = mm(in_own, gate_own) + mm(in_far, gate_far)
    up_pre = mm(in_own, up_own) + mm(in_far, up_far)
    sigmoid_gate = jax.nn.sigmoid(gate_pre)
    hidden = (gate_pre * sigmoid_gate * up_pre).astype(BF16)

    def panel_grad(left_own, left_far, right):
        far = swap(scatter_half(mm_first(left_far, right).astype(BF16)), "dp", half)
        own = scatter_half(mm_first(left_own, right).astype(BF16))
        return join(own, far, upper, 1)

    down_grad = panel_grad(out_own, out_far, hidden)

    hidden_grad = mm(out_own, down_own) + mm(out_far, down_far)
    gate_grad = (
        hidden_grad * up_pre * sigmoid_gate * (1.0 + gate_pre * (1.0 - sigmoid_gate))
    ).astype(BF16)
    up_grad = (hidden_grad * gate_pre * sigmoid_gate).astype(BF16)

    gate_weight_grad = panel_grad(in_own, in_far, gate_grad)
    up_weight_grad = panel_grad(in_own, in_far, up_grad)

    def whole(own, far):
        return join(own.astype(BF16), far.astype(BF16), upper, 1)

    def reduce_rows(value):
        far = scatter_tensor(value[row_limit:], bits)
        got = swap(far.astype(BF16), "dp", half)
        return scatter_tensor(value[:row_limit], bits[::-1]) + got.astype(F32)

    expert_cols = reduce_rows(whole(mm_last(hidden, down_own), mm_last(hidden, down_far)))
    input_cols = reduce_rows(
        whole(
            mm_last(gate_grad, gate_own) + mm_last(up_grad, up_own),
            mm_last(gate_grad, gate_far) + mm_last(up_grad, up_far),
        )
    )

    grad_cols = lax.dynamic_slice_in_dim(rows_grad, me_t * width, width, 1)
    weight_rows = jnp.sum(grad_cols.astype(F32) * expert_cols, axis=1)
    for bit in bits:
        weight_rows = weight_rows + swap(weight_rows, "tensor", bit)
    weight_grad = jnp.sum(jnp.where(match, weight_rows[:, None], 0.0), axis=0)

    mixed = mm_first(hot, (row_weight[:, None] * expert_cols).astype(BF16)).astype(BF16)
    input_grad = mm_first(hot, input_cols.astype(BF16)).astype(BF16)
    return (mixed, input_grad, weight_grad, gate_weight_grad, up_weight_grad, down_grad)


def solution(mesh):
    return jax.shard_map(
        local,
        mesh=mesh,
        in_specs=(
            P("dp", None),
            P("dp", None),
            P("dp", None),
            P("dp", None),
            P("dp", "tensor"),
            P("dp", "tensor"),
            P("dp", "tensor"),
        ),
        out_specs=(
            P("dp", "tensor"),
            P("dp", "tensor"),
            P("dp"),
            P("dp", "tensor"),
            P("dp", "tensor"),
            P("dp", "tensor"),
        ),
        check_vma=False,
    )
```

```python
import jax
import jax.numpy as jnp
from jax import lax
from jax.sharding import PartitionSpec as P

BF16 = jnp.bfloat16
F32 = jnp.float32


def dot(left, right, dims):
    return lax.dot_general(left, right, (dims, ((), ())), preferred_element_type=F32)


def mm(left, right):
    return dot(left, right, ((1,), (0,)))


def mm_last(left, right):
    return dot(left, right, ((1,), (1,)))


def mm_first(left, right):
    return dot(left, right, ((0,), (0,)))


def swap(value, axis, distance):
    size = lax.axis_size(axis)
    return lax.ppermute(value, axis, [(i, i ^ distance) for i in range(size)])


def fence(*values):
    return lax.optimization_barrier(values)


def select_rows(assign_block, combine_block, row_limit):
    expert_hit = assign_block == 0
    routed = jnp.any(expert_hit, axis=1)
    weight = jnp.sum(
        jnp.where(expert_hit, combine_block, jnp.zeros((), combine_block.dtype)), axis=1
    )
    place = jnp.cumsum(routed.astype(jnp.int32)) - 1
    match = routed[None, :] & (place[None, :] == jnp.arange(row_limit, dtype=jnp.int32)[:, None])
    row_weight = jnp.sum(jnp.where(match, weight[None, :], 0.0), axis=1)
    return (match, row_weight)


def halves(value, upper, axis):
    width = value.shape[axis] // 2
    start = upper * width
    mine = lax.dynamic_slice_in_dim(value, start, width, axis)
    other = lax.dynamic_slice_in_dim(value, width - start, width, axis)
    return mine, other


def join(mine, other, upper, axis):
    return jnp.where(
        upper == 0,
        jnp.concatenate([mine, other], axis=axis),
        jnp.concatenate([other, mine], axis=axis),
    )


def columns(value, places, width):
    return jnp.concatenate(
        [lax.dynamic_slice_in_dim(value, p * width, width, 1) for p in places], axis=1
    )


def cat(*values):
    return jnp.concatenate(values, axis=0)


def local(tokens, assign, combine, cotangent, w_gate, w_up, w_down_t):
    token_total, depth = tokens.shape
    row_limit = token_total // 2
    n_dp = lax.axis_size("dp")
    n_tensor = lax.axis_size("tensor")
    me = lax.axis_index("dp")
    me_t = lax.axis_index("tensor")
    far = n_dp // 2
    upper = me // far
    rows_w = w_gate.shape[0]
    width = depth // n_tensor
    mids = [1 << i for i in range(1, far.bit_length() - 1)][::-1]
    t_bits = [1 << i for i in range(n_tensor.bit_length() - 1)]

    own_even = [0]
    for bit in mids:
        own_even = own_even + [k ^ bit for k in own_even]
    even = own_even + [k ^ far for k in own_even]
    odd = [k ^ 1 for k in even]
    n_own = len(own_even)

    def grow(block):
        for bit in mids:
            block = cat(block, swap(block, "dp", bit))
        return block

    def z_far(block):
        return swap(block, "dp", far)

    def core(block):
        return swap(block, "dp", 1)

    (gate_0, gate_1), (up_0, up_1), (down_0, down_1) = (
        halves(w, upper, 1) for w in (w_gate, w_up, w_down_t)
    )
    gate_own = grow(gate_0)
    gate_4 = z_far(gate_1)
    match, row_weight = select_rows(assign, combine, row_limit)
    hot = match.astype(BF16)
    rows_in = mm(hot, tokens).astype(BF16)
    rows_grad = mm(hot, cotangent).astype(BF16)
    out_grad = (row_weight[:, None] * rows_grad.astype(F32)).astype(BF16)
    quarter = jnp.concatenate(
        [lax.dynamic_slice_in_dim(v, me_t * width, width, 1) for v in (rows_in, out_grad)], axis=1
    )
    gate_own, gate_4, rows_in, out_grad, quarter, up_0 = fence(
        gate_own, gate_4, rows_in, out_grad, quarter, up_0
    )

    quarter = z_far(quarter)
    gate_far = grow(gate_4)
    up_own = grow(up_0)
    quarter, gate_far, up_own, up_1, down_0 = fence(quarter, gate_far, up_own, up_1, down_0)

    quarters = [quarter] + [swap(quarter, "tensor", k) for k in range(1, n_tensor)]
    up_4 = z_far(up_1)
    down_own = grow(down_0)
    gate_even = cat(gate_own, gate_far)
    gate_odd = core(gate_even)
    *quarters, up_4, down_own, gate_odd, down_1 = fence(
        *quarters, up_4, down_own, gate_odd, down_1
    )

    def rows_far(part):
        wide = jnp.concatenate(
            [q[:, part * width : (part + 1) * width] for q in quarters], axis=1
        )
        return columns(wide, [me_t ^ k for k in range(n_tensor)], width)

    def relative(value, order):
        return columns(value, [me ^ k for k in order], rows_w)

    both_in = cat(rows_in, rows_far(0))
    both_out = cat(out_grad, rows_far(1))
    in_even, in_odd = relative(both_in, even), relative(both_in, odd)
    out_even, out_odd = relative(both_out, even), relative(both_out, odd)
    down_4 = z_far(down_1)
    up_far = grow(up_4)
    gate_pre = mm(in_even, gate_even) + mm(in_odd, gate_odd)
    down_4, up_far, gate_pre = fence(down_4, up_far, gate_pre)

    up_even = cat(up_own, up_far)
    up_odd = core(up_even)
    down_far = grow(down_4)
    up_pre_even = mm(in_even, up_even)
    up_odd, down_far, up_pre_even = fence(up_odd, down_far, up_pre_even)

    down_even = cat(down_own, down_far)
    down_odd = core(down_even)
    up_pre = up_pre_even + mm(in_odd, up_odd)
    sigmoid_gate = jax.nn.sigmoid(gate_pre)
    hidden = (gate_pre * sigmoid_gate * up_pre).astype(BF16)
    g_down_odd = mm_first(out_odd, hidden).astype(BF16)
    hidden_grad_even = mm(out_even, down_even)
    down_odd, g_down_odd, hidden, hidden_grad_even = fence(
        down_odd, g_down_odd, hidden, hidden_grad_even
    )

    g_down_got = core(g_down_odd)
    hidden_grad = hidden_grad_even + mm(out_odd, down_odd)
    gate_grad = (
        hidden_grad * up_pre * sigmoid_gate * (1.0 + gate_pre * (1.0 - sigmoid_gate))
    ).astype(BF16)
    up_grad = (hidden_grad * gate_pre * sigmoid_gate).astype(BF16)
    g_down_got, gate_grad, up_grad = fence(g_down_got, gate_grad, up_grad)

    def even_grad(left, right, got):
        return (mm_first(left, right) + got.astype(F32)).astype(BF16)

    def shrink(value):
        for bit in mids[::-1]:
            size = value.shape[0] // 2
            got = swap(value[size:], "dp", bit)
            value = (value[:size].astype(F32) + got.astype(F32)).astype(BF16)
        return value

    cut = n_own * rows_w

    g_down = even_grad(out_even, hidden, g_down_got)
    g_down_own, g_down_4 = shrink(g_down[:cut]), shrink(g_down[cut:])
    g_gate_odd = mm_first(in_odd, gate_grad).astype(BF16)
    g_up_odd = mm_first(in_odd, up_grad).astype(BF16)

    def true_order(even_part, odd_part):
        whole = jnp.concatenate([even_part.astype(BF16), odd_part.astype(BF16)], axis=1)
        order = even + odd
        place = [order.index(k) for k in range(n_dp)]
        table = jnp.array(place, jnp.int32)
        return columns(whole, [table[me ^ b] for b in range(n_dp)], rows_w)

    expert_part = true_order(mm_last(hidden, down_even), mm_last(hidden, down_odd))
    g_down_own, g_down_4, g_gate_odd, g_up_odd, expert_part = fence(
        g_down_own, g_down_4, g_gate_odd, g_up_odd, expert_part
    )

    def split_parts(value):
        return {
            k: lax.dynamic_slice_in_dim(value, (me_t ^ k) * width, width, 1)
            for k in range(n_tensor)
        }

    def tensor_step(parts, bit):
        gone = [k for k in parts if k & bit]
        kept = [k for k in parts if not k & bit]
        got = swap(jnp.concatenate([parts[k] for k in gone], axis=1), "tensor", bit)
        return {
            k: (parts[k].astype(F32) + got[:, i * width : (i + 1) * width].astype(F32)).astype(BF16)
            for i, k in enumerate(kept)
        }

    def steps_1(value):
        near, away = split_parts(value[:row_limit]), split_parts(value[row_limit:])
        return tensor_step(near, t_bits[0]), tensor_step(away, t_bits[-1])

    def steps_2(near, away):
        for bit in t_bits[1:]:
            near = tensor_step(near, bit)
        for bit in t_bits[:-1][::-1]:
            away = tensor_step(away, bit)
        return near[0], away[0]

    g_down_far = z_far(g_down_4)
    g_gate_got = core(g_gate_odd)
    g_up_got = core(g_up_odd)
    expert_near, expert_away = steps_1(expert_part)
    input_part = true_order(
        mm_last(gate_grad, gate_even) + mm_last(up_grad, up_even),
        mm_last(gate_grad, gate_odd) + mm_last(up_grad, up_odd),
    )
    g_down_far, g_gate_got, g_up_got, expert_near, expert_away, input_part = fence(
        g_down_far, g_gate_got, g_up_got, expert_near, expert_away, input_part
    )

    g_gate = even_grad(in_even, gate_grad, g_gate_got)
    g_gate_own, g_gate_4 = shrink(g_gate[:cut]), shrink(g_gate[cut:])
    g_up = even_grad(in_even, up_grad, g_up_got)
    expert_near, expert_away = steps_2(expert_near, expert_away)
    input_near, input_away = steps_1(input_part)
    (g_gate_own, g_gate_4, g_up, expert_near, expert_away, input_near, input_away) = fence(
        g_gate_own, g_gate_4, g_up, expert_near, expert_away, input_near, input_away
    )

    g_gate_far = z_far(g_gate_4)
    g_up_own, g_up_4 = shrink(g_up[:cut]), shrink(g_up[cut:])
    expert_got = z_far(expert_away)
    input_near, input_away = steps_2(input_near, input_away)
    g_gate_far, g_up_own, g_up_4, expert_got, input_near, input_away = fence(
        g_gate_far, g_up_own, g_up_4, expert_got, input_near, input_away
    )

    g_up_far = z_far(g_up_4)
    input_got = z_far(input_away)
    expert_cols = expert_near.astype(F32) + expert_got.astype(F32)
    grad_cols = lax.dynamic_slice_in_dim(rows_grad, me_t * width, width, 1)
    weight_rows = jnp.sum(grad_cols.astype(F32) * expert_cols, axis=1)
    for bit in t_bits:
        weight_rows = weight_rows + swap(weight_rows, "tensor", bit)
    weight_grad = jnp.sum(jnp.where(match, weight_rows[:, None], 0.0), axis=0)
    mixed = mm_first(hot, (row_weight[:, None] * expert_cols).astype(BF16)).astype(BF16)
    input_cols = (input_near.astype(F32) + input_got.astype(F32)).astype(BF16)
    input_grad = mm_first(hot, input_cols).astype(BF16)
    return (
        mixed,
        input_grad,
        weight_grad,
        join(g_gate_own, g_gate_far, upper, 1),
        join(g_up_own, g_up_far, upper, 1),
        join(g_down_own, g_down_far, upper, 1),
    )


def solution(mesh):
    return jax.shard_map(
        local,
        mesh=mesh,
        in_specs=(
            P("dp", None),
            P("dp", None),
            P("dp", None),
            P("dp", None),
            P("dp", "tensor"),
            P("dp", "tensor"),
            P("dp", "tensor"),
        ),
        out_specs=(
            P("dp", "tensor"),
            P("dp", "tensor"),
            P("dp"),
            P("dp", "tensor"),
            P("dp", "tensor"),
            P("dp", "tensor"),
        ),
        check_vma=False,
    )
```

```python
import jax
import jax.numpy as jnp
from jax import lax
from jax.sharding import PartitionSpec as P

BF16 = jnp.bfloat16
F32 = jnp.float32


def dot(left, right, dims):
    return lax.dot_general(left, right, (dims, ((), ())), preferred_element_type=F32)


def mm(left, right):
    return dot(left, right, ((1,), (0,)))


def mm_last(left, right):
    return dot(left, right, ((1,), (1,)))


def mm_first(left, right):
    return dot(left, right, ((0,), (0,)))


def swap(value, axis, distance):
    size = lax.axis_size(axis)
    return lax.ppermute(value, axis, [(i, i ^ distance) for i in range(size)])


def fence(*values):
    return lax.optimization_barrier(values)


def select_rows(assign_block, combine_block, row_limit):
    expert_hit = assign_block == 0
    routed = jnp.any(expert_hit, axis=1)
    weight = jnp.sum(
        jnp.where(expert_hit, combine_block, jnp.zeros((), combine_block.dtype)), axis=1
    )
    place = jnp.cumsum(routed.astype(jnp.int32)) - 1
    match = routed[None, :] & (place[None, :] == jnp.arange(row_limit, dtype=jnp.int32)[:, None])
    row_weight = jnp.sum(jnp.where(match, weight[None, :], 0.0), axis=1)
    return (match, row_weight)


def join(mine, other, upper, axis):
    return jnp.where(
        upper == 0,
        jnp.concatenate([mine, other], axis=axis),
        jnp.concatenate([other, mine], axis=axis),
    )


def cat(*values):
    return jnp.concatenate(values, axis=0)


def beside(*values):
    return jnp.concatenate(values, axis=1)


def local(tokens, assign, combine, cotangent, w_gate, w_up, w_down_t):
    token_total, depth = tokens.shape
    row_limit = token_total // 2
    n_dp = lax.axis_size("dp")
    n_tensor = lax.axis_size("tensor")
    me = lax.axis_index("dp")
    me_t = lax.axis_index("tensor")
    chip, core = me // 2, me % 2
    far = n_dp // 2
    upper = me // far
    rows_w = w_gate.shape[0]
    pair = 2 * rows_w
    n_chip = n_dp // 2
    hid = w_gate.shape[1] // 4
    width = depth // n_tensor
    half = depth // 2
    mids = [1 << i for i in range(1, far.bit_length() - 1)]
    t_bits = [1 << i for i in range(n_tensor.bit_length() - 1)]

    def z_far(block):
        return swap(block, "dp", far)

    def across(block):
        return swap(block, "dp", 1)

    def grow(block):
        for bit in mids:
            block = cat(block, swap(block, "dp", bit))
        return block

    def shrink(value):
        for bit in mids[::-1]:
            size = value.shape[0] // 2
            got = swap(value[size:], "dp", bit)
            value = (value[:size].astype(F32) + got.astype(F32)).astype(BF16)
        return value

    def part(w, u, c):
        return lax.dynamic_slice_in_dim(w, (u * 2 + c) * hid, hid, 1)

    def to_sibling(w):
        return beside(part(w, upper, 1 - core), part(w, 1 - upper, 1 - core))

    def pair_rows(w, got):
        mine = join(part(w, upper, core), got[:, :hid], core, 0)
        other = join(part(w, 1 - upper, core), got[:, hid:], core, 0)
        return mine, other

    wide = 2 * hid
    gate_0 = lax.dynamic_slice_in_dim(w_gate, upper * wide, wide, 1)
    gate_4 = z_far(lax.dynamic_slice_in_dim(w_gate, (1 - upper) * wide, wide, 1))
    gate_own = grow(gate_0)
    match, row_weight = select_rows(assign, combine, row_limit)
    hot = match.astype(BF16)
    rows_in = mm(hot, tokens).astype(BF16)
    rows_grad = mm(hot, cotangent).astype(BF16)
    out_grad = (row_weight[:, None] * rows_grad.astype(F32)).astype(BF16)
    quarter = beside(
        *(lax.dynamic_slice_in_dim(v, me_t * width, width, 1) for v in (rows_in, out_grad))
    )
    near = jnp.zeros((2 * row_limit, depth), BF16)
    for i, value in enumerate((rows_in, out_grad)):
        for j in range(n_chip):
            block = lax.dynamic_slice_in_dim(value, (chip ^ j) * pair, pair, 1)
            near = lax.dynamic_update_slice(near, block, (i * row_limit, j * pair))
    send = cat(to_sibling(w_up), to_sibling(w_down_t))
    gate_4, gate_own, quarter, near, send = fence(gate_4, gate_own, quarter, near, send)

    quarter = z_far(quarter)
    gate_far = grow(gate_4)
    near_sib = across(near)
    got = across(send)
    up_0, up_1 = pair_rows(w_up, got[:rows_w])
    down_0, down_1 = pair_rows(w_down_t, got[rows_w:])
    quarter, gate_far, near_sib, up_0, up_1, down_0, down_1 = fence(
        quarter, gate_far, near_sib, up_0, up_1, down_0, down_1
    )

    up_4 = z_far(up_1)
    own = grow(beside(up_0, down_0))
    quarters = [quarter] + [swap(quarter, "tensor", k) for k in range(1, n_tensor)]
    gate_all = cat(gate_own, gate_far)
    gate_mine = lax.dynamic_slice_in_dim(gate_all, core * hid, hid, 1)
    gate_send = lax.dynamic_slice_in_dim(gate_all, (1 - core) * hid, hid, 1)
    up_4, own, gate_mine, gate_send, down_1, *quarters = fence(
        up_4, own, gate_mine, gate_send, down_1, *quarters
    )
    up_own, down_own = own[:, :hid], own[:, hid:]

    up_far = grow(up_4)
    down_4 = z_far(down_1)
    gate = join(
        gate_mine.reshape(n_chip, rows_w, hid),
        across(gate_send).reshape(n_chip, rows_w, hid),
        core,
        1,
    ).reshape(depth, hid)
    away = jnp.zeros((2 * row_limit, depth), BF16)
    for i in range(2):
        for k, piece in enumerate(quarters):
            for q in range(width // pair):
                block = piece[:, i * width + q * pair : i * width + (q + 1) * pair]
                place = ((me_t ^ k) * (width // pair) + q) ^ chip
                away = lax.dynamic_update_slice(away, block, (i * row_limit, place * pair))
    away_sib = across(away)
    in_all = cat(near[:row_limit], away[:row_limit], near_sib[:row_limit], away_sib[:row_limit])
    gate_pre = mm(in_all, gate)
    up_far, down_4, in_all, gate_pre, away, away_sib, gate = fence(
        up_far, down_4, in_all, gate_pre, away, away_sib, gate
    )

    down_far = grow(down_4)
    up = cat(up_own, up_far)
    out_all = cat(near[row_limit:], away[row_limit:], near_sib[row_limit:], away_sib[row_limit:])
    up_pre = mm(in_all, up)
    sigmoid_gate = jax.nn.sigmoid(gate_pre)
    hidden = (gate_pre * sigmoid_gate * up_pre).astype(BF16)
    g_down = mm_first(out_all, hidden).astype(BF16)
    g_down, hidden, up_pre, down_far, out_all, up = fence(
        g_down, hidden, up_pre, down_far, out_all, up
    )

    g_down_4 = shrink(g_down[half:])
    g_down_own = shrink(g_down[:half])
    down = cat(down_own, down_far)
    hidden_grad = mm(out_all, down)
    gate_grad = (
        hidden_grad * up_pre * sigmoid_gate * (1.0 + gate_pre * (1.0 - sigmoid_gate))
    ).astype(BF16)
    up_grad = (hidden_grad * gate_pre * sigmoid_gate).astype(BF16)
    g_gate = mm_first(in_all, gate_grad).astype(BF16)
    g_up = mm_first(in_all, up_grad).astype(BF16)
    table = 2 * row_limit
    expert_got = across(mm_last(hidden[table:], down).astype(BF16))
    g_down_4, g_down_own, down, gate_grad, up_grad, g_gate, g_up, expert_got = fence(
        g_down_4, g_down_own, down, gate_grad, up_grad, g_gate, g_up, expert_got
    )

    def features(value, rank):
        count = width // pair
        return beside(
            *(
                lax.dynamic_slice_in_dim(value, ((rank * count + q) ^ chip) * pair, pair, 1)
                for q in range(count)
            )
        )

    def split_parts(value):
        return {k: features(value, me_t ^ k) for k in range(n_tensor)}

    def tensor_step(parts, bit):
        gone = [k for k in parts if k & bit]
        kept = [k for k in parts if not k & bit]
        got = swap(beside(*(parts[k] for k in gone)), "tensor", bit)
        return {
            k: (parts[k].astype(F32) + got[:, i * width : (i + 1) * width].astype(F32)).astype(BF16)
            for i, k in enumerate(kept)
        }

    def steps_1(value):
        return (
            tensor_step(split_parts(value[:row_limit]), t_bits[0]),
            tensor_step(split_parts(value[row_limit:]), t_bits[-1]),
        )

    def steps_2(mine, other):
        for bit in t_bits[1:]:
            mine = tensor_step(mine, bit)
        for bit in t_bits[:-1][::-1]:
            other = tensor_step(other, bit)
        return mine[0], other[0]

    def panel(own, other):
        both = beside(own, other)
        mine = lax.dynamic_slice_in_dim(both, core * rows_w, rows_w, 0)
        got = across(lax.dynamic_slice_in_dim(both, (1 - core) * rows_w, rows_w, 0))
        whole = jnp.zeros((rows_w, 4 * hid), BF16)
        for block, u, c in (
            (mine[:, :hid], upper, core),
            (mine[:, hid:], 1 - upper, core),
            (got[:, :hid], upper, 1 - core),
            (got[:, hid:], 1 - upper, 1 - core),
        ):
            whole = lax.dynamic_update_slice(whole, block, (0, (u * 2 + c) * hid))
        return whole

    g_down_far = z_far(g_down_4)
    g_gate_4 = shrink(g_gate[half:])
    expert_sum = (mm_last(hidden[:table], down) + expert_got.astype(F32)).astype(BF16)
    expert_mine, expert_other = steps_2(*steps_1(expert_sum))
    input_got = across(
        (mm_last(gate_grad[table:], gate) + mm_last(up_grad[table:], up)).astype(BF16)
    )
    input_sum = (
        mm_last(gate_grad[:table], gate)
        + mm_last(up_grad[:table], up)
        + input_got.astype(F32)
    ).astype(BF16)
    g_down_far, g_gate_4, expert_mine, expert_other, input_sum, g_gate, g_up = fence(
        g_down_far, g_gate_4, expert_mine, expert_other, input_sum, g_gate, g_up
    )

    g_gate_far = z_far(g_gate_4)
    g_up_4 = shrink(g_up[half:])
    input_mine, input_other = steps_1(input_sum)
    down_out = panel(g_down_own, g_down_far)
    g_gate_far, g_up_4, input_mine, input_other, g_gate, g_up, down_out = fence(
        g_gate_far, g_up_4, input_mine, input_other, g_gate, g_up, down_out
    )

    g_up_far = z_far(g_up_4)
    g_gate_own = shrink(g_gate[:half])
    expert_got = z_far(expert_other)
    input_mine, input_other = steps_2(input_mine, input_other)
    g_up_far, g_gate_own, expert_got, input_mine, input_other, g_up = fence(
        g_up_far, g_gate_own, expert_got, input_mine, input_other, g_up
    )

    g_up_own = shrink(g_up[:half])
    input_got = z_far(input_other)
    expert_cols = expert_mine.astype(F32) + expert_got.astype(F32)
    grad_cols = lax.dynamic_slice_in_dim(rows_grad, me_t * width, width, 1)
    weight_rows = jnp.sum(grad_cols.astype(F32) * expert_cols, axis=1)
    for bit in t_bits:
        weight_rows = weight_rows + swap(weight_rows, "tensor", bit)
    weight_grad = jnp.sum(jnp.where(match, weight_rows[:, None], 0.0), axis=0)
    mixed = mm_first(hot, (row_weight[:, None] * expert_cols).astype(BF16)).astype(BF16)
    input_cols = (input_mine.astype(F32) + input_got.astype(F32)).astype(BF16)
    input_grad = mm_first(hot, input_cols).astype(BF16)
    return (
        mixed,
        input_grad,
        weight_grad,
        panel(g_gate_own, g_gate_far),
        panel(g_up_own, g_up_far),
        down_out,
    )


def solution(mesh):
    return jax.shard_map(
        local,
        mesh=mesh,
        in_specs=(
            P("dp", None),
            P("dp", None),
            P("dp", None),
            P("dp", None),
            P("dp", "tensor"),
            P("dp", "tensor"),
            P("dp", "tensor"),
        ),
        out_specs=(
            P("dp", "tensor"),
            P("dp", "tensor"),
            P("dp"),
            P("dp", "tensor"),
            P("dp", "tensor"),
            P("dp", "tensor"),
        ),
        check_vma=False,
    )
```

```python
import jax
import jax.numpy as jnp
from jax import lax
from jax.sharding import PartitionSpec as P

BF16 = jnp.bfloat16
F32 = jnp.float32


def dot(left, right, dims):
    return lax.dot_general(left, right, (dims, ((), ())), preferred_element_type=F32)


def mm(left, right):
    return dot(left, right, ((1,), (0,)))


def mm_last(left, right):
    return dot(left, right, ((1,), (1,)))


def mm_first(left, right):
    return dot(left, right, ((0,), (0,)))


def swap(value, axis, distance):
    size = lax.axis_size(axis)
    return lax.ppermute(value, axis, [(i, i ^ distance) for i in range(size)])


def fence(*values):
    return lax.optimization_barrier(values)


def select_rows(assign_block, combine_block, row_limit):
    expert_hit = assign_block == 0
    routed = jnp.any(expert_hit, axis=1)
    weight = jnp.sum(
        jnp.where(expert_hit, combine_block, jnp.zeros((), combine_block.dtype)), axis=1
    )
    place = jnp.cumsum(routed.astype(jnp.int32)) - 1
    match = routed[None, :] & (place[None, :] == jnp.arange(row_limit, dtype=jnp.int32)[:, None])
    row_weight = jnp.sum(jnp.where(match, weight[None, :], 0.0), axis=1)
    return (match, row_weight)


def cat(*values):
    return jnp.concatenate(values, axis=0)


def beside(*values):
    return jnp.concatenate(values, axis=1)


def by_bits(blocks, index):
    bit = 1
    while bit < len(blocks):
        flag = (index & bit) != 0
        blocks = [jnp.where(flag, blocks[p ^ bit], blocks[p]) for p in range(len(blocks))]
        bit *= 2
    return blocks


def local(tokens, assign, combine, cotangent, w_gate, w_up, w_down_t):
    token_total, depth = tokens.shape
    row_limit = token_total // 2
    n_dp = lax.axis_size("dp")
    n_tensor = lax.axis_size("tensor")
    me = lax.axis_index("dp")
    me_t = lax.axis_index("tensor")
    chip, core = me // 2, me % 2
    far = n_dp // 2
    upper = me // far
    rows_w = w_gate.shape[0]
    pair = 2 * rows_w
    n_chip = n_dp // 2
    hid = w_gate.shape[1] // 4
    width = depth // n_tensor
    mids = [1 << i for i in range(1, far.bit_length() - 1)]
    t_bits = [1 << i for i in range(n_tensor.bit_length() - 1)]

    def z_far(block):
        return swap(block, "dp", far)

    def across(block):
        return swap(block, "dp", 1)

    def grow(block):
        for bit in mids:
            block = cat(block, swap(block, "dp", bit))
        return block

    def whole_panel(own, away):
        full = jnp.zeros((n_chip,) + own.shape[1:], BF16)
        for j in range(n_chip // 2):
            full = lax.dynamic_update_index_in_dim(full, own[j], chip ^ j, 0)
            full = lax.dynamic_update_index_in_dim(full, away[j], chip ^ j ^ (n_chip // 2), 0)
        return full.reshape(depth, hid)

    def block_of(panel, j):
        return lax.dynamic_index_in_dim(panel.reshape(n_chip, pair, hid), chip ^ j, 0, False)

    def blocks_own(panel):
        return {j: block_of(panel, j) for j in range(n_chip // 2)}

    def blocks_far(panel):
        return {j: block_of(panel, j ^ (n_chip // 2)) for j in range(n_chip // 2)}

    def shrink(blocks):
        for bit in mids[::-1]:
            gone = [j for j in blocks if j & (bit // 2)]
            kept = [j for j in blocks if not j & (bit // 2)]
            got = swap(cat(*(blocks[j] for j in gone)), "dp", bit)
            blocks = {
                j: (blocks[j].astype(F32) + got[i * pair : (i + 1) * pair].astype(F32)).astype(BF16)
                for i, j in enumerate(kept)
            }
        return blocks[0]

    def part(w, u, c):
        return lax.dynamic_slice_in_dim(w, (u * 2 + c) * hid, hid, 1)

    def to_sibling(w):
        return beside(part(w, upper, 1 - core), part(w, 1 - upper, 1 - core))

    def by_core(mine, got):
        return jnp.where(core == 0, cat(mine, got), cat(got, mine))

    def pair_rows(w, got):
        mine = by_core(part(w, upper, core), got[:, :hid])
        other = by_core(part(w, 1 - upper, core), got[:, hid:])
        return mine, other

    gate_0 = lax.dynamic_slice_in_dim(w_gate, upper * 2 * hid, 2 * hid, 1)
    gate_4 = z_far(lax.dynamic_slice_in_dim(w_gate, (1 - upper) * 2 * hid, 2 * hid, 1))
    gate_own = grow(gate_0[None])
    match, row_weight = select_rows(assign, combine, row_limit)
    hot = match.astype(BF16)
    rows_in = mm(hot, tokens).astype(BF16)
    rows_grad = mm(hot, cotangent).astype(BF16)
    out_grad = (row_weight[:, None] * rows_grad.astype(F32)).astype(BF16)
    quarter = cat(
        *(lax.dynamic_slice_in_dim(v, me_t * width, width, 1) for v in (rows_in, out_grad))
    )
    send = cat(to_sibling(w_up), to_sibling(w_down_t))
    gate_4, gate_own, quarter, rows_in, out_grad, send = fence(
        gate_4, gate_own, quarter, rows_in, out_grad, send
    )

    quarter = z_far(quarter)
    gate_far = grow(gate_4[None])
    in_sib, out_sib = across(rows_in), across(out_grad)
    got = across(send)
    up_0, up_1 = pair_rows(w_up, got[:rows_w])
    down_0, down_1 = pair_rows(w_down_t, got[rows_w:])
    own = beside(up_0, down_0)[None]
    quarter, gate_far, in_sib, out_sib, own, up_1, down_1 = fence(
        quarter, gate_far, in_sib, out_sib, own, up_1, down_1
    )

    up_4 = z_far(up_1)
    own = grow(own)
    quarters = [quarter] + [swap(quarter, "tensor", k) for k in range(1, n_tensor)]
    gate_all = cat(gate_own, gate_far)
    gate_mine = lax.dynamic_slice_in_dim(gate_all, core * hid, hid, 2)
    gate_send = lax.dynamic_slice_in_dim(gate_all, (1 - core) * hid, hid, 2)
    up_4, own, gate_mine, gate_send, down_1, *quarters = fence(
        up_4, own, gate_mine, gate_send, down_1, *quarters
    )
    up_own, down_own = own[:, :, :hid], own[:, :, hid:]

    up_far = grow(up_4[None])
    down_4 = z_far(down_1)
    gate_got = across(gate_send)
    gate = jnp.zeros((n_chip, 2, rows_w, hid), BF16)
    for j in range(n_chip):
        gate = lax.dynamic_update_slice(gate, gate_mine[j][None, None], (chip ^ j, core, 0, 0))
        gate = lax.dynamic_update_slice(gate, gate_got[j][None, None], (chip ^ j, 1 - core, 0, 0))
    gate = gate.reshape(depth, hid)

    def true_rows(first):
        return beside(*by_bits([q[first : first + row_limit] for q in quarters], me_t))

    in_away, out_away = true_rows(0), true_rows(row_limit)
    in_away_sib, out_away_sib = across(in_away), across(out_away)
    in_all = cat(rows_in, in_away, in_sib, in_away_sib)
    gate_pre = mm(in_all, gate)
    up_far, down_4, in_all, gate_pre, out_away, out_away_sib, gate, up_own, down_own = fence(
        up_far, down_4, in_all, gate_pre, out_away, out_away_sib, gate, up_own, down_own
    )

    down_far = grow(down_4[None])
    up = whole_panel(up_own, up_far)
    out_all = cat(out_grad, out_away, out_sib, out_away_sib)
    up_pre = mm(in_all, up)
    sigmoid_gate = jax.nn.sigmoid(gate_pre)
    hidden = (gate_pre * sigmoid_gate * up_pre).astype(BF16)
    g_down = mm_first(out_all, hidden).astype(BF16)
    g_down, hidden, up_pre, down_far, out_all, up = fence(
        g_down, hidden, up_pre, down_far, out_all, up
    )

    table = 2 * row_limit
    g_down_4 = shrink(blocks_far(g_down))
    g_down_own = shrink(blocks_own(g_down))
    down = whole_panel(down_own, down_far)
    hidden_grad = mm(out_all, down)
    gate_grad = (
        hidden_grad * up_pre * sigmoid_gate * (1.0 + gate_pre * (1.0 - sigmoid_gate))
    ).astype(BF16)
    up_grad = (hidden_grad * gate_pre * sigmoid_gate).astype(BF16)
    g_gate = mm_first(in_all, gate_grad).astype(BF16)
    expert_sib = mm_last(hidden[table:], down).astype(BF16)

    def input_part(rows):
        return mm_last(gate_grad[rows], gate) + mm_last(up_grad[rows], up)

    input_sib = input_part(slice(table, None)).astype(BF16)
    g_down_4, g_down_own, down, gate_grad, up_grad, g_gate, expert_sib, input_sib = fence(
        g_down_4, g_down_own, down, gate_grad, up_grad, g_gate, expert_sib, input_sib
    )

    g_down_far = z_far(g_down_4)
    g_gate_4 = shrink(blocks_far(g_gate))
    expert_got, input_got = across(expert_sib), across(input_sib)
    g_up = mm_first(in_all, up_grad).astype(BF16)
    expert_sum = (mm_last(hidden[:table], down) + expert_got.astype(F32)).astype(BF16)
    input_sum = (input_part(slice(None, table)) + input_got.astype(F32)).astype(BF16)

    def split_parts(value):
        return {
            k: lax.dynamic_slice_in_dim(value, (me_t ^ k) * width, width, 1)
            for k in range(n_tensor)
        }

    def gone(parts, bit):
        return beside(*(parts[k] for k in parts if k & bit))

    def kept(parts, bit, got):
        keep = [k for k in parts if not k & bit]
        return {
            k: (parts[k].astype(F32) + got[:, i * width : (i + 1) * width].astype(F32)).astype(BF16)
            for i, k in enumerate(keep)
        }

    def step(parts, bit):
        return kept(parts, bit, swap(gone(parts, bit), "tensor", bit))

    def split_rows(value):
        return split_parts(value[:row_limit]), split_parts(value[row_limit:])

    def flat(parts):
        return [parts[k] for k in parts]

    expert_mine, expert_other = split_rows(expert_sum)
    g_down_far, g_gate_4, input_sum, g_gate, g_up, expert_mine, expert_other = fence(
        g_down_far, g_gate_4, input_sum, g_gate, g_up, expert_mine, expert_other
    )

    def panel(own, other):
        both = beside(own, other)
        mine = lax.dynamic_slice_in_dim(both, core * rows_w, rows_w, 0)
        got = across(lax.dynamic_slice_in_dim(both, (1 - core) * rows_w, rows_w, 0))
        whole = jnp.zeros((rows_w, 4 * hid), BF16)
        for block, u, c in (
            (mine[:, :hid], upper, core),
            (mine[:, hid:], 1 - upper, core),
            (got[:, :hid], upper, 1 - core),
            (got[:, hid:], 1 - upper, 1 - core),
        ):
            whole = lax.dynamic_update_slice(whole, block, (0, (u * 2 + c) * hid))
        return whole

    g_gate_far = z_far(g_gate_4)
    g_up_4 = shrink(blocks_far(g_up))
    low, high = t_bits[0], t_bits[-1]
    expert_mine = step(expert_mine, low)
    expert_other = step(expert_other, high)
    input_mine, input_other = split_rows(input_sum)
    down_out = panel(g_down_own, g_down_far)
    (g_gate_far, g_up_4, expert_mine, expert_other, input_mine, input_other, g_gate, g_up, down_out) = (
        fence(
            g_gate_far, g_up_4, expert_mine, expert_other, input_mine, input_other, g_gate, g_up, down_out
        )
    )

    g_up_far = z_far(g_up_4)
    g_gate_own = shrink(blocks_own(g_gate))
    for i, bit in enumerate(t_bits[1:]):
        back = t_bits[-2 - i]
        if i == 0:
            cut = len(expert_mine) // 2 * width
            got_high = swap(
                beside(gone(expert_mine, high), gone(input_other, high)), "tensor", high
            ) if bit == high else None
            got_low = swap(
                beside(gone(expert_other, low), gone(input_mine, low)), "tensor", low
            ) if back == low else None
            if got_high is None:
                expert_mine = step(expert_mine, bit)
                input_other = step(input_other, high)
                expert_other = step(expert_other, back)
                input_mine = step(input_mine, low)
            else:
                expert_mine = kept(expert_mine, high, got_high[:, :cut])
                input_other = kept(input_other, high, got_high[:, cut:])
                expert_other = kept(expert_other, low, got_low[:, :cut])
                input_mine = kept(input_mine, low, got_low[:, cut:])
        else:
            expert_mine = step(expert_mine, bit)
            expert_other = step(expert_other, back)
    g_up_far, g_gate_own, expert_mine, expert_other, input_mine, input_other, g_up = fence(
        g_up_far, g_gate_own, expert_mine[0], expert_other[0], input_mine, input_other, g_up
    )

    g_up_own = shrink(blocks_own(g_up))
    expert_got = z_far(expert_other)
    for bit in t_bits[1:]:
        input_mine = step(input_mine, bit)
    for bit in t_bits[:-1][::-1]:
        input_other = step(input_other, bit)
    g_up_own, expert_got, input_mine, input_other = fence(
        g_up_own, expert_got, input_mine[0], input_other[0]
    )

    input_got = z_far(input_other)
    expert_cols = expert_mine.astype(F32) + expert_got.astype(F32)
    grad_cols = lax.dynamic_slice_in_dim(rows_grad, me_t * width, width, 1)
    weight_rows = jnp.sum(grad_cols.astype(F32) * expert_cols, axis=1)
    for bit in t_bits:
        weight_rows = weight_rows + swap(weight_rows, "tensor", bit)
    weight_grad = jnp.sum(jnp.where(match, weight_rows[:, None], 0.0), axis=0)
    mixed = mm_first(hot, (row_weight[:, None] * expert_cols).astype(BF16)).astype(BF16)
    input_cols = (input_mine.astype(F32) + input_got.astype(F32)).astype(BF16)
    input_grad = mm_first(hot, input_cols).astype(BF16)
    return (
        mixed,
        input_grad,
        weight_grad,
        panel(g_gate_own, g_gate_far),
        panel(g_up_own, g_up_far),
        down_out,
    )


def solution(mesh):
    return jax.shard_map(
        local,
        mesh=mesh,
        in_specs=(
            P("dp", None),
            P("dp", None),
            P("dp", None),
            P("dp", None),
            P("dp", "tensor"),
            P("dp", "tensor"),
            P("dp", "tensor"),
        ),
        out_specs=(
            P("dp", "tensor"),
            P("dp", "tensor"),
            P("dp"),
            P("dp", "tensor"),
            P("dp", "tensor"),
            P("dp", "tensor"),
        ),
        check_vma=False,
    )
```

```python
import jax
import jax.numpy as jnp
from jax import lax
from jax.sharding import PartitionSpec as P

BF16 = jnp.bfloat16
F32 = jnp.float32


def dot(left, right, dims):
    return lax.dot_general(left, right, (dims, ((), ())), preferred_element_type=F32)


def mm(left, right):
    return dot(left, right, ((1,), (0,)))


def mm_last(left, right):
    return dot(left, right, ((1,), (1,)))


def mm_first(left, right):
    return dot(left, right, ((0,), (0,)))


def swap(value, axis, distance):
    size = lax.axis_size(axis)
    return lax.ppermute(value, axis, [(i, i ^ distance) for i in range(size)])


def fence(*values):
    return lax.optimization_barrier(values)


def select_rows(assign_block, combine_block, row_limit):
    expert_hit = assign_block == 0
    routed = jnp.any(expert_hit, axis=1)
    weight = jnp.sum(
        jnp.where(expert_hit, combine_block, jnp.zeros((), combine_block.dtype)), axis=1
    )
    place = jnp.cumsum(routed.astype(jnp.int32)) - 1
    match = routed[None, :] & (place[None, :] == jnp.arange(row_limit, dtype=jnp.int32)[:, None])
    row_weight = jnp.sum(jnp.where(match, weight[None, :], 0.0), axis=1)
    return (match, row_weight)


def cat(*values):
    return jnp.concatenate(values, axis=0)


def beside(*values):
    return jnp.concatenate(values, axis=1)


def by_bits(blocks, index):
    bit = 1
    while bit < len(blocks):
        flag = (index & bit) != 0
        blocks = [jnp.where(flag, blocks[p ^ bit], blocks[p]) for p in range(len(blocks))]
        bit *= 2
    return blocks


def local(tokens, assign, combine, cotangent, w_gate, w_up, w_down_t):
    token_total, depth = tokens.shape
    row_limit = token_total // 2
    n_dp = lax.axis_size("dp")
    n_tensor = lax.axis_size("tensor")
    me = lax.axis_index("dp")
    me_t = lax.axis_index("tensor")
    chip, core = me // 2, me % 2
    far = n_dp // 2
    upper = me // far
    rows_w = w_gate.shape[0]
    pair = 2 * rows_w
    n_chip = n_dp // 2
    hid = w_gate.shape[1] // 4
    width = depth // n_tensor
    mids = [1 << i for i in range(1, far.bit_length() - 1)]
    t_bits = [1 << i for i in range(n_tensor.bit_length() - 1)]

    def z_far(block):
        return swap(block, "dp", far)

    def across(block):
        return swap(block, "dp", 1)

    def grow(block):
        blocks = [block]
        for bit in mids:
            count, rows = len(blocks), block.shape[0]
            got = swap(cat(*blocks) if count > 1 else block, "dp", bit)
            blocks = blocks + [got[i * rows : (i + 1) * rows] for i in range(count)]
        return blocks

    def whole_panel(own, away):
        full = jnp.zeros((n_chip, pair, hid), BF16)
        for j in range(n_chip // 2):
            full = lax.dynamic_update_index_in_dim(full, own[j], chip ^ j, 0)
            full = lax.dynamic_update_index_in_dim(full, away[j], chip ^ j ^ (n_chip // 2), 0)
        return full.reshape(depth, hid)

    def block_of(panel, j):
        return lax.dynamic_index_in_dim(panel.reshape(n_chip, pair, hid), chip ^ j, 0, False)

    def blocks_own(panel):
        return {j: block_of(panel, j) for j in range(n_chip // 2)}

    def blocks_far(panel):
        return {j: block_of(panel, j ^ (n_chip // 2)) for j in range(n_chip // 2)}

    def add(blocks, got):
        return {
            j: (blocks[j].astype(F32) + got[i * pair : (i + 1) * pair].astype(F32)).astype(BF16)
            for i, j in enumerate(blocks)
        }

    def first_send(blocks):
        bit = mids[-1] // 2
        gone = [blocks[j] for j in blocks if j & bit]
        return (
            cat(*gone) if len(gone) > 1 else gone[0],
            *(blocks[j] for j in blocks if not j & bit),
        )

    def shrink(send, *kept):
        got = swap(send, "dp", mids[-1])
        for bit in mids[:-1][::-1]:
            blocks = add(dict(enumerate(kept)), got)
            count = len(blocks) // 2
            got = swap(cat(*(blocks[j + count] for j in range(count))), "dp", bit)
            kept = tuple(blocks[j] for j in range(count))
        return kept[0], got

    def done(kept, got):
        return (kept.astype(F32) + got.astype(F32)).astype(BF16)

    def part(w, u, c):
        return lax.dynamic_slice_in_dim(w, (u * 2 + c) * hid, hid, 1)

    def to_sibling(w):
        return beside(part(w, upper, 1 - core), part(w, 1 - upper, 1 - core))

    def by_core(mine, got):
        return jnp.where(core == 0, cat(mine, got), cat(got, mine))

    def pair_rows(w, got):
        mine = by_core(part(w, upper, core), got[:, :hid])
        other = by_core(part(w, 1 - upper, core), got[:, hid:])
        return mine, other

    gate_0 = lax.dynamic_slice_in_dim(w_gate, upper * 2 * hid, 2 * hid, 1)
    gate_4 = z_far(lax.dynamic_slice_in_dim(w_gate, (1 - upper) * 2 * hid, 2 * hid, 1))
    gate_own = grow(gate_0)
    match, row_weight = select_rows(assign, combine, row_limit)
    hot = match.astype(BF16)
    rows_in = mm(hot, tokens).astype(BF16)
    rows_grad = mm(hot, cotangent).astype(BF16)
    out_grad = (row_weight[:, None] * rows_grad.astype(F32)).astype(BF16)
    quarter = cat(
        *(lax.dynamic_slice_in_dim(v, me_t * width, width, 1) for v in (rows_in, out_grad))
    )
    send = cat(to_sibling(w_up), to_sibling(w_down_t))
    gate_4, quarter, rows_in, out_grad, send, *gate_own = fence(
        gate_4, quarter, rows_in, out_grad, send, *gate_own
    )

    quarter = z_far(quarter)
    gate_far = grow(gate_4)
    in_sib, out_sib = across(rows_in), across(out_grad)
    got = across(send)
    up_0, up_1 = pair_rows(w_up, got[:rows_w])
    down_0, down_1 = pair_rows(w_down_t, got[rows_w:])
    own = beside(up_0, down_0)
    quarter, in_sib, out_sib, own, up_1, down_1, *gate_far = fence(
        quarter, in_sib, out_sib, own, up_1, down_1, *gate_far
    )

    up_4 = z_far(up_1)
    own = grow(own)
    quarters = [quarter] + [swap(quarter, "tensor", k) for k in range(1, n_tensor)]
    gate_all = jnp.stack(gate_own + gate_far)
    gate_mine = lax.dynamic_slice_in_dim(gate_all, core * hid, hid, 2)
    gate_send = lax.dynamic_slice_in_dim(gate_all, (1 - core) * hid, hid, 2)
    up_4, gate_mine, gate_send, down_1, *rest = fence(
        up_4, gate_mine, gate_send, down_1, *quarters, *own
    )
    quarters, own = rest[: len(quarters)], rest[len(quarters) :]
    up_own, down_own = [b[:, :hid] for b in own], [b[:, hid:] for b in own]

    up_far = grow(up_4)
    down_4 = z_far(down_1)
    gate_got, *quarters = fence(across(gate_send), *quarters)
    gate = jnp.zeros((n_chip, 2, rows_w, hid), BF16)
    for j in range(n_chip):
        gate = lax.dynamic_update_slice(gate, gate_mine[j][None, None], (chip ^ j, core, 0, 0))
        gate = lax.dynamic_update_slice(gate, gate_got[j][None, None], (chip ^ j, 1 - core, 0, 0))
    gate = gate.reshape(depth, hid)

    def true_rows(first):
        return beside(*by_bits([q[first : first + row_limit] for q in quarters], me_t))

    in_away, out_away = true_rows(0), true_rows(row_limit)
    in_away_sib, out_away_sib = across(in_away), across(out_away)
    in_all = cat(rows_in, in_away, in_sib, in_away_sib)
    out_all = cat(out_grad, out_away, out_sib, out_away_sib)
    gate_pre = mm(in_all, gate)
    down_4, in_all, out_all, gate_pre, gate, *up_far = fence(
        down_4, in_all, out_all, gate_pre, gate, *up_far
    )

    down_far = grow(down_4)
    up = whole_panel(up_own, up_far)
    up_pre = mm(in_all, up)
    sigmoid_gate = jax.nn.sigmoid(gate_pre)
    hidden = (gate_pre * sigmoid_gate * up_pre).astype(BF16)
    g_down = mm_first(out_all, hidden).astype(BF16)
    g_down, hidden, up_pre, up, *down_far = fence(g_down, hidden, up_pre, up, *down_far)

    table = 2 * row_limit
    g_down_4 = first_send(blocks_far(g_down))
    n_kept = len(g_down_4)
    g_down_4 = shrink(*g_down_4)
    g_down_own = shrink(*first_send(blocks_own(g_down)))
    down = whole_panel(down_own, down_far)
    hidden_grad = mm(out_all, down)
    gate_grad = (
        hidden_grad * up_pre * sigmoid_gate * (1.0 + gate_pre * (1.0 - sigmoid_gate))
    ).astype(BF16)
    up_grad = (hidden_grad * gate_pre * sigmoid_gate).astype(BF16)
    g_gate = mm_first(in_all, gate_grad).astype(BF16)
    expert_sib = mm_last(hidden[table:], down).astype(BF16)

    def input_part(rows):
        return mm_last(gate_grad[rows], gate) + mm_last(up_grad[rows], up)

    input_sib = input_part(slice(table, None)).astype(BF16)
    down, gate_grad, up_grad, g_gate, expert_sib, input_sib, *rest = fence(
        down, gate_grad, up_grad, g_gate, expert_sib, input_sib, *g_down_4, *g_down_own
    )
    g_down_own = rest[2:]
    g_down_4, expert_sib, input_sib, g_gate = fence(done(*rest[:2]), expert_sib, input_sib, g_gate)
    g_gate_4, g_gate_own = first_send(blocks_far(g_gate)), first_send(blocks_own(g_gate))

    g_down_far = z_far(g_down_4)
    g_gate_4 = shrink(*g_gate_4)
    expert_got, input_got = across(expert_sib), across(input_sib)
    g_up = mm_first(in_all, up_grad).astype(BF16)
    expert_sum = (mm_last(hidden[:table], down) + expert_got.astype(F32)).astype(BF16)
    input_sum = (input_part(slice(None, table)) + input_got.astype(F32)).astype(BF16)

    def split_parts(value):
        return {
            k: lax.dynamic_slice_in_dim(value, (me_t ^ k) * width, width, 1)
            for k in range(n_tensor)
        }

    def gone(parts, bit):
        return beside(*(parts[k] for k in parts if k & bit))

    def kept(parts, bit, got):
        keep = [k for k in parts if not k & bit]
        return {
            k: (parts[k].astype(F32) + got[:, i * width : (i + 1) * width].astype(F32)).astype(BF16)
            for i, k in enumerate(keep)
        }

    def step(parts, bit):
        return kept(parts, bit, swap(gone(parts, bit), "tensor", bit))

    def split_rows(value):
        return split_parts(value[:row_limit]), split_parts(value[row_limit:])

    def flat(parts):
        return [parts[k] for k in parts]

    low, high = t_bits[0], t_bits[-1]
    expert_mine, expert_other = split_rows(expert_sum)
    send_low, send_high = gone(expert_mine, low), gone(expert_other, high)
    g_up_4, g_up_own = first_send(blocks_far(g_up)), first_send(blocks_own(g_up))
    g_down_far, input_sum, send_low, send_high, *rest = fence(
        g_down_far, input_sum, send_low, send_high, *g_gate_4, *g_up_4, *g_up_own
    )
    g_up_own = rest[2 + n_kept :]
    g_gate_4, send_low, send_high, input_sum, *g_up_4 = fence(
        done(*rest[:2]), send_low, send_high, input_sum, *rest[2 : 2 + n_kept]
    )

    def panel(own, other):
        both = beside(own, other)
        mine = lax.dynamic_slice_in_dim(both, core * rows_w, rows_w, 0)
        got = across(lax.dynamic_slice_in_dim(both, (1 - core) * rows_w, rows_w, 0))
        whole = jnp.zeros((rows_w, 4 * hid), BF16)
        for block, u, c in (
            (mine[:, :hid], upper, core),
            (mine[:, hid:], 1 - upper, core),
            (got[:, :hid], upper, 1 - core),
            (got[:, hid:], 1 - upper, 1 - core),
        ):
            whole = lax.dynamic_update_slice(whole, block, (0, (u * 2 + c) * hid))
        return whole

    g_gate_far = z_far(g_gate_4)
    g_up_4 = shrink(*g_up_4)
    expert_mine = kept(expert_mine, low, swap(send_low, "tensor", low))
    expert_other = kept(expert_other, high, swap(send_high, "tensor", high))
    input_mine, input_other = split_rows(input_sum)
    merged = len(t_bits) == 2
    if merged:
        send_high = beside(gone(expert_mine, high), gone(input_other, high))
        send_low = beside(gone(expert_other, low), gone(input_mine, low))
    else:
        send_high, send_low = gone(input_other, high), gone(input_mine, low)
    g_gate_far, expert_mine, expert_other, input_mine, input_other, send_low, send_high, *rest = (
        fence(
            g_gate_far, expert_mine, expert_other, input_mine, input_other, send_low, send_high,
            *g_up_4, *g_gate_own
        )
    )
    g_up_4, send_low, send_high, *g_gate_own = fence(
        done(*rest[:2]), send_low, send_high, *rest[2:]
    )

    g_up_far = z_far(g_up_4)
    g_gate_own = shrink(*g_gate_own)
    got_high, got_low = swap(send_high, "tensor", high), swap(send_low, "tensor", low)
    if merged:
        expert_mine = kept(expert_mine, high, got_high[:, :width])
        expert_other = kept(expert_other, low, got_low[:, :width])
        got_high, got_low = got_high[:, width:], got_low[:, width:]
    else:
        for bit in t_bits[1:]:
            expert_mine = step(expert_mine, bit)
        for bit in t_bits[:-1][::-1]:
            expert_other = step(expert_other, bit)
    input_other = kept(input_other, high, got_high)
    input_mine = kept(input_mine, low, got_low)
    g_up_far, expert_mine, expert_other, input_mine, input_other, *rest = fence(
        g_up_far, expert_mine[0], expert_other[0], input_mine, input_other, *g_gate_own, *g_up_own
    )
    g_gate_own, g_up_own = rest[:2], rest[2:]

    g_up_own = shrink(*g_up_own)
    expert_got = z_far(expert_other)
    for bit in t_bits[1:]:
        input_mine = step(input_mine, bit)
    for bit in t_bits[:-1][::-1]:
        input_other = step(input_other, bit)
    expert_got, input_mine, input_other, g_down_far, g_gate_far, *rest = fence(
        expert_got, input_mine[0], input_other[0], g_down_far, g_gate_far,
        *g_down_own, *g_gate_own, *g_up_own
    )
    g_down_own, g_gate_own, g_up_own = rest[:2], rest[2:4], rest[4:]

    input_got = z_far(input_other)
    expert_cols = expert_mine.astype(F32) + expert_got.astype(F32)
    grad_cols = lax.dynamic_slice_in_dim(rows_grad, me_t * width, width, 1)
    weight_rows = jnp.sum(grad_cols.astype(F32) * expert_cols, axis=1)
    for bit in t_bits:
        weight_rows = weight_rows + swap(weight_rows, "tensor", bit)
    weight_grad = jnp.sum(jnp.where(match, weight_rows[:, None], 0.0), axis=0)
    mixed = mm_first(hot, (row_weight[:, None] * expert_cols).astype(BF16)).astype(BF16)
    input_cols = (input_mine.astype(F32) + input_got.astype(F32)).astype(BF16)
    input_grad = mm_first(hot, input_cols).astype(BF16)
    return (
        mixed,
        input_grad,
        weight_grad,
        panel(done(*g_gate_own), g_gate_far),
        panel(done(*g_up_own), g_up_far),
        panel(done(*g_down_own), g_down_far),
    )


def solution(mesh):
    return jax.shard_map(
        local,
        mesh=mesh,
        in_specs=(
            P("dp", None),
            P("dp", None),
            P("dp", None),
            P("dp", None),
            P("dp", "tensor"),
            P("dp", "tensor"),
            P("dp", "tensor"),
        ),
        out_specs=(
            P("dp", "tensor"),
            P("dp", "tensor"),
            P("dp"),
            P("dp", "tensor"),
            P("dp", "tensor"),
            P("dp", "tensor"),
        ),
        check_vma=False,
    )
```

```python
import jax
import jax.numpy as jnp
from jax import lax
from jax.sharding import PartitionSpec as P

BF16 = jnp.bfloat16
F32 = jnp.float32


def dot(left, right, dims):
    return lax.dot_general(left, right, (dims, ((), ())), preferred_element_type=F32)


def mm(left, right):
    return dot(left, right, ((1,), (0,)))


def mm_last(left, right):
    return dot(left, right, ((1,), (1,)))


def mm_first(left, right):
    return dot(left, right, ((0,), (0,)))


def swap(value, axis, distance):
    size = lax.axis_size(axis)
    return lax.ppermute(value, axis, [(i, i ^ distance) for i in range(size)])


def fence(*values):
    return lax.optimization_barrier(values)


def select_rows(assign_block, combine_block, row_limit):
    expert_hit = assign_block == 0
    routed = jnp.any(expert_hit, axis=1)
    weight = jnp.sum(
        jnp.where(expert_hit, combine_block, jnp.zeros((), combine_block.dtype)), axis=1
    )
    place = jnp.cumsum(routed.astype(jnp.int32)) - 1
    match = routed[None, :] & (place[None, :] == jnp.arange(row_limit, dtype=jnp.int32)[:, None])
    row_weight = jnp.sum(jnp.where(match, weight[None, :], 0.0), axis=1)
    return (match, row_weight)


def cat(*values):
    return jnp.concatenate(values, axis=0)


def beside(*values):
    return jnp.concatenate(values, axis=1)


def by_bits(blocks, index):
    bit = 1
    while bit < len(blocks):
        flag = (index & bit) != 0
        blocks = [jnp.where(flag, blocks[p ^ bit], blocks[p]) for p in range(len(blocks))]
        bit *= 2
    return blocks


def local(tokens, assign, combine, cotangent, w_gate, w_up, w_down_t):
    token_total, depth = tokens.shape
    row_limit = token_total // 2
    n_dp = lax.axis_size("dp")
    n_tensor = lax.axis_size("tensor")
    me = lax.axis_index("dp")
    me_t = lax.axis_index("tensor")
    chip, core = me // 2, me % 2
    far = n_dp // 2
    upper = me // far
    rows_w = w_gate.shape[0]
    pair = 2 * rows_w
    n_chip = n_dp // 2
    hid = w_gate.shape[1] // 4
    width = depth // n_tensor
    mids = [1 << i for i in range(1, far.bit_length() - 1)]
    t_bits = [1 << i for i in range(n_tensor.bit_length() - 1)]

    def z_far(block):
        return swap(block, "dp", far)

    def across(block):
        return swap(block, "dp", 1)

    def grow(block):
        blocks = [block]
        for bit in mids:
            count, rows = len(blocks), block.shape[0]
            got = swap(cat(*blocks) if count > 1 else block, "dp", bit)
            blocks = blocks + [got[i * rows : (i + 1) * rows] for i in range(count)]
        return blocks

    def whole_panel(own, away):
        full = jnp.zeros((n_chip, pair, hid), BF16)
        for j in range(n_chip // 2):
            full = lax.dynamic_update_index_in_dim(full, own[j], chip ^ j, 0)
            full = lax.dynamic_update_index_in_dim(full, away[j], chip ^ j ^ (n_chip // 2), 0)
        return full.reshape(depth, hid)

    half_rows = depth // 2
    same_core = [[u * far + 2 * i + c for i in range(n_chip // 2)] for u in range(2) for c in range(2)]

    def side(value, u):
        return lax.dynamic_slice_in_dim(value, u * half_rows, half_rows, 0)

    def scatter(value):
        return lax.psum_scatter(
            value, "dp", scatter_dimension=0, tiled=True, axis_index_groups=same_core
        )

    def part(w, u, c):
        return lax.dynamic_slice_in_dim(w, (u * 2 + c) * hid, hid, 1)

    def to_sibling(w):
        return beside(part(w, upper, 1 - core), part(w, 1 - upper, 1 - core))

    def by_core(mine, got):
        return jnp.where(core == 0, cat(mine, got), cat(got, mine))

    def pair_rows(w, got):
        mine = by_core(part(w, upper, core), got[:, :hid])
        other = by_core(part(w, 1 - upper, core), got[:, hid:])
        return mine, other

    gate_0 = lax.dynamic_slice_in_dim(w_gate, upper * 2 * hid, 2 * hid, 1)
    gate_4 = z_far(lax.dynamic_slice_in_dim(w_gate, (1 - upper) * 2 * hid, 2 * hid, 1))
    gate_own = grow(gate_0)
    match, row_weight = select_rows(assign, combine, row_limit)
    hot = match.astype(BF16)
    rows_in = mm(hot, tokens).astype(BF16)
    rows_grad = mm(hot, cotangent).astype(BF16)
    out_grad = (row_weight[:, None] * rows_grad.astype(F32)).astype(BF16)
    quarter = cat(
        *(lax.dynamic_slice_in_dim(v, me_t * width, width, 1) for v in (rows_in, out_grad))
    )
    send = cat(to_sibling(w_up), to_sibling(w_down_t))
    gate_4, quarter, rows_in, out_grad, send, *gate_own = fence(
        gate_4, quarter, rows_in, out_grad, send, *gate_own
    )

    quarter = z_far(quarter)
    gate_far = grow(gate_4)
    in_sib, out_sib = across(rows_in), across(out_grad)
    got = across(send)
    up_0, up_1 = pair_rows(w_up, got[:rows_w])
    down_0, down_1 = pair_rows(w_down_t, got[rows_w:])
    own = beside(up_0, down_0)
    quarter, in_sib, out_sib, own, up_1, down_1, *gate_far = fence(
        quarter, in_sib, out_sib, own, up_1, down_1, *gate_far
    )

    up_4 = z_far(up_1)
    own = grow(own)
    quarters = [quarter] + [swap(quarter, "tensor", k) for k in range(1, n_tensor)]
    gate_all = jnp.stack(gate_own + gate_far)
    gate_mine = lax.dynamic_slice_in_dim(gate_all, core * hid, hid, 2)
    gate_send = lax.dynamic_slice_in_dim(gate_all, (1 - core) * hid, hid, 2)
    up_4, gate_mine, gate_send, down_1, *rest = fence(
        up_4, gate_mine, gate_send, down_1, *quarters, *own
    )
    quarters, own = rest[: len(quarters)], rest[len(quarters) :]
    up_own, down_own = [b[:, :hid] for b in own], [b[:, hid:] for b in own]

    up_far = grow(up_4)
    down_4 = z_far(down_1)
    gate_got, *quarters = fence(across(gate_send), *quarters)
    gate = jnp.zeros((n_chip, 2, rows_w, hid), BF16)
    for j in range(n_chip):
        gate = lax.dynamic_update_slice(gate, gate_mine[j][None, None], (chip ^ j, core, 0, 0))
        gate = lax.dynamic_update_slice(gate, gate_got[j][None, None], (chip ^ j, 1 - core, 0, 0))
    gate = gate.reshape(depth, hid)

    def true_rows(first):
        return beside(*by_bits([q[first : first + row_limit] for q in quarters], me_t))

    in_away, out_away = true_rows(0), true_rows(row_limit)
    in_away_sib, out_away_sib = across(in_away), across(out_away)
    in_all = cat(rows_in, in_away, in_sib, in_away_sib)
    out_all = cat(out_grad, out_away, out_sib, out_away_sib)
    gate_pre = mm(in_all, gate)
    down_4, in_all, out_all, gate_pre, gate, *up_far = fence(
        down_4, in_all, out_all, gate_pre, gate, *up_far
    )

    down_far = grow(down_4)
    up = whole_panel(up_own, up_far)
    up_pre = mm(in_all, up)
    sigmoid_gate = jax.nn.sigmoid(gate_pre)
    hidden = (gate_pre * sigmoid_gate * up_pre).astype(BF16)
    g_down = mm_first(out_all, hidden).astype(BF16)
    g_down, hidden, up_pre, up, *down_far = fence(g_down, hidden, up_pre, up, *down_far)

    table = 2 * row_limit
    g_down_4 = scatter(side(g_down, 1 - upper))
    g_down_own = scatter(side(g_down, upper))
    down = whole_panel(down_own, down_far)
    hidden_grad = mm(out_all, down)
    gate_grad = (
        hidden_grad * up_pre * sigmoid_gate * (1.0 + gate_pre * (1.0 - sigmoid_gate))
    ).astype(BF16)
    up_grad = (hidden_grad * gate_pre * sigmoid_gate).astype(BF16)
    g_gate = mm_first(in_all, gate_grad).astype(BF16)
    expert_sib = mm_last(hidden[table:], down).astype(BF16)

    def input_part(rows):
        return mm_last(gate_grad[rows], gate) + mm_last(up_grad[rows], up)

    input_sib = input_part(slice(table, None)).astype(BF16)
    g_gate_4, g_gate_own = side(g_gate, 1 - upper), side(g_gate, upper)
    down, gate_grad, up_grad, expert_sib, input_sib, g_down_4, g_down_own, g_gate_4, g_gate_own = fence(
        down, gate_grad, up_grad, expert_sib, input_sib, g_down_4, g_down_own, g_gate_4, g_gate_own
    )

    g_down_far = z_far(g_down_4)
    g_gate_4 = scatter(g_gate_4)
    expert_got, input_got = across(expert_sib), across(input_sib)
    g_up = mm_first(in_all, up_grad).astype(BF16)
    expert_sum = (mm_last(hidden[:table], down) + expert_got.astype(F32)).astype(BF16)
    input_sum = (input_part(slice(None, table)) + input_got.astype(F32)).astype(BF16)

    def split_parts(value):
        return {
            k: lax.dynamic_slice_in_dim(value, (me_t ^ k) * width, width, 1)
            for k in range(n_tensor)
        }

    def gone(parts, bit):
        return beside(*(parts[k] for k in parts if k & bit))

    def kept(parts, bit, got):
        keep = [k for k in parts if not k & bit]
        return {
            k: (parts[k].astype(F32) + got[:, i * width : (i + 1) * width].astype(F32)).astype(BF16)
            for i, k in enumerate(keep)
        }

    def step(parts, bit):
        return kept(parts, bit, swap(gone(parts, bit), "tensor", bit))

    def split_rows(value):
        return split_parts(value[:row_limit]), split_parts(value[row_limit:])

    def flat(parts):
        return [parts[k] for k in parts]

    low, high = t_bits[0], t_bits[-1]
    expert_mine, expert_other = split_rows(expert_sum)
    send_low, send_high = gone(expert_mine, low), gone(expert_other, high)
    g_up_4, g_up_own = side(g_up, 1 - upper), side(g_up, upper)
    g_down_far, input_sum, send_low, send_high, g_gate_4, g_up_4, g_up_own = fence(
        g_down_far, input_sum, send_low, send_high, g_gate_4, g_up_4, g_up_own
    )

    def panel(own, other):
        both = beside(own, other)
        mine = lax.dynamic_slice_in_dim(both, core * rows_w, rows_w, 0)
        got = across(lax.dynamic_slice_in_dim(both, (1 - core) * rows_w, rows_w, 0))
        whole = jnp.zeros((rows_w, 4 * hid), BF16)
        for block, u, c in (
            (mine[:, :hid], upper, core),
            (mine[:, hid:], 1 - upper, core),
            (got[:, :hid], upper, 1 - core),
            (got[:, hid:], 1 - upper, 1 - core),
        ):
            whole = lax.dynamic_update_slice(whole, block, (0, (u * 2 + c) * hid))
        return whole

    g_gate_far = z_far(g_gate_4)
    g_up_4 = scatter(g_up_4)
    expert_mine = kept(expert_mine, low, swap(send_low, "tensor", low))
    expert_other = kept(expert_other, high, swap(send_high, "tensor", high))
    input_mine, input_other = split_rows(input_sum)
    merged = len(t_bits) == 2
    if merged:
        send_high = beside(gone(expert_mine, high), gone(input_other, high))
        send_low = beside(gone(expert_other, low), gone(input_mine, low))
    else:
        send_high, send_low = gone(input_other, high), gone(input_mine, low)
    (
        g_gate_far, expert_mine, expert_other, input_mine, input_other,
        send_low, send_high, g_up_4, g_gate_own,
    ) = fence(
        g_gate_far, expert_mine, expert_other, input_mine, input_other,
        send_low, send_high, g_up_4, g_gate_own,
    )

    g_up_far = z_far(g_up_4)
    g_gate_own = scatter(g_gate_own)
    got_high, got_low = swap(send_high, "tensor", high), swap(send_low, "tensor", low)
    if merged:
        expert_mine = kept(expert_mine, high, got_high[:, :width])
        expert_other = kept(expert_other, low, got_low[:, :width])
        got_high, got_low = got_high[:, width:], got_low[:, width:]
    else:
        for bit in t_bits[1:]:
            expert_mine = step(expert_mine, bit)
        for bit in t_bits[:-1][::-1]:
            expert_other = step(expert_other, bit)
    input_other = kept(input_other, high, got_high)
    input_mine = kept(input_mine, low, got_low)
    (
        g_up_far, expert_mine, expert_other, input_mine, input_other,
        g_gate_own, g_up_own, g_down_own, g_down_far, g_gate_far,
    ) = fence(
        g_up_far, expert_mine[0], expert_other[0], input_mine, input_other,
        g_gate_own, g_up_own, g_down_own, g_down_far, g_gate_far,
    )

    g_up_own = scatter(g_up_own)
    expert_got = z_far(expert_other)
    for bit in t_bits[1:]:
        input_mine = step(input_mine, bit)
    for bit in t_bits[:-1][::-1]:
        input_other = step(input_other, bit)
    input_got = z_far(input_other[0])
    expert_cols = expert_mine.astype(F32) + expert_got.astype(F32)
    grad_cols = lax.dynamic_slice_in_dim(rows_grad, me_t * width, width, 1)
    weight_rows = jnp.sum(grad_cols.astype(F32) * expert_cols, axis=1)
    for bit in t_bits:
        weight_rows = weight_rows + swap(weight_rows, "tensor", bit)
    weight_grad = jnp.sum(jnp.where(match, weight_rows[:, None], 0.0), axis=0)
    mixed = mm_first(hot, (row_weight[:, None] * expert_cols).astype(BF16)).astype(BF16)
    input_cols = (input_mine[0].astype(F32) + input_got.astype(F32)).astype(BF16)
    input_grad = mm_first(hot, input_cols).astype(BF16)
    return (
        mixed,
        input_grad,
        weight_grad,
        panel(g_gate_own, g_gate_far),
        panel(g_up_own, g_up_far),
        panel(g_down_own, g_down_far),
    )


def solution(mesh):
    return jax.shard_map(
        local,
        mesh=mesh,
        in_specs=(
            P("dp", None),
            P("dp", None),
            P("dp", None),
            P("dp", None),
            P("dp", "tensor"),
            P("dp", "tensor"),
            P("dp", "tensor"),
        ),
        out_specs=(
            P("dp", "tensor"),
            P("dp", "tensor"),
            P("dp"),
            P("dp", "tensor"),
            P("dp", "tensor"),
            P("dp", "tensor"),
        ),
        check_vma=False,
    )
```

```python
import jax
import jax.numpy as jnp
from jax import lax
from jax.sharding import PartitionSpec as P

BF16 = jnp.bfloat16
F32 = jnp.float32


def dot(left, right, dims):
    return lax.dot_general(left, right, (dims, ((), ())), preferred_element_type=F32)


def mm(left, right):
    return dot(left, right, ((1,), (0,)))


def mm_last(left, right):
    return dot(left, right, ((1,), (1,)))


def mm_first(left, right):
    return dot(left, right, ((0,), (0,)))


def swap(value, axis, distance):
    size = lax.axis_size(axis)
    return lax.ppermute(value, axis, [(i, i ^ distance) for i in range(size)])


def fence(*values):
    return lax.optimization_barrier(values)


def select_rows(assign_block, combine_block, row_limit):
    expert_hit = assign_block == 0
    routed = jnp.any(expert_hit, axis=1)
    weight = jnp.sum(
        jnp.where(expert_hit, combine_block, jnp.zeros((), combine_block.dtype)), axis=1
    )
    place = jnp.cumsum(routed.astype(jnp.int32)) - 1
    match = routed[None, :] & (place[None, :] == jnp.arange(row_limit, dtype=jnp.int32)[:, None])
    row_weight = jnp.sum(jnp.where(match, weight[None, :], 0.0), axis=1)
    return (match, row_weight)


def cat(*values):
    return jnp.concatenate(values, axis=0)


def beside(*values):
    return jnp.concatenate(values, axis=1)


def by_bits(blocks, index):
    bit = 1
    while bit < len(blocks):
        flag = (index & bit) != 0
        blocks = [jnp.where(flag, blocks[p ^ bit], blocks[p]) for p in range(len(blocks))]
        bit *= 2
    return blocks


def local(tokens, assign, combine, cotangent, w_gate, w_up, w_down_t):
    token_total, depth = tokens.shape
    row_limit = token_total // 2
    n_dp = lax.axis_size("dp")
    n_tensor = lax.axis_size("tensor")
    me = lax.axis_index("dp")
    me_t = lax.axis_index("tensor")
    chip, core = me // 2, me % 2
    far = n_dp // 2
    upper = me // far
    rows_w = w_gate.shape[0]
    pair = 2 * rows_w
    n_chip = n_dp // 2
    hid = w_gate.shape[1] // 4
    width = depth // n_tensor
    mids = [1 << i for i in range(1, far.bit_length() - 1)]
    t_bits = [1 << i for i in range(n_tensor.bit_length() - 1)]

    def z_far(block):
        return swap(block, "dp", far)

    def across(block):
        return swap(block, "dp", 1)

    def grow(block):
        blocks = [block]
        for bit in mids:
            count, rows = len(blocks), block.shape[0]
            got = swap(cat(*blocks) if count > 1 else block, "dp", bit)
            blocks = blocks + [got[i * rows : (i + 1) * rows] for i in range(count)]
        return blocks

    def whole_panel(own, away):
        full = jnp.zeros((n_chip, pair, hid), BF16)
        for j in range(n_chip // 2):
            full = lax.dynamic_update_index_in_dim(full, own[j], chip ^ j, 0)
            full = lax.dynamic_update_index_in_dim(full, away[j], chip ^ j ^ (n_chip // 2), 0)
        return full.reshape(depth, hid)

    def block_of(panel, j):
        return lax.dynamic_index_in_dim(panel.reshape(n_chip, pair, hid), chip ^ j, 0, False)

    def blocks_own(panel):
        return {j: block_of(panel, j) for j in range(n_chip // 2)}

    def blocks_far(panel):
        return {j: block_of(panel, j ^ (n_chip // 2)) for j in range(n_chip // 2)}

    def add(blocks, got):
        return {
            j: (blocks[j].astype(F32) + got[i * pair : (i + 1) * pair].astype(F32)).astype(BF16)
            for i, j in enumerate(blocks)
        }

    def first_send(blocks):
        bit = mids[-1] // 2
        gone = [blocks[j] for j in blocks if j & bit]
        return (
            cat(*gone) if len(gone) > 1 else gone[0],
            *(blocks[j] for j in blocks if not j & bit),
        )

    def shrink(send, *kept):
        got = swap(send, "dp", mids[-1])
        for bit in mids[:-1][::-1]:
            blocks = add(dict(enumerate(kept)), got)
            count = len(blocks) // 2
            got = swap(cat(*(blocks[j + count] for j in range(count))), "dp", bit)
            kept = tuple(blocks[j] for j in range(count))
        return kept[0], got

    def done(kept, got):
        return (kept.astype(F32) + got.astype(F32)).astype(BF16)

    half_rows = depth // 2
    same_core = [[u * far + 2 * i + c for i in range(n_chip // 2)] for u in range(2) for c in range(2)]

    def scatter_far(panel):
        rows = lax.dynamic_slice_in_dim(panel, (1 - upper) * half_rows, half_rows, 0)
        return lax.psum_scatter(
            rows, "dp", scatter_dimension=0, tiled=True, axis_index_groups=same_core
        )

    def part(w, u, c):
        return lax.dynamic_slice_in_dim(w, (u * 2 + c) * hid, hid, 1)

    def to_sibling(w):
        return beside(part(w, upper, 1 - core), part(w, 1 - upper, 1 - core))

    def by_core(mine, got):
        return jnp.where(core == 0, cat(mine, got), cat(got, mine))

    def pair_rows(w, got):
        mine = by_core(part(w, upper, core), got[:, :hid])
        other = by_core(part(w, 1 - upper, core), got[:, hid:])
        return mine, other

    gate_0 = lax.dynamic_slice_in_dim(w_gate, upper * 2 * hid, 2 * hid, 1)
    gate_4 = z_far(lax.dynamic_slice_in_dim(w_gate, (1 - upper) * 2 * hid, 2 * hid, 1))
    gate_own = grow(gate_0)
    match, row_weight = select_rows(assign, combine, row_limit)
    hot = match.astype(BF16)
    rows_in = mm(hot, tokens).astype(BF16)
    rows_grad = mm(hot, cotangent).astype(BF16)
    out_grad = (row_weight[:, None] * rows_grad.astype(F32)).astype(BF16)
    quarter = cat(
        *(lax.dynamic_slice_in_dim(v, me_t * width, width, 1) for v in (rows_in, out_grad))
    )
    send = cat(to_sibling(w_up), to_sibling(w_down_t))
    gate_4, quarter, rows_in, out_grad, send, *gate_own = fence(
        gate_4, quarter, rows_in, out_grad, send, *gate_own
    )

    quarter = z_far(quarter)
    gate_far = grow(gate_4)
    in_sib, out_sib = across(rows_in), across(out_grad)
    got = across(send)
    up_0, up_1 = pair_rows(w_up, got[:rows_w])
    down_0, down_1 = pair_rows(w_down_t, got[rows_w:])
    own = beside(up_0, down_0)
    quarter, in_sib, out_sib, own, up_1, down_1, *gate_far = fence(
        quarter, in_sib, out_sib, own, up_1, down_1, *gate_far
    )

    up_4 = z_far(up_1)
    own = grow(own)
    quarters = [quarter] + [swap(quarter, "tensor", k) for k in range(1, n_tensor)]
    gate_all = jnp.stack(gate_own + gate_far)
    gate_mine = lax.dynamic_slice_in_dim(gate_all, core * hid, hid, 2)
    gate_send = lax.dynamic_slice_in_dim(gate_all, (1 - core) * hid, hid, 2)
    up_4, gate_mine, gate_send, down_1, *rest = fence(
        up_4, gate_mine, gate_send, down_1, *quarters, *own
    )
    quarters, own = rest[: len(quarters)], rest[len(quarters) :]
    up_own, down_own = [b[:, :hid] for b in own], [b[:, hid:] for b in own]

    up_far = grow(up_4)
    down_4 = z_far(down_1)
    gate_got, *quarters = fence(across(gate_send), *quarters)
    gate = jnp.zeros((n_chip, 2, rows_w, hid), BF16)
    for j in range(n_chip):
        gate = lax.dynamic_update_slice(gate, gate_mine[j][None, None], (chip ^ j, core, 0, 0))
        gate = lax.dynamic_update_slice(gate, gate_got[j][None, None], (chip ^ j, 1 - core, 0, 0))
    gate = gate.reshape(depth, hid)

    def true_rows(first):
        return beside(*by_bits([q[first : first + row_limit] for q in quarters], me_t))

    in_away, out_away = true_rows(0), true_rows(row_limit)
    in_away_sib, out_away_sib = across(in_away), across(out_away)
    in_all = cat(rows_in, in_away, in_sib, in_away_sib)
    out_all = cat(out_grad, out_away, out_sib, out_away_sib)
    gate_pre = mm(in_all, gate)
    down_4, in_all, out_all, gate_pre, gate, *up_far = fence(
        down_4, in_all, out_all, gate_pre, gate, *up_far
    )

    down_far = grow(down_4)
    up = whole_panel(up_own, up_far)
    up_pre = mm(in_all, up)
    sigmoid_gate = jax.nn.sigmoid(gate_pre)
    hidden = (gate_pre * sigmoid_gate * up_pre).astype(BF16)
    g_down = mm_first(out_all, hidden).astype(BF16)
    g_down, hidden, up_pre, up, *down_far = fence(g_down, hidden, up_pre, up, *down_far)

    table = 2 * row_limit
    g_down_4 = scatter_far(g_down)
    down = whole_panel(down_own, down_far)
    hidden_grad = mm(out_all, down)
    gate_grad = (
        hidden_grad * up_pre * sigmoid_gate * (1.0 + gate_pre * (1.0 - sigmoid_gate))
    ).astype(BF16)
    up_grad = (hidden_grad * gate_pre * sigmoid_gate).astype(BF16)
    g_gate = mm_first(in_all, gate_grad).astype(BF16)
    expert_sib = mm_last(hidden[table:], down).astype(BF16)

    def input_part(rows):
        return mm_last(gate_grad[rows], gate) + mm_last(up_grad[rows], up)

    g_gate_4, g_gate_own = first_send(blocks_far(g_gate)), first_send(blocks_own(g_gate))
    n_kept = len(g_gate_4)
    down, gate_grad, up_grad, expert_sib, g_down_4, g_down, *rest = fence(
        down, gate_grad, up_grad, expert_sib, g_down_4, g_down, *g_gate_4, *g_gate_own
    )
    g_gate_4, g_gate_own = rest[:n_kept], rest[n_kept:]

    g_down_far = z_far(g_down_4)
    g_gate_4 = shrink(*g_gate_4)
    expert_got, in_all, gate_grad, up_grad, hidden = fence(
        across(expert_sib[:row_limit]), in_all, gate_grad, up_grad, hidden
    )
    expert_got = cat(expert_got, across(expert_sib[row_limit:]))
    g_up = mm_first(in_all, up_grad).astype(BF16)
    expert_sum = (mm_last(hidden[:table], down) + expert_got.astype(F32)).astype(BF16)
    input_sib = input_part(slice(table, None)).astype(BF16)
    input_sum = input_part(slice(None, table)).astype(BF16)

    def split_parts(value):
        return {
            k: lax.dynamic_slice_in_dim(value, (me_t ^ k) * width, width, 1)
            for k in range(n_tensor)
        }

    def gone(parts, bit):
        return beside(*(parts[k] for k in parts if k & bit))

    def kept(parts, bit, got):
        keep = [k for k in parts if not k & bit]
        return {
            k: (parts[k].astype(F32) + got[:, i * width : (i + 1) * width].astype(F32)).astype(BF16)
            for i, k in enumerate(keep)
        }

    def step(parts, bit):
        return kept(parts, bit, swap(gone(parts, bit), "tensor", bit))

    def split_rows(value):
        return split_parts(value[:row_limit]), split_parts(value[row_limit:])

    def flat(parts):
        return [parts[k] for k in parts]

    low, high = t_bits[0], t_bits[-1]
    expert_mine, expert_other = split_rows(expert_sum)
    send_low, send_high = gone(expert_mine, low), gone(expert_other, high)
    g_up_4, g_up_own = first_send(blocks_far(g_up)), first_send(blocks_own(g_up))
    g_down_far, input_sum, input_sib, send_low, send_high, *rest = fence(
        g_down_far, input_sum, input_sib, send_low, send_high, *g_gate_4, *g_up_4, *g_up_own
    )
    g_up_own = rest[2 + n_kept :]
    g_gate_4, send_low, send_high, input_sib, *g_up_4 = fence(
        done(*rest[:2]), send_low, send_high, input_sib, *rest[2 : 2 + n_kept]
    )

    def panel(own, other):
        both = beside(own, other)
        mine = lax.dynamic_slice_in_dim(both, core * rows_w, rows_w, 0)
        got = across(lax.dynamic_slice_in_dim(both, (1 - core) * rows_w, rows_w, 0))
        whole = jnp.zeros((rows_w, 4 * hid), BF16)
        for block, u, c in (
            (mine[:, :hid], upper, core),
            (mine[:, hid:], 1 - upper, core),
            (got[:, :hid], upper, 1 - core),
            (got[:, hid:], 1 - upper, 1 - core),
        ):
            whole = lax.dynamic_update_slice(whole, block, (0, (u * 2 + c) * hid))
        return whole

    g_gate_far = z_far(g_gate_4)
    g_up_4 = shrink(*g_up_4)
    expert_mine = kept(expert_mine, low, swap(send_low, "tensor", low))
    expert_other = kept(expert_other, high, swap(send_high, "tensor", high))
    input_sum = (input_sum.astype(F32) + across(input_sib).astype(F32)).astype(BF16)
    input_mine, input_other = split_rows(input_sum)
    merged = len(t_bits) == 2
    if merged:
        send_high = beside(gone(expert_mine, high), gone(input_other, high))
        send_low = beside(gone(expert_other, low), gone(input_mine, low))
    else:
        send_high, send_low = gone(input_other, high), gone(input_mine, low)
    g_gate_far, expert_mine, expert_other, input_mine, input_other, send_low, send_high, *rest = (
        fence(
            g_gate_far, expert_mine, expert_other, input_mine, input_other, send_low, send_high,
            *g_up_4, *g_gate_own
        )
    )
    g_up_4, send_low, send_high, *g_gate_own = fence(
        done(*rest[:2]), send_low, send_high, *rest[2:]
    )

    g_up_far = z_far(g_up_4)
    g_gate_own = shrink(*g_gate_own)
    got_high, got_low = swap(send_high, "tensor", high), swap(send_low, "tensor", low)
    if merged:
        expert_mine = kept(expert_mine, high, got_high[:, :width])
        expert_other = kept(expert_other, low, got_low[:, :width])
        got_high, got_low = got_high[:, width:], got_low[:, width:]
    else:
        for bit in t_bits[1:]:
            expert_mine = step(expert_mine, bit)
        for bit in t_bits[:-1][::-1]:
            expert_other = step(expert_other, bit)
    input_other = kept(input_other, high, got_high)
    input_mine = kept(input_mine, low, got_low)
    last_own = tuple(beside(*both) for both in zip(g_up_own, first_send(blocks_own(g_down))))
    g_up_far, expert_mine, expert_other, input_mine, input_other, g_down_far, g_gate_far, *rest = fence(
        g_up_far, expert_mine[0], expert_other[0], input_mine, input_other, g_down_far, g_gate_far,
        *g_gate_own, *last_own
    )
    g_gate_own, last_own = rest[:2], rest[2:]

    last_own = done(*shrink(*last_own))
    g_up_own, g_down_own = last_own[:, :hid], last_own[:, hid:]
    expert_got = z_far(expert_other)
    for bit in t_bits[1:]:
        input_mine = step(input_mine, bit)
    for bit in t_bits[:-1][::-1]:
        input_other = step(input_other, bit)
    input_got = z_far(input_other[0])
    expert_cols = expert_mine.astype(F32) + expert_got.astype(F32)
    grad_cols = lax.dynamic_slice_in_dim(rows_grad, me_t * width, width, 1)
    weight_rows = jnp.sum(grad_cols.astype(F32) * expert_cols, axis=1)
    for bit in t_bits:
        weight_rows = weight_rows + swap(weight_rows, "tensor", bit)
    weight_grad = jnp.sum(jnp.where(match, weight_rows[:, None], 0.0), axis=0)
    mixed = mm_first(hot, (row_weight[:, None] * expert_cols).astype(BF16)).astype(BF16)
    gate_out, up_out, down_out, input_got = fence(
        panel(done(*g_gate_own), g_gate_far),
        panel(g_up_own, g_up_far),
        panel(g_down_own, g_down_far),
        input_got,
    )
    input_cols = (input_mine[0].astype(F32) + input_got.astype(F32)).astype(BF16)
    input_grad = mm_first(hot, input_cols).astype(BF16)
    return (mixed, input_grad, weight_grad, gate_out, up_out, down_out)


def solution(mesh):
    return jax.shard_map(
        local,
        mesh=mesh,
        in_specs=(
            P("dp", None),
            P("dp", None),
            P("dp", None),
            P("dp", None),
            P("dp", "tensor"),
            P("dp", "tensor"),
            P("dp", "tensor"),
        ),
        out_specs=(
            P("dp", "tensor"),
            P("dp", "tensor"),
            P("dp"),
            P("dp", "tensor"),
            P("dp", "tensor"),
            P("dp", "tensor"),
        ),
        check_vma=False,
    )
```

```python
import jax
import jax.numpy as jnp
from jax import lax
from jax.sharding import PartitionSpec as P

BF16 = jnp.bfloat16
F32 = jnp.float32


def dot(left, right, dims):
    return lax.dot_general(left, right, (dims, ((), ())), preferred_element_type=F32)


def mm(left, right):
    return dot(left, right, ((1,), (0,)))


def mm_last(left, right):
    return dot(left, right, ((1,), (1,)))


def mm_first(left, right):
    return dot(left, right, ((0,), (0,)))


def swap(value, axis, distance):
    size = lax.axis_size(axis)
    return lax.ppermute(value, axis, [(i, i ^ distance) for i in range(size)])


def fence(*values):
    return lax.optimization_barrier(values)


def select_rows(assign_block, combine_block, row_limit):
    expert_hit = assign_block == 0
    routed = jnp.any(expert_hit, axis=1)
    weight = jnp.sum(
        jnp.where(expert_hit, combine_block, jnp.zeros((), combine_block.dtype)), axis=1
    )
    place = jnp.cumsum(routed.astype(jnp.int32)) - 1
    match = routed[None, :] & (place[None, :] == jnp.arange(row_limit, dtype=jnp.int32)[:, None])
    row_weight = jnp.sum(jnp.where(match, weight[None, :], 0.0), axis=1)
    return (match, row_weight)


def cat(*values):
    return jnp.concatenate(values, axis=0)


def beside(*values):
    return jnp.concatenate(values, axis=1)


def by_bits(blocks, index):
    bit = 1
    while bit < len(blocks):
        flag = (index & bit) != 0
        blocks = [jnp.where(flag, blocks[p ^ bit], blocks[p]) for p in range(len(blocks))]
        bit *= 2
    return blocks


def local(tokens, assign, combine, cotangent, w_gate, w_up, w_down_t):
    token_total, depth = tokens.shape
    row_limit = token_total // 2
    n_dp = lax.axis_size("dp")
    n_tensor = lax.axis_size("tensor")
    me = lax.axis_index("dp")
    me_t = lax.axis_index("tensor")
    chip, core = me // 2, me % 2
    far = n_dp // 2
    upper = me // far
    rows_w = w_gate.shape[0]
    pair = 2 * rows_w
    n_chip = n_dp // 2
    hid = w_gate.shape[1] // 4
    width = depth // n_tensor
    mids = [1 << i for i in range(1, far.bit_length() - 1)]
    t_bits = [1 << i for i in range(n_tensor.bit_length() - 1)]

    def z_far(block):
        return swap(block, "dp", far)

    def across(block):
        return swap(block, "dp", 1)

    def grow(block):
        blocks = [block]
        for bit in mids:
            count, rows = len(blocks), block.shape[0]
            got = swap(cat(*blocks) if count > 1 else block, "dp", bit)
            blocks = blocks + [got[i * rows : (i + 1) * rows] for i in range(count)]
        return blocks

    def whole_panel(own, away):
        full = jnp.zeros((n_chip, pair, hid), BF16)
        for j in range(n_chip // 2):
            full = lax.dynamic_update_index_in_dim(full, own[j], chip ^ j, 0)
            full = lax.dynamic_update_index_in_dim(full, away[j], chip ^ j ^ (n_chip // 2), 0)
        return full.reshape(depth, hid)

    def block_of(panel, j):
        return lax.dynamic_index_in_dim(panel.reshape(n_chip, pair, hid), chip ^ j, 0, False)

    def blocks_own(panel):
        return {j: block_of(panel, j) for j in range(n_chip // 2)}

    def blocks_far(panel):
        return {j: block_of(panel, j ^ (n_chip // 2)) for j in range(n_chip // 2)}

    def add(blocks, got):
        return {
            j: (blocks[j].astype(F32) + got[i * pair : (i + 1) * pair].astype(F32)).astype(BF16)
            for i, j in enumerate(blocks)
        }

    def first_send(blocks):
        bit = mids[-1] // 2
        gone = [blocks[j] for j in blocks if j & bit]
        return (
            cat(*gone) if len(gone) > 1 else gone[0],
            *(blocks[j] for j in blocks if not j & bit),
        )

    def shrink(send, *kept):
        got = swap(send, "dp", mids[-1])
        for bit in mids[:-1][::-1]:
            blocks = add(dict(enumerate(kept)), got)
            count = len(blocks) // 2
            got = swap(cat(*(blocks[j + count] for j in range(count))), "dp", bit)
            kept = tuple(blocks[j] for j in range(count))
        return kept[0], got

    def done(kept, got):
        return (kept.astype(F32) + got.astype(F32)).astype(BF16)

    def part(w, u, c):
        return lax.dynamic_slice_in_dim(w, (u * 2 + c) * hid, hid, 1)

    def to_sibling(w):
        return beside(part(w, upper, 1 - core), part(w, 1 - upper, 1 - core))

    def by_core(mine, got):
        return jnp.where(core == 0, cat(mine, got), cat(got, mine))

    def pair_rows(w, got):
        mine = by_core(part(w, upper, core), got[:, :hid])
        other = by_core(part(w, 1 - upper, core), got[:, hid:])
        return mine, other

    gate_0 = lax.dynamic_slice_in_dim(w_gate, upper * 2 * hid, 2 * hid, 1)
    gate_4 = z_far(lax.dynamic_slice_in_dim(w_gate, (1 - upper) * 2 * hid, 2 * hid, 1))
    gate_own = grow(gate_0)
    match, row_weight = select_rows(assign, combine, row_limit)
    hot = match.astype(BF16)
    rows_in = mm(hot, tokens).astype(BF16)
    rows_grad = mm(hot, cotangent).astype(BF16)
    out_grad = (row_weight[:, None] * rows_grad.astype(F32)).astype(BF16)
    quarter = cat(
        *(lax.dynamic_slice_in_dim(v, me_t * width, width, 1) for v in (rows_in, out_grad))
    )
    send = cat(to_sibling(w_up), to_sibling(w_down_t))
    gate_4, quarter, rows_in, out_grad, send, *gate_own = fence(
        gate_4, quarter, rows_in, out_grad, send, *gate_own
    )

    quarter = z_far(quarter)
    gate_far = grow(gate_4)
    in_sib, out_sib = across(rows_in), across(out_grad)
    got = across(send)
    up_0, up_1 = pair_rows(w_up, got[:rows_w])
    down_0, down_1 = pair_rows(w_down_t, got[rows_w:])
    own = beside(up_0, down_0)
    quarter, in_sib, out_sib, own, up_1, down_1, *gate_far = fence(
        quarter, in_sib, out_sib, own, up_1, down_1, *gate_far
    )

    up_4 = z_far(up_1)
    own = grow(own)
    quarters = [quarter] + [swap(quarter, "tensor", k) for k in range(1, n_tensor)]
    gate_all = jnp.stack(gate_own + gate_far)
    gate_mine = lax.dynamic_slice_in_dim(gate_all, core * hid, hid, 2)
    gate_send = lax.dynamic_slice_in_dim(gate_all, (1 - core) * hid, hid, 2)
    up_4, gate_mine, gate_send, down_1, *rest = fence(
        up_4, gate_mine, gate_send, down_1, *quarters, *own
    )
    quarters, own = rest[: len(quarters)], rest[len(quarters) :]
    up_own, down_own = [b[:, :hid] for b in own], [b[:, hid:] for b in own]

    up_far = grow(up_4)
    down_4 = z_far(down_1)
    gate_got, *quarters = fence(across(gate_send), *quarters)
    gate = jnp.zeros((n_chip, 2, rows_w, hid), BF16)
    for j in range(n_chip):
        gate = lax.dynamic_update_slice(gate, gate_mine[j][None, None], (chip ^ j, core, 0, 0))
        gate = lax.dynamic_update_slice(gate, gate_got[j][None, None], (chip ^ j, 1 - core, 0, 0))
    gate = gate.reshape(depth, hid)

    def true_rows(first):
        return beside(*by_bits([q[first : first + row_limit] for q in quarters], me_t))

    in_away, out_away = true_rows(0), true_rows(row_limit)
    in_away_sib, out_away_sib = across(in_away), across(out_away)
    in_all = cat(rows_in, in_away, in_sib, in_away_sib)
    out_all = cat(out_grad, out_away, out_sib, out_away_sib)
    gate_pre = mm(in_all, gate)
    down_4, in_all, out_all, gate_pre, gate, *up_far = fence(
        down_4, in_all, out_all, gate_pre, gate, *up_far
    )

    down_far = grow(down_4)
    up = whole_panel(up_own, up_far)
    up_pre = mm(in_all, up)
    sigmoid_gate = jax.nn.sigmoid(gate_pre)
    hidden = (gate_pre * sigmoid_gate * up_pre).astype(BF16)
    g_down = mm_first(out_all, hidden).astype(BF16)
    g_down, hidden, up_pre, up, *down_far = fence(g_down, hidden, up_pre, up, *down_far)

    table = 2 * row_limit
    g_down_4 = first_send(blocks_far(g_down))
    n_kept = len(g_down_4)
    g_down_4 = shrink(*g_down_4)
    g_down_own = shrink(*first_send(blocks_own(g_down)))
    down = whole_panel(down_own, down_far)
    hidden_grad = mm(out_all, down)
    gate_grad = (
        hidden_grad * up_pre * sigmoid_gate * (1.0 + gate_pre * (1.0 - sigmoid_gate))
    ).astype(BF16)
    up_grad = (hidden_grad * gate_pre * sigmoid_gate).astype(BF16)
    g_gate = mm_first(in_all, gate_grad).astype(BF16)
    expert_got = across(mm_last(hidden[table:], down).astype(BF16))

    def input_part(rows):
        return mm_last(gate_grad[rows], gate) + mm_last(up_grad[rows], up)

    input_sib = input_part(slice(table, None)).astype(BF16)
    down, gate_grad, up_grad, g_gate, expert_got, input_sib, *rest = fence(
        down, gate_grad, up_grad, g_gate, expert_got, input_sib, *g_down_4, *g_down_own
    )
    g_down_own = rest[2:]
    g_down_4, input_sib, g_gate = fence(done(*rest[:2]), input_sib, g_gate)
    g_gate_4, g_gate_own = first_send(blocks_far(g_gate)), first_send(blocks_own(g_gate))

    g_down_far = z_far(g_down_4)
    g_gate_4 = shrink(*g_gate_4)
    input_got, in_all, gate_grad, up_grad, hidden = fence(
        across(input_sib[:row_limit]), in_all, gate_grad, up_grad, hidden
    )
    input_got = cat(input_got, across(input_sib[row_limit:]))
    g_up = mm_first(in_all, up_grad).astype(BF16)
    expert_sum = (mm_last(hidden[:table], down) + expert_got.astype(F32)).astype(BF16)
    input_sum = (input_part(slice(None, table)) + input_got.astype(F32)).astype(BF16)

    def split_parts(value):
        return {
            k: lax.dynamic_slice_in_dim(value, (me_t ^ k) * width, width, 1)
            for k in range(n_tensor)
        }

    def gone(parts, bit):
        return beside(*(parts[k] for k in parts if k & bit))

    def kept(parts, bit, got):
        keep = [k for k in parts if not k & bit]
        return {
            k: (parts[k].astype(F32) + got[:, i * width : (i + 1) * width].astype(F32)).astype(BF16)
            for i, k in enumerate(keep)
        }

    def step(parts, bit):
        return kept(parts, bit, swap(gone(parts, bit), "tensor", bit))

    def split_rows(value):
        return split_parts(value[:row_limit]), split_parts(value[row_limit:])

    def flat(parts):
        return [parts[k] for k in parts]

    low, high = t_bits[0], t_bits[-1]
    expert_mine, expert_other = split_rows(expert_sum)
    send_low, send_high = gone(expert_mine, low), gone(expert_other, high)
    g_up_4, g_up_own = first_send(blocks_far(g_up)), first_send(blocks_own(g_up))
    g_down_far, input_sum, send_low, send_high, *rest = fence(
        g_down_far, input_sum, send_low, send_high, *g_gate_4, *g_up_4, *g_up_own
    )
    g_up_own = rest[2 + n_kept :]
    g_gate_4, send_low, send_high, input_sum, *g_up_4 = fence(
        done(*rest[:2]), send_low, send_high, input_sum, *rest[2 : 2 + n_kept]
    )

    def panel(own, other):
        both = beside(own, other)
        mine = lax.dynamic_slice_in_dim(both, core * rows_w, rows_w, 0)
        got = across(lax.dynamic_slice_in_dim(both, (1 - core) * rows_w, rows_w, 0))
        whole = jnp.zeros((rows_w, 4 * hid), BF16)
        for block, u, c in (
            (mine[:, :hid], upper, core),
            (mine[:, hid:], 1 - upper, core),
            (got[:, :hid], upper, 1 - core),
            (got[:, hid:], 1 - upper, 1 - core),
        ):
            whole = lax.dynamic_update_slice(whole, block, (0, (u * 2 + c) * hid))
        return whole

    g_gate_far = z_far(g_gate_4)
    g_up_4 = shrink(*g_up_4)
    expert_mine = kept(expert_mine, low, swap(send_low, "tensor", low))
    expert_other = kept(expert_other, high, swap(send_high, "tensor", high))
    input_mine, input_other = split_rows(input_sum)
    merged = len(t_bits) == 2
    if merged:
        send_high = beside(gone(expert_mine, high), gone(input_other, high))
        send_low = beside(gone(expert_other, low), gone(input_mine, low))
    else:
        send_high, send_low = gone(input_other, high), gone(input_mine, low)
    g_gate_far, expert_mine, expert_other, input_mine, input_other, send_low, send_high, *rest = (
        fence(
            g_gate_far, expert_mine, expert_other, input_mine, input_other, send_low, send_high,
            *g_up_4, *g_gate_own
        )
    )
    g_up_4, send_low, send_high, *g_gate_own = fence(
        done(*rest[:2]), send_low, send_high, *rest[2:]
    )

    g_up_far = z_far(g_up_4)
    g_gate_own = shrink(*g_gate_own)
    got_high, got_low = swap(send_high, "tensor", high), swap(send_low, "tensor", low)
    if merged:
        expert_mine = kept(expert_mine, high, got_high[:, :width])
        expert_other = kept(expert_other, low, got_low[:, :width])
        got_high, got_low = got_high[:, width:], got_low[:, width:]
    else:
        for bit in t_bits[1:]:
            expert_mine = step(expert_mine, bit)
        for bit in t_bits[:-1][::-1]:
            expert_other = step(expert_other, bit)
    input_other = kept(input_other, high, got_high)
    input_mine = kept(input_mine, low, got_low)
    g_up_far, expert_mine, expert_other, input_mine, input_other, g_down_far, g_gate_far, *rest = fence(
        g_up_far, expert_mine[0], expert_other[0], input_mine, input_other, g_down_far, g_gate_far,
        *g_gate_own, *g_down_own, *g_up_own
    )
    g_gate_own, g_down_own, g_up_own = rest[:2], rest[2:4], rest[4:]

    g_up_own = shrink(*g_up_own)
    expert_got = z_far(expert_other)
    for bit in t_bits[1:]:
        input_mine = step(input_mine, bit)
    for bit in t_bits[:-1][::-1]:
        input_other = step(input_other, bit)
    input_other, g_down_far, g_gate_far, *rest = fence(
        input_other[0], g_down_far, g_gate_far, *g_down_own, *g_gate_own
    )
    g_down_own, g_gate_own = rest[:2], rest[2:]
    input_got = z_far(input_other)
    expert_cols = expert_mine.astype(F32) + expert_got.astype(F32)
    grad_cols = lax.dynamic_slice_in_dim(rows_grad, me_t * width, width, 1)
    weight_rows = jnp.sum(grad_cols.astype(F32) * expert_cols, axis=1)
    for bit in t_bits:
        weight_rows = weight_rows + swap(weight_rows, "tensor", bit)
    weight_grad = jnp.sum(jnp.where(match, weight_rows[:, None], 0.0), axis=0)
    mixed = mm_first(hot, (row_weight[:, None] * expert_cols).astype(BF16)).astype(BF16)
    input_cols = (input_mine[0].astype(F32) + input_got.astype(F32)).astype(BF16)
    input_grad = mm_first(hot, input_cols).astype(BF16)
    return (
        mixed,
        input_grad,
        weight_grad,
        panel(done(*g_gate_own), g_gate_far),
        panel(done(*g_up_own), g_up_far),
        panel(done(*g_down_own), g_down_far),
    )


def solution(mesh):
    return jax.shard_map(
        local,
        mesh=mesh,
        in_specs=(
            P("dp", None),
            P("dp", None),
            P("dp", None),
            P("dp", None),
            P("dp", "tensor"),
            P("dp", "tensor"),
            P("dp", "tensor"),
        ),
        out_specs=(
            P("dp", "tensor"),
            P("dp", "tensor"),
            P("dp"),
            P("dp", "tensor"),
            P("dp", "tensor"),
            P("dp", "tensor"),
        ),
        check_vma=False,
    )
```

```python
import jax
import jax.numpy as jnp
from jax import lax
from jax.sharding import PartitionSpec as P

BF16 = jnp.bfloat16
F32 = jnp.float32


def dot(left, right, dims):
    return lax.dot_general(left, right, (dims, ((), ())), preferred_element_type=F32)


def mm(left, right):
    return dot(left, right, ((1,), (0,)))


def mm_last(left, right):
    return dot(left, right, ((1,), (1,)))


def mm_first(left, right):
    return dot(left, right, ((0,), (0,)))


def swap(value, axis, distance):
    size = lax.axis_size(axis)
    return lax.ppermute(value, axis, [(i, i ^ distance) for i in range(size)])


def fence(*values):
    return lax.optimization_barrier(values)


def select_rows(assign_block, combine_block, row_limit):
    expert_hit = assign_block == 0
    routed = jnp.any(expert_hit, axis=1)
    weight = jnp.sum(
        jnp.where(expert_hit, combine_block, jnp.zeros((), combine_block.dtype)), axis=1
    )
    place = jnp.cumsum(routed.astype(jnp.int32)) - 1
    match = routed[None, :] & (place[None, :] == jnp.arange(row_limit, dtype=jnp.int32)[:, None])
    row_weight = jnp.sum(jnp.where(match, weight[None, :], 0.0), axis=1)
    return (match, row_weight)


def cat(*values):
    return jnp.concatenate(values, axis=0)


def beside(*values):
    return jnp.concatenate(values, axis=1)


def by_bits(blocks, index):
    bit = 1
    while bit < len(blocks):
        flag = (index & bit) != 0
        blocks = [jnp.where(flag, blocks[p ^ bit], blocks[p]) for p in range(len(blocks))]
        bit *= 2
    return blocks


def local(tokens, assign, combine, cotangent, w_gate, w_up, w_down_t):
    token_total, depth = tokens.shape
    row_limit = token_total // 2
    n_dp = lax.axis_size("dp")
    n_tensor = lax.axis_size("tensor")
    me = lax.axis_index("dp")
    me_t = lax.axis_index("tensor")
    chip, core = me // 2, me % 2
    far = n_dp // 2
    upper = me // far
    rows_w = w_gate.shape[0]
    pair = 2 * rows_w
    n_chip = n_dp // 2
    hid = w_gate.shape[1] // 4
    width = depth // n_tensor
    mids = [1 << i for i in range(1, far.bit_length() - 1)]
    t_bits = [1 << i for i in range(n_tensor.bit_length() - 1)]

    def z_far(block):
        return swap(block, "dp", far)

    def across(block):
        return swap(block, "dp", 1)

    def grow(block):
        blocks = [block]
        for bit in mids:
            count, rows = len(blocks), block.shape[0]
            got = swap(cat(*blocks) if count > 1 else block, "dp", bit)
            blocks = blocks + [got[i * rows : (i + 1) * rows] for i in range(count)]
        return blocks

    def whole_panel(own, away):
        full = jnp.zeros((n_chip, pair, hid), BF16)
        for j in range(n_chip // 2):
            full = lax.dynamic_update_index_in_dim(full, own[j], chip ^ j, 0)
            full = lax.dynamic_update_index_in_dim(full, away[j], chip ^ j ^ (n_chip // 2), 0)
        return full.reshape(depth, hid)

    def block_of(panel, j):
        return lax.dynamic_index_in_dim(panel.reshape(n_chip, pair, hid), chip ^ j, 0, False)

    def blocks_own(panel):
        return {j: block_of(panel, j) for j in range(n_chip // 2)}

    def blocks_far(panel):
        return {j: block_of(panel, j ^ (n_chip // 2)) for j in range(n_chip // 2)}

    def add(blocks, got):
        return {
            j: (blocks[j].astype(F32) + got[i * pair : (i + 1) * pair].astype(F32)).astype(BF16)
            for i, j in enumerate(blocks)
        }

    def first_send(blocks):
        bit = mids[-1] // 2
        gone = [blocks[j] for j in blocks if j & bit]
        return (
            cat(*gone) if len(gone) > 1 else gone[0],
            *(blocks[j] for j in blocks if not j & bit),
        )

    def shrink(send, *kept):
        got = swap(send, "dp", mids[-1])
        for bit in mids[:-1][::-1]:
            blocks = add(dict(enumerate(kept)), got)
            count = len(blocks) // 2
            got = swap(cat(*(blocks[j + count] for j in range(count))), "dp", bit)
            kept = tuple(blocks[j] for j in range(count))
        return kept[0], got

    def done(kept, got):
        return (kept.astype(F32) + got.astype(F32)).astype(BF16)

    def part(w, u, c):
        return lax.dynamic_slice_in_dim(w, (u * 2 + c) * hid, hid, 1)

    def to_sibling(w):
        return beside(part(w, upper, 1 - core), part(w, 1 - upper, 1 - core))

    def by_core(mine, got):
        return jnp.where(core == 0, cat(mine, got), cat(got, mine))

    def pair_rows(w, got):
        mine = by_core(part(w, upper, core), got[:, :hid])
        other = by_core(part(w, 1 - upper, core), got[:, hid:])
        return mine, other

    gate_0 = lax.dynamic_slice_in_dim(w_gate, upper * 2 * hid, 2 * hid, 1)
    gate_4 = z_far(lax.dynamic_slice_in_dim(w_gate, (1 - upper) * 2 * hid, 2 * hid, 1))
    gate_own = grow(gate_0)
    match, row_weight = select_rows(assign, combine, row_limit)
    hot = match.astype(BF16)
    rows_in = mm(hot, tokens).astype(BF16)
    rows_grad = mm(hot, cotangent).astype(BF16)
    out_grad = (row_weight[:, None] * rows_grad.astype(F32)).astype(BF16)
    quarter = cat(
        *(lax.dynamic_slice_in_dim(v, me_t * width, width, 1) for v in (rows_in, out_grad))
    )
    send = cat(to_sibling(w_up), to_sibling(w_down_t))
    gate_4, quarter, rows_in, out_grad, send, *gate_own = fence(
        gate_4, quarter, rows_in, out_grad, send, *gate_own
    )

    quarter = z_far(quarter)
    gate_far = grow(gate_4)
    in_sib, out_sib = across(rows_in), across(out_grad)
    got = across(send)
    up_0, up_1 = pair_rows(w_up, got[:rows_w])
    down_0, down_1 = pair_rows(w_down_t, got[rows_w:])
    own = beside(up_0, down_0)
    quarter, in_sib, out_sib, own, up_1, down_1, *gate_far = fence(
        quarter, in_sib, out_sib, own, up_1, down_1, *gate_far
    )

    up_4 = z_far(up_1)
    own = grow(own)
    quarters = [quarter] + [swap(quarter, "tensor", k) for k in range(1, n_tensor)]
    gate_all = jnp.stack(gate_own + gate_far)
    gate_mine = lax.dynamic_slice_in_dim(gate_all, core * hid, hid, 2)
    gate_send = lax.dynamic_slice_in_dim(gate_all, (1 - core) * hid, hid, 2)
    up_4, gate_mine, gate_send, down_1, *rest = fence(
        up_4, gate_mine, gate_send, down_1, *quarters, *own
    )
    quarters, own = rest[: len(quarters)], rest[len(quarters) :]
    up_own, down_own = [b[:, :hid] for b in own], [b[:, hid:] for b in own]

    up_far = grow(up_4)
    down_4 = z_far(down_1)
    gate_got, *quarters = fence(across(gate_send), *quarters)
    gate = jnp.zeros((n_chip, 2, rows_w, hid), BF16)
    for j in range(n_chip):
        gate = lax.dynamic_update_slice(gate, gate_mine[j][None, None], (chip ^ j, core, 0, 0))
        gate = lax.dynamic_update_slice(gate, gate_got[j][None, None], (chip ^ j, 1 - core, 0, 0))
    gate = gate.reshape(depth, hid)

    def true_rows(first):
        return beside(*by_bits([q[first : first + row_limit] for q in quarters], me_t))

    in_away, out_away = true_rows(0), true_rows(row_limit)
    in_away_sib, out_away_sib = across(in_away), across(out_away)
    in_all = cat(rows_in, in_away, in_sib, in_away_sib)
    out_all = cat(out_grad, out_away, out_sib, out_away_sib)
    gate_pre = mm(in_all, gate)
    down_4, in_all, out_all, gate_pre, gate, *up_far = fence(
        down_4, in_all, out_all, gate_pre, gate, *up_far
    )

    down_far = grow(down_4)
    up = whole_panel(up_own, up_far)
    up_pre = mm(in_all, up)
    sigmoid_gate = jax.nn.sigmoid(gate_pre)
    hidden = (gate_pre * sigmoid_gate * up_pre).astype(BF16)
    g_down = mm_first(out_all, hidden).astype(BF16)
    g_down, hidden, up_pre, up, *down_far = fence(g_down, hidden, up_pre, up, *down_far)

    table = 2 * row_limit
    g_down_4 = first_send(blocks_far(g_down))
    n_kept = len(g_down_4)
    g_down_4 = shrink(*g_down_4)
    g_down_own = shrink(*first_send(blocks_own(g_down)))
    down = whole_panel(down_own, down_far)
    hidden_grad = mm(out_all, down)
    gate_grad = (
        hidden_grad * up_pre * sigmoid_gate * (1.0 + gate_pre * (1.0 - sigmoid_gate))
    ).astype(BF16)
    up_grad = (hidden_grad * gate_pre * sigmoid_gate).astype(BF16)
    g_gate = mm_first(in_all, gate_grad).astype(BF16)
    expert_got = across(mm_last(hidden[table:], down).astype(BF16))

    def input_part(rows):
        return mm_last(gate_grad[rows], gate) + mm_last(up_grad[rows], up)

    input_sib = input_part(slice(table, None)).astype(BF16)
    input_a, input_b = input_sib[:row_limit], input_sib[row_limit:]
    down, gate_grad, up_grad, g_gate, expert_got, input_a, input_b, *rest = fence(
        down, gate_grad, up_grad, g_gate, expert_got, input_a, input_b, *g_down_4, *g_down_own
    )
    g_down_own = rest[2:]
    g_down_4, input_a, input_b, g_gate = fence(done(*rest[:2]), input_a, input_b, g_gate)
    g_gate_4, g_gate_own = first_send(blocks_far(g_gate)), first_send(blocks_own(g_gate))

    g_down_far = z_far(g_down_4)
    g_gate_4 = shrink(*g_gate_4)
    input_got, in_all, gate_grad, up_grad, hidden = fence(
        across(input_a), in_all, gate_grad, up_grad, hidden
    )
    input_got = cat(input_got, across(input_b))
    g_up = mm_first(in_all, up_grad).astype(BF16)
    expert_sum = (mm_last(hidden[:table], down) + expert_got.astype(F32)).astype(BF16)
    input_sum = (input_part(slice(None, table)) + input_got.astype(F32)).astype(BF16)

    def split_parts(value):
        return {
            k: lax.dynamic_slice_in_dim(value, (me_t ^ k) * width, width, 1)
            for k in range(n_tensor)
        }

    def gone(parts, bit):
        return beside(*(parts[k] for k in parts if k & bit))

    def kept(parts, bit, got):
        keep = [k for k in parts if not k & bit]
        return {
            k: (parts[k].astype(F32) + got[:, i * width : (i + 1) * width].astype(F32)).astype(BF16)
            for i, k in enumerate(keep)
        }

    def step(parts, bit):
        return kept(parts, bit, swap(gone(parts, bit), "tensor", bit))

    def split_rows(value):
        return split_parts(value[:row_limit]), split_parts(value[row_limit:])

    def flat(parts):
        return [parts[k] for k in parts]

    low, high = t_bits[0], t_bits[-1]
    expert_mine, expert_other = split_rows(expert_sum)
    send_low, send_high = gone(expert_mine, low), gone(expert_other, high)
    g_up_4, g_up_own = first_send(blocks_far(g_up)), first_send(blocks_own(g_up))
    g_down_far, input_sum, send_low, send_high, *rest = fence(
        g_down_far, input_sum, send_low, send_high, *g_gate_4, *g_up_4, *g_up_own
    )
    g_up_own = rest[2 + n_kept :]
    g_gate_4, send_low, send_high, input_sum, *g_up_4 = fence(
        done(*rest[:2]), send_low, send_high, input_sum, *rest[2 : 2 + n_kept]
    )

    def halves_of(own, other):
        both = beside(own, other)
        mine = lax.dynamic_slice_in_dim(both, core * rows_w, rows_w, 0)
        return mine, lax.dynamic_slice_in_dim(both, (1 - core) * rows_w, rows_w, 0)

    def panel(mine, got):
        whole = jnp.zeros((rows_w, 4 * hid), BF16)
        for block, u, c in (
            (mine[:, :hid], upper, core),
            (mine[:, hid:], 1 - upper, core),
            (got[:, :hid], upper, 1 - core),
            (got[:, hid:], 1 - upper, 1 - core),
        ):
            whole = lax.dynamic_update_slice(whole, block, (0, (u * 2 + c) * hid))
        return whole

    g_gate_far = z_far(g_gate_4)
    g_up_4 = shrink(*g_up_4)
    expert_mine = kept(expert_mine, low, swap(send_low, "tensor", low))
    expert_other = kept(expert_other, high, swap(send_high, "tensor", high))
    input_mine, input_other = split_rows(input_sum)
    merged = len(t_bits) == 2
    if merged:
        send_high = beside(gone(expert_mine, high), gone(input_other, high))
        send_low = beside(gone(expert_other, low), gone(input_mine, low))
    else:
        send_high, send_low = gone(input_other, high), gone(input_mine, low)
    g_gate_far, expert_mine, expert_other, input_mine, input_other, send_low, send_high, *rest = (
        fence(
            g_gate_far, expert_mine, expert_other, input_mine, input_other, send_low, send_high,
            *g_up_4, *g_gate_own
        )
    )
    g_up_4, send_low, send_high, *g_gate_own = fence(
        done(*rest[:2]), send_low, send_high, *rest[2:]
    )

    g_up_far = z_far(g_up_4)
    g_gate_own = shrink(*g_gate_own)
    got_high, got_low = swap(send_high, "tensor", high), swap(send_low, "tensor", low)
    if merged:
        expert_mine = kept(expert_mine, high, got_high[:, :width])
        expert_other = kept(expert_other, low, got_low[:, :width])
        got_high, got_low = got_high[:, width:], got_low[:, width:]
    else:
        for bit in t_bits[1:]:
            expert_mine = step(expert_mine, bit)
        for bit in t_bits[:-1][::-1]:
            expert_other = step(expert_other, bit)
    input_other = kept(input_other, high, got_high)
    input_mine = kept(input_mine, low, got_low)
    g_up_far, expert_mine, expert_other, input_mine, input_other, g_down_far, g_gate_far, *rest = fence(
        g_up_far, expert_mine[0], expert_other[0], input_mine, input_other, g_down_far, g_gate_far,
        *g_gate_own, *g_down_own, *g_up_own
    )
    g_gate_own, g_down_own, g_up_own = rest[:2], rest[2:4], rest[4:]

    g_up_own = shrink(*g_up_own)
    expert_got = z_far(expert_other)
    for bit in t_bits[1:]:
        input_mine = step(input_mine, bit)
    for bit in t_bits[:-1][::-1]:
        input_other = step(input_other, bit)
    input_mine, input_other, g_down_far, g_gate_far, *rest = fence(
        input_mine[0], input_other[0], g_down_far, g_gate_far, *g_down_own, *g_gate_own
    )
    down_mine, down_send = halves_of(done(*rest[:2]), g_down_far)
    gate_mine, gate_send = halves_of(done(*rest[2:]), g_gate_far)
    got = across(cat(down_send, gate_send))
    down_out, gate_out = panel(down_mine, got[:rows_w]), panel(gate_mine, got[rows_w:])
    up_mine, up_send = halves_of(done(*g_up_own), g_up_far)
    up_out = panel(up_mine, across(up_send))
    input_got = z_far(input_other)
    expert_cols = expert_mine.astype(F32) + expert_got.astype(F32)
    grad_cols = lax.dynamic_slice_in_dim(rows_grad, me_t * width, width, 1)
    weight_rows = jnp.sum(grad_cols.astype(F32) * expert_cols, axis=1)
    for bit in t_bits:
        weight_rows = weight_rows + swap(weight_rows, "tensor", bit)
    weight_grad = jnp.sum(jnp.where(match, weight_rows[:, None], 0.0), axis=0)
    mixed = mm_first(hot, (row_weight[:, None] * expert_cols).astype(BF16)).astype(BF16)
    input_cols = (input_mine.astype(F32) + input_got.astype(F32)).astype(BF16)
    input_grad = mm_first(hot, input_cols).astype(BF16)
    return (mixed, input_grad, weight_grad, gate_out, up_out, down_out)


def solution(mesh):
    return jax.shard_map(
        local,
        mesh=mesh,
        in_specs=(
            P("dp", None),
            P("dp", None),
            P("dp", None),
            P("dp", None),
            P("dp", "tensor"),
            P("dp", "tensor"),
            P("dp", "tensor"),
        ),
        out_specs=(
            P("dp", "tensor"),
            P("dp", "tensor"),
            P("dp"),
            P("dp", "tensor"),
            P("dp", "tensor"),
            P("dp", "tensor"),
        ),
        check_vma=False,
    )
```

```python
import jax
import jax.numpy as jnp
from jax import lax
from jax.sharding import PartitionSpec as P

BF16 = jnp.bfloat16
F32 = jnp.float32


def dot(left, right, dims):
    return lax.dot_general(left, right, (dims, ((), ())), preferred_element_type=F32)


def mm(left, right):
    return dot(left, right, ((1,), (0,)))


def mm_last(left, right):
    return dot(left, right, ((1,), (1,)))


def mm_first(left, right):
    return dot(left, right, ((0,), (0,)))


def swap(value, axis, distance):
    size = lax.axis_size(axis)
    return lax.ppermute(value, axis, [(i, i ^ distance) for i in range(size)])


def fence(*values):
    return lax.optimization_barrier(values)


def select_rows(assign_block, combine_block, row_limit):
    expert_hit = assign_block == 0
    routed = jnp.any(expert_hit, axis=1)
    weight = jnp.sum(
        jnp.where(expert_hit, combine_block, jnp.zeros((), combine_block.dtype)), axis=1
    )
    place = jnp.cumsum(routed.astype(jnp.int32)) - 1
    match = routed[None, :] & (place[None, :] == jnp.arange(row_limit, dtype=jnp.int32)[:, None])
    row_weight = jnp.sum(jnp.where(match, weight[None, :], 0.0), axis=1)
    return (match, row_weight)


def cat(*values):
    return jnp.concatenate(values, axis=0)


def beside(*values):
    return jnp.concatenate(values, axis=1)


def by_bits(blocks, index):
    bit = 1
    while bit < len(blocks):
        flag = (index & bit) != 0
        blocks = [jnp.where(flag, blocks[p ^ bit], blocks[p]) for p in range(len(blocks))]
        bit *= 2
    return blocks


def local(tokens, assign, combine, cotangent, w_gate, w_up, w_down_t):
    token_total, depth = tokens.shape
    row_limit = token_total // 2
    n_dp = lax.axis_size("dp")
    n_tensor = lax.axis_size("tensor")
    me = lax.axis_index("dp")
    me_t = lax.axis_index("tensor")
    chip, core = me // 2, me % 2
    far = n_dp // 2
    upper = me // far
    rows_w = w_gate.shape[0]
    pair = 2 * rows_w
    n_chip = n_dp // 2
    hid = w_gate.shape[1] // 4
    width = depth // n_tensor
    mids = [1 << i for i in range(1, far.bit_length() - 1)]
    t_bits = [1 << i for i in range(n_tensor.bit_length() - 1)]

    def z_far(block):
        return swap(block, "dp", far)

    def across(block):
        return swap(block, "dp", 1)

    def grow(block):
        blocks = [block]
        for bit in mids:
            count, rows = len(blocks), block.shape[0]
            got = swap(cat(*blocks) if count > 1 else block, "dp", bit)
            blocks = blocks + [got[i * rows : (i + 1) * rows] for i in range(count)]
        return blocks

    def whole_panel(own, away):
        full = jnp.zeros((n_chip, pair, hid), BF16)
        for j in range(n_chip // 2):
            full = lax.dynamic_update_index_in_dim(full, own[j], chip ^ j, 0)
            full = lax.dynamic_update_index_in_dim(full, away[j], chip ^ j ^ (n_chip // 2), 0)
        return full.reshape(depth, hid)

    def block_of(panel, j):
        return lax.dynamic_index_in_dim(panel.reshape(n_chip, pair, hid), chip ^ j, 0, False)

    def blocks_own(panel):
        return {j: block_of(panel, j) for j in range(n_chip // 2)}

    def blocks_far(panel):
        return {j: block_of(panel, j ^ (n_chip // 2)) for j in range(n_chip // 2)}

    def add(blocks, got):
        return {
            j: (blocks[j].astype(F32) + got[i * pair : (i + 1) * pair].astype(F32)).astype(BF16)
            for i, j in enumerate(blocks)
        }

    def first_send(blocks):
        bit = mids[-1] // 2
        gone = [blocks[j] for j in blocks if j & bit]
        return (
            cat(*gone) if len(gone) > 1 else gone[0],
            *(blocks[j] for j in blocks if not j & bit),
        )

    def shrink(send, *kept):
        got = swap(send, "dp", mids[-1])
        for bit in mids[:-1][::-1]:
            blocks = add(dict(enumerate(kept)), got)
            count = len(blocks) // 2
            got = swap(cat(*(blocks[j + count] for j in range(count))), "dp", bit)
            kept = tuple(blocks[j] for j in range(count))
        return kept[0], got

    def done(kept, got):
        return (kept.astype(F32) + got.astype(F32)).astype(BF16)

    def part(w, u, c):
        return lax.dynamic_slice_in_dim(w, (u * 2 + c) * hid, hid, 1)

    def to_sibling(w):
        return beside(part(w, upper, 1 - core), part(w, 1 - upper, 1 - core))

    def by_core(mine, got):
        return jnp.where(core == 0, cat(mine, got), cat(got, mine))

    def pair_rows(w, got):
        mine = by_core(part(w, upper, core), got[:, :hid])
        other = by_core(part(w, 1 - upper, core), got[:, hid:])
        return mine, other

    gate_0 = lax.dynamic_slice_in_dim(w_gate, upper * 2 * hid, 2 * hid, 1)
    gate_4 = z_far(lax.dynamic_slice_in_dim(w_gate, (1 - upper) * 2 * hid, 2 * hid, 1))
    gate_own = grow(gate_0)
    match, row_weight = select_rows(assign, combine, row_limit)
    hot = match.astype(BF16)
    rows_in = mm(hot, tokens).astype(BF16)
    rows_grad = mm(hot, cotangent).astype(BF16)
    out_grad = (row_weight[:, None] * rows_grad.astype(F32)).astype(BF16)
    quarter = cat(
        *(lax.dynamic_slice_in_dim(v, me_t * width, width, 1) for v in (rows_in, out_grad))
    )
    send = cat(to_sibling(w_up), to_sibling(w_down_t))
    gate_4, quarter, rows_in, out_grad, send, *gate_own = fence(
        gate_4, quarter, rows_in, out_grad, send, *gate_own
    )

    quarter = z_far(quarter)
    gate_far = grow(gate_4)
    in_sib, out_sib = across(rows_in), across(out_grad)
    got = across(send)
    up_0, up_1 = pair_rows(w_up, got[:rows_w])
    down_0, down_1 = pair_rows(w_down_t, got[rows_w:])
    own = beside(up_0, down_0)
    quarter, in_sib, out_sib, own, up_1, down_1, *gate_far = fence(
        quarter, in_sib, out_sib, own, up_1, down_1, *gate_far
    )

    up_4 = z_far(up_1)
    own = grow(own)
    quarters = [quarter] + [swap(quarter, "tensor", k) for k in range(1, n_tensor)]
    gate_all = jnp.stack(gate_own + gate_far)
    gate_mine = lax.dynamic_slice_in_dim(gate_all, core * hid, hid, 2)
    gate_send = lax.dynamic_slice_in_dim(gate_all, (1 - core) * hid, hid, 2)
    up_4, gate_mine, gate_send, down_1, *rest = fence(
        up_4, gate_mine, gate_send, down_1, *quarters, *own
    )
    quarters, own = rest[: len(quarters)], rest[len(quarters) :]
    up_own, down_own = [b[:, :hid] for b in own], [b[:, hid:] for b in own]

    up_far = grow(up_4)
    down_4 = z_far(down_1)
    gate_got, *quarters = fence(across(gate_send), *quarters)
    gate = jnp.zeros((n_chip, 2, rows_w, hid), BF16)
    for j in range(n_chip):
        gate = lax.dynamic_update_slice(gate, gate_mine[j][None, None], (chip ^ j, core, 0, 0))
        gate = lax.dynamic_update_slice(gate, gate_got[j][None, None], (chip ^ j, 1 - core, 0, 0))
    gate = gate.reshape(depth, hid)

    def true_rows(first):
        return beside(*by_bits([q[first : first + row_limit] for q in quarters], me_t))

    in_away, out_away = true_rows(0), true_rows(row_limit)
    in_away_sib, out_away_sib = across(in_away), across(out_away)
    in_all = cat(rows_in, in_away, in_sib, in_away_sib)
    out_all = cat(out_grad, out_away, out_sib, out_away_sib)
    gate_pre = mm(in_all, gate)
    down_4, in_all, out_all, gate_pre, gate, *up_far = fence(
        down_4, in_all, out_all, gate_pre, gate, *up_far
    )

    down_far = grow(down_4)
    up = whole_panel(up_own, up_far)
    up_pre = mm(in_all, up)
    sigmoid_gate = jax.nn.sigmoid(gate_pre)
    hidden = (gate_pre * sigmoid_gate * up_pre).astype(BF16)
    g_down = mm_first(out_all, hidden).astype(BF16)
    g_down, hidden, up_pre, up, *down_far = fence(g_down, hidden, up_pre, up, *down_far)

    table = 2 * row_limit
    g_down_4 = first_send(blocks_far(g_down))
    n_kept = len(g_down_4)
    g_down_4 = shrink(*g_down_4)
    g_down_own = shrink(*first_send(blocks_own(g_down)))
    down = whole_panel(down_own, down_far)
    hidden_grad = mm(out_all, down)
    gate_grad = (
        hidden_grad * up_pre * sigmoid_gate * (1.0 + gate_pre * (1.0 - sigmoid_gate))
    ).astype(BF16)
    up_grad = (hidden_grad * gate_pre * sigmoid_gate).astype(BF16)
    g_gate = mm_first(in_all, gate_grad).astype(BF16)
    expert_got = across(mm_last(hidden[table:], down).astype(BF16))

    def input_part(rows):
        return mm_last(gate_grad[rows], gate) + mm_last(up_grad[rows], up)

    input_sib = input_part(slice(table, None)).astype(BF16)
    down, gate_grad, up_grad, g_gate, expert_got, input_sib, *rest = fence(
        down, gate_grad, up_grad, g_gate, expert_got, input_sib, *g_down_4, *g_down_own
    )
    g_down_own = rest[2:]
    g_down_4, input_sib, g_gate = fence(done(*rest[:2]), input_sib, g_gate)
    g_gate_4, g_gate_own = first_send(blocks_far(g_gate)), first_send(blocks_own(g_gate))

    g_down_far = z_far(g_down_4)
    g_gate_4 = shrink(*g_gate_4)
    input_got, in_all, gate_grad, up_grad, hidden = fence(
        across(input_sib[:row_limit]), in_all, gate_grad, up_grad, hidden
    )
    input_got = cat(input_got, across(input_sib[row_limit:]))
    g_up = mm_first(in_all, up_grad).astype(BF16)
    expert_sum = (mm_last(hidden[:table], down) + expert_got.astype(F32)).astype(BF16)
    input_sum = (input_part(slice(None, table)) + input_got.astype(F32)).astype(BF16)

    def split_parts(value):
        return {
            k: lax.dynamic_slice_in_dim(value, (me_t ^ k) * width, width, 1)
            for k in range(n_tensor)
        }

    def gone(parts, bit):
        return beside(*(parts[k] for k in parts if k & bit))

    def kept(parts, bit, got):
        keep = [k for k in parts if not k & bit]
        return {
            k: (parts[k].astype(F32) + got[:, i * width : (i + 1) * width].astype(F32)).astype(BF16)
            for i, k in enumerate(keep)
        }

    def step(parts, bit):
        return kept(parts, bit, swap(gone(parts, bit), "tensor", bit))

    def split_rows(value):
        return split_parts(value[:row_limit]), split_parts(value[row_limit:])

    def flat(parts):
        return [parts[k] for k in parts]

    low, high = t_bits[0], t_bits[-1]
    expert_mine, expert_other = split_rows(expert_sum)
    send_low, send_high = gone(expert_mine, low), gone(expert_other, high)
    g_up_4, g_up_own = first_send(blocks_far(g_up)), first_send(blocks_own(g_up))
    g_down_far, input_sum, send_low, send_high, *rest = fence(
        g_down_far, input_sum, send_low, send_high, *g_gate_4, *g_up_4, *g_up_own
    )
    g_up_own = rest[2 + n_kept :]
    g_gate_4, send_low, send_high, input_sum, *g_up_4 = fence(
        done(*rest[:2]), send_low, send_high, input_sum, *rest[2 : 2 + n_kept]
    )

    def halves_of(own, other):
        both = beside(own, other)
        mine = lax.dynamic_slice_in_dim(both, core * rows_w, rows_w, 0)
        return mine, lax.dynamic_slice_in_dim(both, (1 - core) * rows_w, rows_w, 0)

    def panel(mine, got):
        whole = jnp.zeros((rows_w, 4 * hid), BF16)
        for block, u, c in (
            (mine[:, :hid], upper, core),
            (mine[:, hid:], 1 - upper, core),
            (got[:, :hid], upper, 1 - core),
            (got[:, hid:], 1 - upper, 1 - core),
        ):
            whole = lax.dynamic_update_slice(whole, block, (0, (u * 2 + c) * hid))
        return whole

    g_gate_far = z_far(g_gate_4)
    g_up_4 = shrink(*g_up_4)
    expert_mine = kept(expert_mine, low, swap(send_low, "tensor", low))
    expert_other = kept(expert_other, high, swap(send_high, "tensor", high))
    input_mine, input_other = split_rows(input_sum)
    merged = len(t_bits) == 2
    if merged:
        send_high = beside(gone(expert_mine, high), gone(input_other, high))
        send_low = beside(gone(expert_other, low), gone(input_mine, low))
    else:
        send_high, send_low = gone(input_other, high), gone(input_mine, low)
    g_gate_far, expert_mine, expert_other, input_mine, input_other, send_low, send_high, *rest = (
        fence(
            g_gate_far, expert_mine, expert_other, input_mine, input_other, send_low, send_high,
            *g_up_4, *g_gate_own
        )
    )
    g_up_4, send_low, send_high, *g_gate_own = fence(
        done(*rest[:2]), send_low, send_high, *rest[2:]
    )

    g_up_far = z_far(g_up_4)
    g_gate_own = shrink(*g_gate_own)
    got_high, got_low = swap(send_high, "tensor", high), swap(send_low, "tensor", low)
    if merged:
        expert_mine = kept(expert_mine, high, got_high[:, :width])
        expert_other = kept(expert_other, low, got_low[:, :width])
        got_high, got_low = got_high[:, width:], got_low[:, width:]
    else:
        for bit in t_bits[1:]:
            expert_mine = step(expert_mine, bit)
        for bit in t_bits[:-1][::-1]:
            expert_other = step(expert_other, bit)
    input_other = kept(input_other, high, got_high)
    input_mine = kept(input_mine, low, got_low)
    g_up_far, expert_mine, expert_other, input_mine, input_other, g_down_far, g_gate_far, *rest = fence(
        g_up_far, expert_mine[0], expert_other[0], input_mine, input_other, g_down_far, g_gate_far,
        *g_gate_own, *g_down_own, *g_up_own
    )
    g_gate_own, g_down_own, g_up_own = rest[:2], rest[2:4], rest[4:]

    g_up_own = shrink(*g_up_own)
    expert_got = z_far(expert_other)
    for bit in t_bits[1:]:
        input_mine = step(input_mine, bit)
    for bit in t_bits[:-1][::-1]:
        input_other = step(input_other, bit)
    input_mine, input_other, g_down_far, g_gate_far, *rest = fence(
        input_mine[0], input_other[0], g_down_far, g_gate_far, *g_down_own, *g_gate_own
    )
    down_mine, down_send = halves_of(done(*rest[:2]), g_down_far)
    gate_mine, gate_send = halves_of(done(*rest[2:]), g_gate_far)
    got = across(cat(down_send, gate_send))
    down_out, gate_out = panel(down_mine, got[:rows_w]), panel(gate_mine, got[rows_w:])
    up_mine, up_send = halves_of(done(*g_up_own), g_up_far)
    up_out = panel(up_mine, across(up_send))
    input_got = z_far(input_other)
    expert_cols = expert_mine.astype(F32) + expert_got.astype(F32)
    grad_cols = lax.dynamic_slice_in_dim(rows_grad, me_t * width, width, 1)
    weight_rows = jnp.sum(grad_cols.astype(F32) * expert_cols, axis=1)
    for bit in t_bits:
        weight_rows = weight_rows + swap(weight_rows, "tensor", bit)
    weight_grad = jnp.sum(jnp.where(match, weight_rows[:, None], 0.0), axis=0)
    mixed = mm_first(hot, (row_weight[:, None] * expert_cols).astype(BF16)).astype(BF16)
    input_cols = (input_mine.astype(F32) + input_got.astype(F32)).astype(BF16)
    input_grad = mm_first(hot, input_cols).astype(BF16)
    return (mixed, input_grad, weight_grad, gate_out, up_out, down_out)


def solution(mesh):
    return jax.shard_map(
        local,
        mesh=mesh,
        in_specs=(
            P("dp", None),
            P("dp", None),
            P("dp", None),
            P("dp", None),
            P("dp", "tensor"),
            P("dp", "tensor"),
            P("dp", "tensor"),
        ),
        out_specs=(
            P("dp", "tensor"),
            P("dp", "tensor"),
            P("dp"),
            P("dp", "tensor"),
            P("dp", "tensor"),
            P("dp", "tensor"),
        ),
        check_vma=False,
    )
```

```python
import functools

import jax
import jax.numpy as jnp
from jax import lax
from jax.experimental import pallas as pl
from jax.experimental.pallas import tpu as pltpu
from jax.sharding import PartitionSpec as P

BF16 = jnp.bfloat16
F32 = jnp.float32


def dot(left, right, dims):
    return lax.dot_general(left, right, (dims, ((), ())), preferred_element_type=F32)


def mm(left, right):
    return dot(left, right, ((1,), (0,)))


def mm_last(left, right):
    return dot(left, right, ((1,), (1,)))


def mm_first(left, right):
    return dot(left, right, ((0,), (0,)))


def swap(value, axis, distance):
    size = lax.axis_size(axis)
    return lax.ppermute(value, axis, [(i, i ^ distance) for i in range(size)])


def fence(*values):
    return lax.optimization_barrier(values)


def select_rows(assign_block, combine_block, row_limit):
    expert_hit = assign_block == 0
    routed = jnp.any(expert_hit, axis=1)
    weight = jnp.sum(
        jnp.where(expert_hit, combine_block, jnp.zeros((), combine_block.dtype)), axis=1
    )
    place = jnp.cumsum(routed.astype(jnp.int32)) - 1
    match = routed[None, :] & (place[None, :] == jnp.arange(row_limit, dtype=jnp.int32)[:, None])
    row_weight = jnp.sum(jnp.where(match, weight[None, :], 0.0), axis=1)
    return (match, row_weight)


def cat(*values):
    return jnp.concatenate(values, axis=0)


def beside(*values):
    return jnp.concatenate(values, axis=1)


def by_bits(blocks, index):
    bit = 1
    while bit < len(blocks):
        flag = (index & bit) != 0
        blocks = [jnp.where(flag, blocks[p ^ bit], blocks[p]) for p in range(len(blocks))]
        bit *= 2
    return blocks


def backward_kernel(
    tiles, step, out_ref, hidden_ref, gate_pre_ref, up_pre_ref, down_ref, gate_ref, up_ref, in_ref,
    expert_ref, expert_sib_ref, input_ref, input_sib_ref, g_gate_ref, g_up_ref, grads,
):
    i = pl.program_id(0)
    rows, depth = out_ref.shape
    hid = hidden_ref.shape[1]

    def outputs(expert, inputs, gate_grad, up_grad):
        for c in range(0, depth, step):
            part = slice(c, c + step)
            expert[:, part] = mm_last(hidden_ref[...], down_ref[part, :]).astype(BF16)
            inputs[:, part] = (
                mm_last(gate_grad, gate_ref[part, :]) + mm_last(up_grad, up_ref[part, :])
            ).astype(BF16)

    @pl.when(i < tiles)
    def _():
        hidden_grad = mm(out_ref[...], down_ref[...])
        gate_pre, up_pre = gate_pre_ref[...], up_pre_ref[...]
        sigmoid_gate = jax.nn.sigmoid(gate_pre)
        gate_grad = (
            hidden_grad * up_pre * sigmoid_gate * (1.0 + gate_pre * (1.0 - sigmoid_gate))
        ).astype(BF16)
        up_grad = (hidden_grad * gate_pre * sigmoid_gate).astype(BF16)
        place = pl.ds(pl.multiple_of(i * rows, rows), rows)
        grads[place, :hid] = gate_grad
        grads[place, hid:] = up_grad

        @pl.when(i < tiles // 2)
        def _():
            outputs(expert_ref, input_ref, gate_grad, up_grad)

        @pl.when(i >= tiles // 2)
        def _():
            outputs(expert_sib_ref, input_sib_ref, gate_grad, up_grad)

    @pl.when(i >= tiles)
    def _():
        both = mm_first(in_ref[...], grads[...])
        g_gate_ref[...] = both[:, :hid].astype(BF16)
        g_up_ref[...] = both[:, hid:].astype(BF16)


def backward(out_all, hidden, gate_pre, up_pre, down, gate, up, in_all):
    total, depth = out_all.shape
    hid = hidden.shape[1]
    rows, block = total // 6, depth // 8
    tiles, blocks = 6, 8
    half = tiles // 2

    def row(width):
        return pl.BlockSpec((rows, width), lambda i: (jnp.minimum(i, tiles - 1), 0))

    def first_rows():
        return pl.BlockSpec((rows, depth), lambda i: (jnp.minimum(i, half - 1), 0))

    def last_rows():
        return pl.BlockSpec((rows, depth), lambda i: (jnp.clip(i - half, 0, half - 1), 0))

    def weights():
        return pl.BlockSpec((depth, hid), lambda i: (0, 0), pipeline_mode=pl.Buffered(1))

    def width_rows():
        return pl.BlockSpec((block, hid), lambda i: (jnp.maximum(i - tiles, 0), 0))

    half_out = jax.ShapeDtypeStruct((total // 2, depth), BF16)
    panel_out = jax.ShapeDtypeStruct((depth, hid), BF16)
    return pl.pallas_call(
        functools.partial(backward_kernel, tiles, depth // 4),
        grid=(tiles + blocks,),
        in_specs=[
            row(depth), row(hid), row(hid), row(hid), weights(), weights(), weights(),
            pl.BlockSpec((total, block), lambda i: (0, jnp.maximum(i - tiles, 0))),
        ],
        out_specs=[first_rows(), last_rows(), first_rows(), last_rows(), width_rows(), width_rows()],
        out_shape=[half_out, half_out, half_out, half_out, panel_out, panel_out],
        scratch_shapes=[pltpu.VMEM((total, 2 * hid), BF16)],
        compiler_params=pltpu.CompilerParams(
            dimension_semantics=("arbitrary",), vmem_limit_bytes=52 * 1024 * 1024
        ),
        cost_estimate=pl.CostEstimate(
            flops=12 * total * depth * hid,
            bytes_accessed=2 * (4 * total * depth + 5 * depth * hid + 5 * total * hid),
            transcendentals=total * hid,
        ),
    )(out_all, hidden, gate_pre, up_pre, down, gate, up, in_all)


def local(tokens, assign, combine, cotangent, w_gate, w_up, w_down_t):
    token_total, depth = tokens.shape
    row_limit = token_total // 2
    n_dp = lax.axis_size("dp")
    n_tensor = lax.axis_size("tensor")
    me = lax.axis_index("dp")
    me_t = lax.axis_index("tensor")
    chip, core = me // 2, me % 2
    far = n_dp // 2
    upper = me // far
    rows_w = w_gate.shape[0]
    pair = 2 * rows_w
    n_chip = n_dp // 2
    hid = w_gate.shape[1] // 4
    width = depth // n_tensor
    mids = [1 << i for i in range(1, far.bit_length() - 1)]
    t_bits = [1 << i for i in range(n_tensor.bit_length() - 1)]

    def z_far(block):
        return swap(block, "dp", far)

    def across(block):
        return swap(block, "dp", 1)

    def grow(block):
        blocks = [block]
        for bit in mids:
            count, rows = len(blocks), block.shape[0]
            got = swap(cat(*blocks) if count > 1 else block, "dp", bit)
            blocks = blocks + [got[i * rows : (i + 1) * rows] for i in range(count)]
        return blocks

    def whole_panel(own, away):
        full = jnp.zeros((n_chip, pair, hid), BF16)
        for j in range(n_chip // 2):
            full = lax.dynamic_update_index_in_dim(full, own[j], chip ^ j, 0)
            full = lax.dynamic_update_index_in_dim(full, away[j], chip ^ j ^ (n_chip // 2), 0)
        return full.reshape(depth, hid)

    def block_of(panel, j):
        return lax.dynamic_index_in_dim(panel.reshape(n_chip, pair, hid), chip ^ j, 0, False)

    def blocks_own(panel):
        return {j: block_of(panel, j) for j in range(n_chip // 2)}

    def blocks_far(panel):
        return {j: block_of(panel, j ^ (n_chip // 2)) for j in range(n_chip // 2)}

    def add(blocks, got):
        return {
            j: (blocks[j].astype(F32) + got[i * pair : (i + 1) * pair].astype(F32)).astype(BF16)
            for i, j in enumerate(blocks)
        }

    def first_send(blocks):
        bit = mids[-1] // 2
        gone = [blocks[j] for j in blocks if j & bit]
        return (
            cat(*gone) if len(gone) > 1 else gone[0],
            *(blocks[j] for j in blocks if not j & bit),
        )

    def shrink(send, *kept):
        got = swap(send, "dp", mids[-1])
        for bit in mids[:-1][::-1]:
            blocks = add(dict(enumerate(kept)), got)
            count = len(blocks) // 2
            got = swap(cat(*(blocks[j + count] for j in range(count))), "dp", bit)
            kept = tuple(blocks[j] for j in range(count))
        return kept[0], got

    def done(kept, got):
        return (kept.astype(F32) + got.astype(F32)).astype(BF16)

    def part(w, u, c):
        return lax.dynamic_slice_in_dim(w, (u * 2 + c) * hid, hid, 1)

    def to_sibling(w):
        return beside(part(w, upper, 1 - core), part(w, 1 - upper, 1 - core))

    def by_core(mine, got):
        return jnp.where(core == 0, cat(mine, got), cat(got, mine))

    def pair_rows(w, got):
        mine = by_core(part(w, upper, core), got[:, :hid])
        other = by_core(part(w, 1 - upper, core), got[:, hid:])
        return mine, other

    gate_0 = lax.dynamic_slice_in_dim(w_gate, upper * 2 * hid, 2 * hid, 1)
    gate_4 = z_far(lax.dynamic_slice_in_dim(w_gate, (1 - upper) * 2 * hid, 2 * hid, 1))
    gate_own = grow(gate_0)
    match, row_weight = select_rows(assign, combine, row_limit)
    hot = match.astype(BF16)
    rows_in = mm(hot, tokens).astype(BF16)
    rows_grad = mm(hot, cotangent).astype(BF16)
    out_grad = (row_weight[:, None] * rows_grad.astype(F32)).astype(BF16)
    quarter = cat(
        *(lax.dynamic_slice_in_dim(v, me_t * width, width, 1) for v in (rows_in, out_grad))
    )
    send = cat(to_sibling(w_up), to_sibling(w_down_t))
    gate_4, quarter, rows_in, out_grad, send, *gate_own = fence(
        gate_4, quarter, rows_in, out_grad, send, *gate_own
    )

    quarter = z_far(quarter)
    gate_far = grow(gate_4)
    in_sib, out_sib = across(rows_in), across(out_grad)
    got = across(send)
    up_0, up_1 = pair_rows(w_up, got[:rows_w])
    down_0, down_1 = pair_rows(w_down_t, got[rows_w:])
    own = beside(up_0, down_0)
    quarter, in_sib, out_sib, own, up_1, down_1, *gate_far = fence(
        quarter, in_sib, out_sib, own, up_1, down_1, *gate_far
    )

    up_4 = z_far(up_1)
    own = grow(own)
    quarters = [quarter] + [swap(quarter, "tensor", k) for k in range(1, n_tensor)]
    gate_all = jnp.stack(gate_own + gate_far)
    gate_mine = lax.dynamic_slice_in_dim(gate_all, core * hid, hid, 2)
    gate_send = lax.dynamic_slice_in_dim(gate_all, (1 - core) * hid, hid, 2)
    up_4, gate_mine, gate_send, down_1, *rest = fence(
        up_4, gate_mine, gate_send, down_1, *quarters, *own
    )
    quarters, own = rest[: len(quarters)], rest[len(quarters) :]
    up_own, down_own = [b[:, :hid] for b in own], [b[:, hid:] for b in own]

    up_far = grow(up_4)
    down_4 = z_far(down_1)
    gate_got, *quarters = fence(across(gate_send), *quarters)
    gate = jnp.zeros((n_chip, 2, rows_w, hid), BF16)
    for j in range(n_chip):
        gate = lax.dynamic_update_slice(gate, gate_mine[j][None, None], (chip ^ j, core, 0, 0))
        gate = lax.dynamic_update_slice(gate, gate_got[j][None, None], (chip ^ j, 1 - core, 0, 0))
    gate = gate.reshape(depth, hid)

    def true_rows(first):
        return beside(*by_bits([q[first : first + row_limit] for q in quarters], me_t))

    in_away, out_away = true_rows(0), true_rows(row_limit)
    in_away_sib, out_away_sib = across(in_away), across(out_away)
    in_all = cat(rows_in, in_away, in_sib, in_away_sib)
    out_all = cat(out_grad, out_away, out_sib, out_away_sib)
    gate_pre = mm(in_all, gate)
    down_4, in_all, out_all, gate_pre, gate, *up_far = fence(
        down_4, in_all, out_all, gate_pre, gate, *up_far
    )

    down_far = grow(down_4)
    up = whole_panel(up_own, up_far)
    up_pre = mm(in_all, up)
    sigmoid_gate = jax.nn.sigmoid(gate_pre)
    hidden = (gate_pre * sigmoid_gate * up_pre).astype(BF16)
    g_down = mm_first(out_all, hidden).astype(BF16)
    g_down, hidden, up_pre, up, *down_far = fence(g_down, hidden, up_pre, up, *down_far)

    g_down_4 = first_send(blocks_far(g_down))
    n_kept = len(g_down_4)
    g_down_4 = shrink(*g_down_4)
    g_down_own = shrink(*first_send(blocks_own(g_down)))
    down = whole_panel(down_own, down_far)
    expert_part, expert_sib, input_part, input_sib, g_gate, g_up = backward(
        out_all, hidden, gate_pre, up_pre, down, gate, up, in_all
    )
    expert_part, expert_sib, input_part, input_sib, g_gate, g_up, *rest = fence(
        expert_part, expert_sib, input_part, input_sib, g_gate, g_up, *g_down_4, *g_down_own
    )
    g_down_own = rest[2:]
    g_down_4, expert_sib, input_sib, g_gate, g_up = fence(
        done(*rest[:2]), expert_sib, input_sib, g_gate, g_up
    )
    g_gate_4, g_gate_own = first_send(blocks_far(g_gate)), first_send(blocks_own(g_gate))

    g_down_far = z_far(g_down_4)
    g_gate_4 = shrink(*g_gate_4)
    expert_got, input_got = across(expert_sib), across(input_sib)
    expert_sum = (expert_part.astype(F32) + expert_got.astype(F32)).astype(BF16)
    input_sum = (input_part.astype(F32) + input_got.astype(F32)).astype(BF16)

    def split_parts(value):
        return {
            k: lax.dynamic_slice_in_dim(value, (me_t ^ k) * width, width, 1)
            for k in range(n_tensor)
        }

    def gone(parts, bit):
        return beside(*(parts[k] for k in parts if k & bit))

    def kept(parts, bit, got):
        keep = [k for k in parts if not k & bit]
        return {
            k: (parts[k].astype(F32) + got[:, i * width : (i + 1) * width].astype(F32)).astype(BF16)
            for i, k in enumerate(keep)
        }

    def step(parts, bit):
        return kept(parts, bit, swap(gone(parts, bit), "tensor", bit))

    def split_rows(value):
        return split_parts(value[:row_limit]), split_parts(value[row_limit:])

    def flat(parts):
        return [parts[k] for k in parts]

    low, high = t_bits[0], t_bits[-1]
    expert_mine, expert_other = split_rows(expert_sum)
    send_low, send_high = gone(expert_mine, low), gone(expert_other, high)
    g_up_4, g_up_own = first_send(blocks_far(g_up)), first_send(blocks_own(g_up))
    g_down_far, input_sum, send_low, send_high, *rest = fence(
        g_down_far, input_sum, send_low, send_high, *g_gate_4, *g_up_4, *g_up_own
    )
    g_up_own = rest[2 + n_kept :]
    g_gate_4, send_low, send_high, input_sum, *g_up_4 = fence(
        done(*rest[:2]), send_low, send_high, input_sum, *rest[2 : 2 + n_kept]
    )

    def halves_of(own, other):
        both = beside(own, other)
        mine = lax.dynamic_slice_in_dim(both, core * rows_w, rows_w, 0)
        return mine, lax.dynamic_slice_in_dim(both, (1 - core) * rows_w, rows_w, 0)

    def panel(mine, got):
        whole = jnp.zeros((rows_w, 4 * hid), BF16)
        for block, u, c in (
            (mine[:, :hid], upper, core),
            (mine[:, hid:], 1 - upper, core),
            (got[:, :hid], upper, 1 - core),
            (got[:, hid:], 1 - upper, 1 - core),
        ):
            whole = lax.dynamic_update_slice(whole, block, (0, (u * 2 + c) * hid))
        return whole

    g_gate_far = z_far(g_gate_4)
    g_up_4 = shrink(*g_up_4)
    expert_mine = kept(expert_mine, low, swap(send_low, "tensor", low))
    expert_other = kept(expert_other, high, swap(send_high, "tensor", high))
    input_mine, input_other = split_rows(input_sum)
    merged = len(t_bits) == 2
    if merged:
        send_high = beside(gone(expert_mine, high), gone(input_other, high))
        send_low = beside(gone(expert_other, low), gone(input_mine, low))
    else:
        send_high, send_low = gone(input_other, high), gone(input_mine, low)
    g_gate_far, expert_mine, expert_other, input_mine, input_other, send_low, send_high, *rest = (
        fence(
            g_gate_far, expert_mine, expert_other, input_mine, input_other, send_low, send_high,
            *g_up_4, *g_gate_own
        )
    )
    g_up_4, send_low, send_high, *g_gate_own = fence(
        done(*rest[:2]), send_low, send_high, *rest[2:]
    )

    g_up_far = z_far(g_up_4)
    g_gate_own = shrink(*g_gate_own)
    got_high, got_low = swap(send_high, "tensor", high), swap(send_low, "tensor", low)
    if merged:
        expert_mine = kept(expert_mine, high, got_high[:, :width])
        expert_other = kept(expert_other, low, got_low[:, :width])
        got_high, got_low = got_high[:, width:], got_low[:, width:]
    else:
        for bit in t_bits[1:]:
            expert_mine = step(expert_mine, bit)
        for bit in t_bits[:-1][::-1]:
            expert_other = step(expert_other, bit)
    input_other = kept(input_other, high, got_high)
    input_mine = kept(input_mine, low, got_low)
    g_up_far, expert_mine, expert_other, input_mine, input_other, g_down_far, g_gate_far, *rest = fence(
        g_up_far, expert_mine[0], expert_other[0], input_mine, input_other, g_down_far, g_gate_far,
        *g_gate_own, *g_down_own, *g_up_own
    )
    g_gate_own, g_down_own, g_up_own = rest[:2], rest[2:4], rest[4:]

    g_up_own = shrink(*g_up_own)
    expert_got = z_far(expert_other)
    for bit in t_bits[1:]:
        input_mine = step(input_mine, bit)
    for bit in t_bits[:-1][::-1]:
        input_other = step(input_other, bit)
    input_mine, input_other, g_down_far, g_gate_far, *rest = fence(
        input_mine[0], input_other[0], g_down_far, g_gate_far, *g_down_own, *g_gate_own
    )
    down_mine, down_send = halves_of(done(*rest[:2]), g_down_far)
    gate_mine, gate_send = halves_of(done(*rest[2:]), g_gate_far)
    got = across(cat(down_send, gate_send))
    down_out, gate_out = panel(down_mine, got[:rows_w]), panel(gate_mine, got[rows_w:])
    up_mine, up_send = halves_of(done(*g_up_own), g_up_far)
    up_out = panel(up_mine, across(up_send))
    input_got = z_far(input_other)
    expert_cols = expert_mine.astype(F32) + expert_got.astype(F32)
    grad_cols = lax.dynamic_slice_in_dim(rows_grad, me_t * width, width, 1)
    weight_rows = jnp.sum(grad_cols.astype(F32) * expert_cols, axis=1)
    for bit in t_bits:
        weight_rows = weight_rows + swap(weight_rows, "tensor", bit)
    weight_grad = jnp.sum(jnp.where(match, weight_rows[:, None], 0.0), axis=0)
    mixed = mm_first(hot, (row_weight[:, None] * expert_cols).astype(BF16)).astype(BF16)
    input_cols = (input_mine.astype(F32) + input_got.astype(F32)).astype(BF16)
    input_grad = mm_first(hot, input_cols).astype(BF16)
    return (mixed, input_grad, weight_grad, gate_out, up_out, down_out)


def solution(mesh):
    return jax.shard_map(
        local,
        mesh=mesh,
        in_specs=(
            P("dp", None),
            P("dp", None),
            P("dp", None),
            P("dp", None),
            P("dp", "tensor"),
            P("dp", "tensor"),
            P("dp", "tensor"),
        ),
        out_specs=(
            P("dp", "tensor"),
            P("dp", "tensor"),
            P("dp"),
            P("dp", "tensor"),
            P("dp", "tensor"),
            P("dp", "tensor"),
        ),
        check_vma=False,
    )
```

```python
import jax
import jax.numpy as jnp
from jax import lax
from jax.sharding import PartitionSpec as P

BF16 = jnp.bfloat16
F32 = jnp.float32


def dot(left, right, dims):
    return lax.dot_general(left, right, (dims, ((), ())), preferred_element_type=F32)


def mm(left, right):
    return dot(left, right, ((1,), (0,)))


def mm_last(left, right):
    return dot(left, right, ((1,), (1,)))


def mm_first(left, right):
    return dot(left, right, ((0,), (0,)))


def swap(value, axis, distance):
    size = lax.axis_size(axis)
    return lax.ppermute(value, axis, [(i, i ^ distance) for i in range(size)])


def fence(*values):
    return lax.optimization_barrier(values)


def select_rows(assign_block, combine_block, row_limit):
    expert_hit = assign_block == 0
    routed = jnp.any(expert_hit, axis=1)
    weight = jnp.sum(
        jnp.where(expert_hit, combine_block, jnp.zeros((), combine_block.dtype)), axis=1
    )
    place = jnp.cumsum(routed.astype(jnp.int32)) - 1
    match = routed[None, :] & (place[None, :] == jnp.arange(row_limit, dtype=jnp.int32)[:, None])
    row_weight = jnp.sum(jnp.where(match, weight[None, :], 0.0), axis=1)
    return (match, row_weight)


def cat(*values):
    return jnp.concatenate(values, axis=0)


def beside(*values):
    return jnp.concatenate(values, axis=1)


def by_bits(blocks, index):
    bit = 1
    while bit < len(blocks):
        flag = (index & bit) != 0
        blocks = [jnp.where(flag, blocks[p ^ bit], blocks[p]) for p in range(len(blocks))]
        bit *= 2
    return blocks


def local(tokens, assign, combine, cotangent, w_gate, w_up, w_down_t):
    token_total, depth = tokens.shape
    row_limit = token_total // 2
    n_dp = lax.axis_size("dp")
    n_tensor = lax.axis_size("tensor")
    me = lax.axis_index("dp")
    me_t = lax.axis_index("tensor")
    chip, core = me // 2, me % 2
    far = n_dp // 2
    upper = me // far
    rows_w = w_gate.shape[0]
    pair = 2 * rows_w
    n_chip = n_dp // 2
    hid = w_gate.shape[1] // 4
    width = depth // n_tensor
    mids = [1 << i for i in range(1, far.bit_length() - 1)]
    t_bits = [1 << i for i in range(n_tensor.bit_length() - 1)]

    def z_far(block):
        return swap(block, "dp", far)

    def across(block):
        return swap(block, "dp", 1)

    def grow(block):
        blocks = [block]
        for bit in mids:
            count, rows = len(blocks), block.shape[0]
            got = swap(cat(*blocks) if count > 1 else block, "dp", bit)
            blocks = blocks + [got[i * rows : (i + 1) * rows] for i in range(count)]
        return blocks

    def whole_panel(own, away):
        full = jnp.zeros((n_chip, pair, hid), BF16)
        for j in range(n_chip // 2):
            full = lax.dynamic_update_index_in_dim(full, own[j], chip ^ j, 0)
            full = lax.dynamic_update_index_in_dim(full, away[j], chip ^ j ^ (n_chip // 2), 0)
        return full.reshape(depth, hid)

    def block_of(panel, j):
        return lax.dynamic_index_in_dim(panel.reshape(n_chip, pair, hid), chip ^ j, 0, False)

    def blocks_own(panel):
        return {j: block_of(panel, j) for j in range(n_chip // 2)}

    def blocks_far(panel):
        return {j: block_of(panel, j ^ (n_chip // 2)) for j in range(n_chip // 2)}

    def add(blocks, got):
        return {
            j: (blocks[j].astype(F32) + got[i * pair : (i + 1) * pair].astype(F32)).astype(BF16)
            for i, j in enumerate(blocks)
        }

    def first_send(blocks):
        bit = mids[-1] // 2
        gone = [blocks[j] for j in blocks if j & bit]
        return (
            cat(*gone) if len(gone) > 1 else gone[0],
            *(blocks[j] for j in blocks if not j & bit),
        )

    def shrink(send, *kept):
        got = swap(send, "dp", mids[-1])
        for bit in mids[:-1][::-1]:
            blocks = add(dict(enumerate(kept)), got)
            count = len(blocks) // 2
            got = swap(cat(*(blocks[j + count] for j in range(count))), "dp", bit)
            kept = tuple(blocks[j] for j in range(count))
        return kept[0], got

    def done(kept, got):
        return (kept.astype(F32) + got.astype(F32)).astype(BF16)

    def part(w, u, c):
        return lax.dynamic_slice_in_dim(w, (u * 2 + c) * hid, hid, 1)

    def to_sibling(w):
        return beside(part(w, upper, 1 - core), part(w, 1 - upper, 1 - core))

    def by_core(mine, got):
        return jnp.where(core == 0, cat(mine, got), cat(got, mine))

    def pair_rows(w, got):
        mine = by_core(part(w, upper, core), got[:, :hid])
        other = by_core(part(w, 1 - upper, core), got[:, hid:])
        return mine, other

    gate_0 = lax.dynamic_slice_in_dim(w_gate, upper * 2 * hid, 2 * hid, 1)
    gate_4 = z_far(lax.dynamic_slice_in_dim(w_gate, (1 - upper) * 2 * hid, 2 * hid, 1))
    gate_own = grow(gate_0)
    match, row_weight = select_rows(assign, combine, row_limit)
    hot = match.astype(BF16)
    rows_in = mm(hot, tokens).astype(BF16)
    rows_grad = mm(hot, cotangent).astype(BF16)
    out_grad = (row_weight[:, None] * rows_grad.astype(F32)).astype(BF16)
    quarter = cat(
        *(lax.dynamic_slice_in_dim(v, me_t * width, width, 1) for v in (rows_in, out_grad))
    )
    send = cat(to_sibling(w_up), to_sibling(w_down_t))
    gate_4, quarter, rows_in, out_grad, send, *gate_own = fence(
        gate_4, quarter, rows_in, out_grad, send, *gate_own
    )

    quarter = z_far(quarter)
    gate_far = grow(gate_4)
    in_sib, out_sib = across(rows_in), across(out_grad)
    got = across(send)
    up_0, up_1 = pair_rows(w_up, got[:rows_w])
    down_0, down_1 = pair_rows(w_down_t, got[rows_w:])
    own = beside(up_0, down_0)
    quarter, in_sib, out_sib, own, up_1, down_1, *gate_far = fence(
        quarter, in_sib, out_sib, own, up_1, down_1, *gate_far
    )

    up_4 = z_far(up_1)
    own = grow(own)
    quarters = [quarter] + [swap(quarter, "tensor", k) for k in range(1, n_tensor)]
    gate_all = jnp.stack(gate_own + gate_far)
    gate_mine = lax.dynamic_slice_in_dim(gate_all, core * hid, hid, 2)
    gate_send = lax.dynamic_slice_in_dim(gate_all, (1 - core) * hid, hid, 2)
    up_4, gate_mine, gate_send, down_1, *rest = fence(
        up_4, gate_mine, gate_send, down_1, *quarters, *own
    )
    quarters, own = rest[: len(quarters)], rest[len(quarters) :]
    up_own, down_own = [b[:, :hid] for b in own], [b[:, hid:] for b in own]

    up_far = grow(up_4)
    down_4 = z_far(down_1)
    gate_got, *quarters = fence(across(gate_send), *quarters)
    gate = jnp.zeros((n_chip, 2, rows_w, hid), BF16)
    for j in range(n_chip):
        gate = lax.dynamic_update_slice(gate, gate_mine[j][None, None], (chip ^ j, core, 0, 0))
        gate = lax.dynamic_update_slice(gate, gate_got[j][None, None], (chip ^ j, 1 - core, 0, 0))
    gate = gate.reshape(depth, hid)

    def true_rows(first):
        return beside(*by_bits([q[first : first + row_limit] for q in quarters], me_t))

    in_away, out_away = true_rows(0), true_rows(row_limit)
    in_away_sib, out_away_sib = across(in_away), across(out_away)
    in_all = cat(rows_in, in_away, in_sib, in_away_sib)
    out_all = cat(out_grad, out_away, out_sib, out_away_sib)
    gate_pre = mm(in_all, gate)
    down_4, in_all, out_all, gate_pre, gate, *up_far = fence(
        down_4, in_all, out_all, gate_pre, gate, *up_far
    )

    down_far = grow(down_4)
    up = whole_panel(up_own, up_far)
    up_pre = mm(in_all, up)
    sigmoid_gate = jax.nn.sigmoid(gate_pre)
    hidden = (gate_pre * sigmoid_gate * up_pre).astype(BF16)
    g_down = mm_first(out_all, hidden).astype(BF16)
    g_down, hidden, up_pre, up, *down_far = fence(g_down, hidden, up_pre, up, *down_far)

    table = 2 * row_limit
    g_down_4 = first_send(blocks_far(g_down))
    n_kept = len(g_down_4)
    g_down_4 = shrink(*g_down_4)
    g_down_own = shrink(*first_send(blocks_own(g_down)))
    down = whole_panel(down_own, down_far)
    hidden_grad = mm(out_all, down)
    gate_grad = (
        hidden_grad * up_pre * sigmoid_gate * (1.0 + gate_pre * (1.0 - sigmoid_gate))
    ).astype(BF16)
    up_grad = (hidden_grad * gate_pre * sigmoid_gate).astype(BF16)
    g_gate = mm_first(in_all, gate_grad).astype(BF16)
    expert_got = across(mm_last(hidden[table:], down).astype(BF16))

    def input_part(rows):
        return mm_last(gate_grad[rows], gate) + mm_last(up_grad[rows], up)

    input_sib = input_part(slice(table, None)).astype(BF16)
    down, gate_grad, up_grad, g_gate, expert_got, input_sib, *rest = fence(
        down, gate_grad, up_grad, g_gate, expert_got, input_sib, *g_down_4, *g_down_own
    )
    g_down_own = rest[2:]
    g_down_4, input_sib, g_gate = fence(done(*rest[:2]), input_sib, g_gate)
    g_gate_4, g_gate_own = first_send(blocks_far(g_gate)), first_send(blocks_own(g_gate))

    g_down_far = z_far(g_down_4)
    g_gate_4 = shrink(*g_gate_4)
    input_got = across(input_sib)
    g_up = mm_first(in_all, up_grad).astype(BF16)
    expert_sum = (mm_last(hidden[:table], down) + expert_got.astype(F32)).astype(BF16)
    input_sum = (input_part(slice(None, table)) + input_got.astype(F32)).astype(BF16)

    def split_parts(value):
        return {
            k: lax.dynamic_slice_in_dim(value, (me_t ^ k) * width, width, 1)
            for k in range(n_tensor)
        }

    def gone(parts, bit):
        return beside(*(parts[k] for k in parts if k & bit))

    def kept(parts, bit, got):
        keep = [k for k in parts if not k & bit]
        return {
            k: (parts[k].astype(F32) + got[:, i * width : (i + 1) * width].astype(F32)).astype(BF16)
            for i, k in enumerate(keep)
        }

    def step(parts, bit):
        return kept(parts, bit, swap(gone(parts, bit), "tensor", bit))

    def split_rows(value):
        return split_parts(value[:row_limit]), split_parts(value[row_limit:])

    def flat(parts):
        return [parts[k] for k in parts]

    low, high = t_bits[0], t_bits[-1]
    expert_mine, expert_other = split_rows(expert_sum)
    send_low, send_high = gone(expert_mine, low), gone(expert_other, high)
    g_up_4, g_up_own = first_send(blocks_far(g_up)), first_send(blocks_own(g_up))
    g_down_far, input_sum, send_low, send_high, *rest = fence(
        g_down_far, input_sum, send_low, send_high, *g_gate_4, *g_up_4, *g_up_own
    )
    g_up_own = rest[2 + n_kept :]
    g_gate_4, send_low, send_high, input_sum, *g_up_4 = fence(
        done(*rest[:2]), send_low, send_high, input_sum, *rest[2 : 2 + n_kept]
    )

    def halves_of(own, other):
        both = beside(own, other)
        mine = lax.dynamic_slice_in_dim(both, core * rows_w, rows_w, 0)
        return mine, lax.dynamic_slice_in_dim(both, (1 - core) * rows_w, rows_w, 0)

    def panel(mine, got):
        whole = jnp.zeros((rows_w, 4 * hid), BF16)
        for block, u, c in (
            (mine[:, :hid], upper, core),
            (mine[:, hid:], 1 - upper, core),
            (got[:, :hid], upper, 1 - core),
            (got[:, hid:], 1 - upper, 1 - core),
        ):
            whole = lax.dynamic_update_slice(whole, block, (0, (u * 2 + c) * hid))
        return whole

    g_gate_far = z_far(g_gate_4)
    g_up_4 = shrink(*g_up_4)
    expert_mine = kept(expert_mine, low, swap(send_low, "tensor", low))
    expert_other = kept(expert_other, high, swap(send_high, "tensor", high))
    input_mine, input_other = split_rows(input_sum)
    merged = len(t_bits) == 2
    if merged:
        send_high = beside(gone(expert_mine, high), gone(input_other, high))
        send_low = beside(gone(expert_other, low), gone(input_mine, low))
    else:
        send_high, send_low = gone(input_other, high), gone(input_mine, low)
    g_gate_far, expert_mine, expert_other, input_mine, input_other, send_low, send_high, *rest = (
        fence(
            g_gate_far, expert_mine, expert_other, input_mine, input_other, send_low, send_high,
            *g_up_4, *g_gate_own
        )
    )
    g_up_4, send_low, send_high, *g_gate_own = fence(
        done(*rest[:2]), send_low, send_high, *rest[2:]
    )

    g_up_far = z_far(g_up_4)
    g_gate_own = shrink(*g_gate_own)
    got_high, got_low = swap(send_high, "tensor", high), swap(send_low, "tensor", low)
    if merged:
        expert_mine = kept(expert_mine, high, got_high[:, :width])
        expert_other = kept(expert_other, low, got_low[:, :width])
        got_high, got_low = got_high[:, width:], got_low[:, width:]
    else:
        for bit in t_bits[1:]:
            expert_mine = step(expert_mine, bit)
        for bit in t_bits[:-1][::-1]:
            expert_other = step(expert_other, bit)
    input_other = kept(input_other, high, got_high)
    input_mine = kept(input_mine, low, got_low)
    g_up_far, expert_mine, expert_other, input_mine, input_other, g_down_far, g_gate_far, *rest = fence(
        g_up_far, expert_mine[0], expert_other[0], input_mine, input_other, g_down_far, g_gate_far,
        *g_gate_own, *g_down_own, *g_up_own
    )
    g_gate_own, g_down_own, g_up_own = rest[:2], rest[2:4], rest[4:]

    g_up_own = shrink(*g_up_own)
    expert_got = z_far(expert_other)
    for bit in t_bits[1:]:
        input_mine = step(input_mine, bit)
    for bit in t_bits[:-1][::-1]:
        input_other = step(input_other, bit)
    input_mine, input_other, g_down_far, g_gate_far, *rest = fence(
        input_mine[0], input_other[0], g_down_far, g_gate_far, *g_down_own, *g_gate_own
    )
    down_mine, down_send = halves_of(done(*rest[:2]), g_down_far)
    gate_mine, gate_send = halves_of(done(*rest[2:]), g_gate_far)
    got = across(cat(down_send, gate_send))
    down_out, gate_out = panel(down_mine, got[:rows_w]), panel(gate_mine, got[rows_w:])
    up_mine, up_send = halves_of(done(*g_up_own), g_up_far)
    up_out = panel(up_mine, across(up_send))
    input_got = z_far(input_other)
    expert_cols = expert_mine.astype(F32) + expert_got.astype(F32)
    grad_cols = lax.dynamic_slice_in_dim(rows_grad, me_t * width, width, 1)
    weight_rows = jnp.sum(grad_cols.astype(F32) * expert_cols, axis=1)
    for bit in t_bits:
        weight_rows = weight_rows + swap(weight_rows, "tensor", bit)
    weight_grad = jnp.sum(jnp.where(match, weight_rows[:, None], 0.0), axis=0)
    mixed = mm_first(hot, (row_weight[:, None] * expert_cols).astype(BF16)).astype(BF16)
    input_cols = (input_mine.astype(F32) + input_got.astype(F32)).astype(BF16)
    input_grad = mm_first(hot, input_cols).astype(BF16)
    return (mixed, input_grad, weight_grad, gate_out, up_out, down_out)


def solution(mesh):
    return jax.shard_map(
        local,
        mesh=mesh,
        in_specs=(
            P("dp", None),
            P("dp", None),
            P("dp", None),
            P("dp", None),
            P("dp", "tensor"),
            P("dp", "tensor"),
            P("dp", "tensor"),
        ),
        out_specs=(
            P("dp", "tensor"),
            P("dp", "tensor"),
            P("dp"),
            P("dp", "tensor"),
            P("dp", "tensor"),
            P("dp", "tensor"),
        ),
        check_vma=False,
    )
```

```python
import jax
import jax.numpy as jnp
from jax import lax
from jax.sharding import PartitionSpec as P

BF16 = jnp.bfloat16
F32 = jnp.float32


def dot(left, right, dims):
    return lax.dot_general(left, right, (dims, ((), ())), preferred_element_type=F32)


def mm(left, right):
    return dot(left, right, ((1,), (0,)))


def mm_last(left, right):
    return dot(left, right, ((1,), (1,)))


def mm_first(left, right):
    return dot(left, right, ((0,), (0,)))


def swap(value, axis, distance):
    size = lax.axis_size(axis)
    return lax.ppermute(value, axis, [(i, i ^ distance) for i in range(size)])


def fence(*values):
    return lax.optimization_barrier(values)


def select_rows(assign_block, combine_block, row_limit):
    expert_hit = assign_block == 0
    routed = jnp.any(expert_hit, axis=1)
    weight = jnp.sum(
        jnp.where(expert_hit, combine_block, jnp.zeros((), combine_block.dtype)), axis=1
    )
    place = jnp.cumsum(routed.astype(jnp.int32)) - 1
    match = routed[None, :] & (place[None, :] == jnp.arange(row_limit, dtype=jnp.int32)[:, None])
    row_weight = jnp.sum(jnp.where(match, weight[None, :], 0.0), axis=1)
    return (match, row_weight)


def cat(*values):
    return jnp.concatenate(values, axis=0)


def beside(*values):
    return jnp.concatenate(values, axis=1)


def by_bits(blocks, index):
    bit = 1
    while bit < len(blocks):
        flag = (index & bit) != 0
        blocks = [jnp.where(flag, blocks[p ^ bit], blocks[p]) for p in range(len(blocks))]
        bit *= 2
    return blocks


def local(tokens, assign, combine, cotangent, w_gate, w_up, w_down_t):
    token_total, depth = tokens.shape
    row_limit = token_total // 2
    n_dp = lax.axis_size("dp")
    n_tensor = lax.axis_size("tensor")
    me = lax.axis_index("dp")
    me_t = lax.axis_index("tensor")
    chip, core = me // 2, me % 2
    far = n_dp // 2
    upper = me // far
    rows_w = w_gate.shape[0]
    pair = 2 * rows_w
    n_chip = n_dp // 2
    hid = w_gate.shape[1] // 4
    width = depth // n_tensor
    mids = [1 << i for i in range(1, far.bit_length() - 1)]
    t_bits = [1 << i for i in range(n_tensor.bit_length() - 1)]

    def z_far(block):
        return swap(block, "dp", far)

    def across(block):
        return swap(block, "dp", 1)

    def grow(block):
        blocks = [block]
        for bit in mids:
            count, rows = len(blocks), block.shape[0]
            got = swap(cat(*blocks) if count > 1 else block, "dp", bit)
            blocks = blocks + [got[i * rows : (i + 1) * rows] for i in range(count)]
        return blocks

    def put(full, blocks):
        for j, block in blocks.items():
            full = lax.dynamic_update_index_in_dim(full, block, chip ^ j, 0)
        return full

    half_n = n_chip // 2

    def block_of(panel, j):
        return lax.dynamic_index_in_dim(panel.reshape(n_chip, pair, hid), chip ^ j, 0, False)

    def blocks_own(panel):
        return {j: block_of(panel, j) for j in range(n_chip // 2)}

    def blocks_far(panel):
        return {j: block_of(panel, j ^ (n_chip // 2)) for j in range(n_chip // 2)}

    def add(blocks, got):
        return {
            j: (blocks[j].astype(F32) + got[i * pair : (i + 1) * pair].astype(F32)).astype(BF16)
            for i, j in enumerate(blocks)
        }

    def first_send(blocks):
        bit = mids[-1] // 2
        gone = [blocks[j] for j in blocks if j & bit]
        return (
            cat(*gone) if len(gone) > 1 else gone[0],
            *(blocks[j] for j in blocks if not j & bit),
        )

    def shrink(send, *kept):
        got = swap(send, "dp", mids[-1])
        for bit in mids[:-1][::-1]:
            blocks = add(dict(enumerate(kept)), got)
            count = len(blocks) // 2
            got = swap(cat(*(blocks[j + count] for j in range(count))), "dp", bit)
            kept = tuple(blocks[j] for j in range(count))
        return kept[0], got

    def done(kept, got):
        return (kept.astype(F32) + got.astype(F32)).astype(BF16)

    def part(w, u, c):
        return lax.dynamic_slice_in_dim(w, (u * 2 + c) * hid, hid, 1)

    def to_sibling(w):
        return beside(part(w, upper, 1 - core), part(w, 1 - upper, 1 - core))

    def by_core(mine, got):
        return jnp.where(core == 0, cat(mine, got), cat(got, mine))

    def pair_rows(w, got):
        mine = by_core(part(w, upper, core), got[:, :hid])
        other = by_core(part(w, 1 - upper, core), got[:, hid:])
        return mine, other

    gate_0 = lax.dynamic_slice_in_dim(w_gate, upper * 2 * hid, 2 * hid, 1)
    gate_4 = z_far(lax.dynamic_slice_in_dim(w_gate, (1 - upper) * 2 * hid, 2 * hid, 1))
    gate_own = grow(gate_0)
    match, row_weight = select_rows(assign, combine, row_limit)
    hot = match.astype(BF16)
    rows_in = mm(hot, tokens).astype(BF16)
    rows_grad = mm(hot, cotangent).astype(BF16)
    out_grad = (row_weight[:, None] * rows_grad.astype(F32)).astype(BF16)
    quarter = cat(
        *(lax.dynamic_slice_in_dim(v, me_t * width, width, 1) for v in (rows_in, out_grad))
    )
    send = cat(to_sibling(w_up), to_sibling(w_down_t))
    gate_4, quarter, rows_in, out_grad, send, *gate_own = fence(
        gate_4, quarter, rows_in, out_grad, send, *gate_own
    )

    quarter = z_far(quarter)
    gate_far = grow(gate_4)
    in_sib, out_sib = across(rows_in), across(out_grad)
    got = across(send)
    up_0, up_1 = pair_rows(w_up, got[:rows_w])
    down_0, down_1 = pair_rows(w_down_t, got[rows_w:])
    own = beside(up_0, down_0)
    quarter, in_sib, out_sib, own, up_1, down_1, *gate_far = fence(
        quarter, in_sib, out_sib, own, up_1, down_1, *gate_far
    )

    up_4 = z_far(up_1)
    own = grow(own)
    quarters = [quarter] + [swap(quarter, "tensor", k) for k in range(1, n_tensor)]
    gate_all = jnp.stack(gate_own + gate_far)
    gate_mine = lax.dynamic_slice_in_dim(gate_all, core * hid, hid, 2)
    gate_send = lax.dynamic_slice_in_dim(gate_all, (1 - core) * hid, hid, 2)
    empty = jnp.zeros((n_chip, pair, hid), BF16)
    up = put(empty, {0: own[0][:, :hid]})
    down = put(empty, {0: own[0][:, hid:]})
    up_4, gate_mine, gate_send, down_1, up, down, *rest = fence(
        up_4, gate_mine, gate_send, down_1, up, down, *quarters, *own
    )
    quarters, own = rest[: len(quarters)], rest[len(quarters) :]
    up_own, down_own = [b[:, :hid] for b in own], [b[:, hid:] for b in own]

    up_far = grow(up_4)
    down_4 = z_far(down_1)
    gate_got, *quarters = fence(across(gate_send), *quarters)
    gate = jnp.zeros((n_chip, 2, rows_w, hid), BF16)
    for j in range(n_chip):
        gate = lax.dynamic_update_slice(gate, gate_mine[j][None, None], (chip ^ j, core, 0, 0))
        gate = lax.dynamic_update_slice(gate, gate_got[j][None, None], (chip ^ j, 1 - core, 0, 0))
    up = put(up, {j: up_own[j] for j in range(1, half_n)})
    up = put(up, {half_n: up_4})
    down = put(down, {j: down_own[j] for j in range(1, half_n)})
    gate = gate.reshape(depth, hid)

    def true_rows(first):
        return beside(*by_bits([q[first : first + row_limit] for q in quarters], me_t))

    in_away, out_away = true_rows(0), true_rows(row_limit)
    in_away_sib, out_away_sib = across(in_away), across(out_away)
    in_all = cat(rows_in, in_away, in_sib, in_away_sib)
    out_all = cat(out_grad, out_away, out_sib, out_away_sib)
    gate_pre = mm(in_all, gate)
    down_4, in_all, out_all, gate_pre, gate, up, down, *up_far = fence(
        down_4, in_all, out_all, gate_pre, gate, up, down, *up_far
    )

    down_far = grow(down_4)
    up = put(up, {j + half_n: up_far[j] for j in range(1, half_n)}).reshape(depth, hid)
    down = put(down, {half_n: down_4})
    up_pre = mm(in_all, up)
    sigmoid_gate = jax.nn.sigmoid(gate_pre)
    hidden = (gate_pre * sigmoid_gate * up_pre).astype(BF16)
    g_down = mm_first(out_all, hidden).astype(BF16)
    g_down, hidden, up_pre, up, down, *down_far = fence(
        g_down, hidden, up_pre, up, down, *down_far
    )

    table = 2 * row_limit
    g_down_4 = first_send(blocks_far(g_down))
    n_kept = len(g_down_4)
    g_down_4 = shrink(*g_down_4)
    g_down_own = shrink(*first_send(blocks_own(g_down)))
    down = put(down, {j + half_n: down_far[j] for j in range(1, half_n)}).reshape(depth, hid)
    hidden_grad = mm(out_all, down)
    gate_grad = (
        hidden_grad * up_pre * sigmoid_gate * (1.0 + gate_pre * (1.0 - sigmoid_gate))
    ).astype(BF16)
    up_grad = (hidden_grad * gate_pre * sigmoid_gate).astype(BF16)
    g_gate = mm_first(in_all, gate_grad).astype(BF16)
    expert_got = across(mm_last(hidden[table:], down).astype(BF16))

    def input_part(rows):
        return mm_last(gate_grad[rows], gate) + mm_last(up_grad[rows], up)

    input_sib = input_part(slice(table, None)).astype(BF16)
    down, gate_grad, up_grad, g_gate, expert_got, input_sib, *rest = fence(
        down, gate_grad, up_grad, g_gate, expert_got, input_sib, *g_down_4, *g_down_own
    )
    g_down_own = rest[2:]
    g_down_4, input_sib, g_gate = fence(done(*rest[:2]), input_sib, g_gate)
    g_gate_4, g_gate_own = first_send(blocks_far(g_gate)), first_send(blocks_own(g_gate))

    g_down_far = z_far(g_down_4)
    g_gate_4 = shrink(*g_gate_4)
    input_got = across(input_sib)
    g_up = mm_first(in_all, up_grad).astype(BF16)
    expert_sum = (mm_last(hidden[:table], down) + expert_got.astype(F32)).astype(BF16)
    input_sum = (input_part(slice(None, table)) + input_got.astype(F32)).astype(BF16)

    def split_parts(value):
        return {
            k: lax.dynamic_slice_in_dim(value, (me_t ^ k) * width, width, 1)
            for k in range(n_tensor)
        }

    def gone(parts, bit):
        return beside(*(parts[k] for k in parts if k & bit))

    def kept(parts, bit, got):
        keep = [k for k in parts if not k & bit]
        return {
            k: (parts[k].astype(F32) + got[:, i * width : (i + 1) * width].astype(F32)).astype(BF16)
            for i, k in enumerate(keep)
        }

    def step(parts, bit):
        return kept(parts, bit, swap(gone(parts, bit), "tensor", bit))

    def split_rows(value):
        return split_parts(value[:row_limit]), split_parts(value[row_limit:])

    def flat(parts):
        return [parts[k] for k in parts]

    low, high = t_bits[0], t_bits[-1]
    expert_mine, expert_other = split_rows(expert_sum)
    send_low, send_high = gone(expert_mine, low), gone(expert_other, high)
    g_up_4, g_up_own = first_send(blocks_far(g_up)), first_send(blocks_own(g_up))
    g_down_far, input_sum, send_low, send_high, *rest = fence(
        g_down_far, input_sum, send_low, send_high, *g_gate_4, *g_up_4, *g_up_own
    )
    g_up_own = rest[2 + n_kept :]
    g_gate_4, send_low, send_high, input_sum, *g_up_4 = fence(
        done(*rest[:2]), send_low, send_high, input_sum, *rest[2 : 2 + n_kept]
    )

    def halves_of(own, other):
        both = beside(own, other)
        mine = lax.dynamic_slice_in_dim(both, core * rows_w, rows_w, 0)
        return mine, lax.dynamic_slice_in_dim(both, (1 - core) * rows_w, rows_w, 0)

    def panel(mine, got):
        whole = jnp.zeros((rows_w, 4 * hid), BF16)
        for block, u, c in (
            (mine[:, :hid], upper, core),
            (mine[:, hid:], 1 - upper, core),
            (got[:, :hid], upper, 1 - core),
            (got[:, hid:], 1 - upper, 1 - core),
        ):
            whole = lax.dynamic_update_slice(whole, block, (0, (u * 2 + c) * hid))
        return whole

    g_gate_far = z_far(g_gate_4)
    g_up_4 = shrink(*g_up_4)
    expert_mine = kept(expert_mine, low, swap(send_low, "tensor", low))
    expert_other = kept(expert_other, high, swap(send_high, "tensor", high))
    input_mine, input_other = split_rows(input_sum)
    merged = len(t_bits) == 2
    if merged:
        send_high = beside(gone(expert_mine, high), gone(input_other, high))
        send_low = beside(gone(expert_other, low), gone(input_mine, low))
    else:
        send_high, send_low = gone(input_other, high), gone(input_mine, low)
    g_gate_far, expert_mine, expert_other, input_mine, input_other, send_low, send_high, *rest = (
        fence(
            g_gate_far, expert_mine, expert_other, input_mine, input_other, send_low, send_high,
            *g_up_4, *g_gate_own
        )
    )
    g_up_4, send_low, send_high, *g_gate_own = fence(
        done(*rest[:2]), send_low, send_high, *rest[2:]
    )

    g_up_far = z_far(g_up_4)
    g_gate_own = shrink(*g_gate_own)
    got_high, got_low = swap(send_high, "tensor", high), swap(send_low, "tensor", low)
    if merged:
        expert_mine = kept(expert_mine, high, got_high[:, :width])
        expert_other = kept(expert_other, low, got_low[:, :width])
        got_high, got_low = got_high[:, width:], got_low[:, width:]
    else:
        for bit in t_bits[1:]:
            expert_mine = step(expert_mine, bit)
        for bit in t_bits[:-1][::-1]:
            expert_other = step(expert_other, bit)
    input_other = kept(input_other, high, got_high)
    input_mine = kept(input_mine, low, got_low)
    g_up_far, expert_mine, expert_other, input_mine, input_other, g_down_far, g_gate_far, *rest = fence(
        g_up_far, expert_mine[0], expert_other[0], input_mine, input_other, g_down_far, g_gate_far,
        *g_gate_own, *g_down_own, *g_up_own
    )
    g_gate_own, g_down_own, g_up_own = rest[:2], rest[2:4], rest[4:]

    g_up_own = shrink(*g_up_own)
    expert_got = z_far(expert_other)
    for bit in t_bits[1:]:
        input_mine = step(input_mine, bit)
    for bit in t_bits[:-1][::-1]:
        input_other = step(input_other, bit)
    input_mine, input_other, g_down_far, g_gate_far, *rest = fence(
        input_mine[0], input_other[0], g_down_far, g_gate_far, *g_down_own, *g_gate_own
    )
    down_mine, down_send = halves_of(done(*rest[:2]), g_down_far)
    gate_mine, gate_send = halves_of(done(*rest[2:]), g_gate_far)
    got = across(cat(down_send, gate_send))
    down_out, gate_out = panel(down_mine, got[:rows_w]), panel(gate_mine, got[rows_w:])
    up_mine, up_send = halves_of(done(*g_up_own), g_up_far)
    up_out = panel(up_mine, across(up_send))
    input_got = z_far(input_other)
    expert_cols = expert_mine.astype(F32) + expert_got.astype(F32)
    grad_cols = lax.dynamic_slice_in_dim(rows_grad, me_t * width, width, 1)
    weight_rows = jnp.sum(grad_cols.astype(F32) * expert_cols, axis=1)
    for bit in t_bits:
        weight_rows = weight_rows + swap(weight_rows, "tensor", bit)
    weight_grad = jnp.sum(jnp.where(match, weight_rows[:, None], 0.0), axis=0)
    mixed = mm_first(hot, (row_weight[:, None] * expert_cols).astype(BF16)).astype(BF16)
    input_cols = (input_mine.astype(F32) + input_got.astype(F32)).astype(BF16)
    input_grad = mm_first(hot, input_cols).astype(BF16)
    return (mixed, input_grad, weight_grad, gate_out, up_out, down_out)


def solution(mesh):
    return jax.shard_map(
        local,
        mesh=mesh,
        in_specs=(
            P("dp", None),
            P("dp", None),
            P("dp", None),
            P("dp", None),
            P("dp", "tensor"),
            P("dp", "tensor"),
            P("dp", "tensor"),
        ),
        out_specs=(
            P("dp", "tensor"),
            P("dp", "tensor"),
            P("dp"),
            P("dp", "tensor"),
            P("dp", "tensor"),
            P("dp", "tensor"),
        ),
        check_vma=False,
    )
```

```python
import jax
import jax.numpy as jnp
from jax import lax
from jax.sharding import PartitionSpec as P

BF16 = jnp.bfloat16
F32 = jnp.float32


def dot(left, right, dims):
    return lax.dot_general(left, right, (dims, ((), ())), preferred_element_type=F32)


def mm(left, right):
    return dot(left, right, ((1,), (0,)))


def mm_last(left, right):
    return dot(left, right, ((1,), (1,)))


def mm_first(left, right):
    return dot(left, right, ((0,), (0,)))


def swap(value, axis, distance):
    size = lax.axis_size(axis)
    return lax.ppermute(value, axis, [(i, i ^ distance) for i in range(size)])


def fence(*values):
    return lax.optimization_barrier(values)


def select_rows(assign_block, combine_block, row_limit):
    expert_hit = assign_block == 0
    routed = jnp.any(expert_hit, axis=1)
    weight = jnp.sum(
        jnp.where(expert_hit, combine_block, jnp.zeros((), combine_block.dtype)), axis=1
    )
    place = jnp.cumsum(routed.astype(jnp.int32)) - 1
    match = routed[None, :] & (place[None, :] == jnp.arange(row_limit, dtype=jnp.int32)[:, None])
    row_weight = jnp.sum(jnp.where(match, weight[None, :], 0.0), axis=1)
    return (match, row_weight)


def cat(*values):
    return jnp.concatenate(values, axis=0)


def beside(*values):
    return jnp.concatenate(values, axis=1)


def by_bits(blocks, index):
    bit = 1
    while bit < len(blocks):
        flag = (index & bit) != 0
        blocks = [jnp.where(flag, blocks[p ^ bit], blocks[p]) for p in range(len(blocks))]
        bit *= 2
    return blocks


def local(tokens, assign, combine, cotangent, w_gate, w_up, w_down_t):
    token_total, depth = tokens.shape
    row_limit = token_total // 2
    n_dp = lax.axis_size("dp")
    n_tensor = lax.axis_size("tensor")
    me = lax.axis_index("dp")
    me_t = lax.axis_index("tensor")
    chip, core = me // 2, me % 2
    far = n_dp // 2
    upper = me // far
    rows_w = w_gate.shape[0]
    pair = 2 * rows_w
    n_chip = n_dp // 2
    hid = w_gate.shape[1] // 4
    width = depth // n_tensor
    mids = [1 << i for i in range(1, far.bit_length() - 1)]
    t_bits = [1 << i for i in range(n_tensor.bit_length() - 1)]

    def z_far(block):
        return swap(block, "dp", far)

    def across(block):
        return swap(block, "dp", 1)

    def grow(block):
        blocks = [block]
        for bit in mids:
            count, rows = len(blocks), block.shape[0]
            got = swap(cat(*blocks) if count > 1 else block, "dp", bit)
            blocks = blocks + [got[i * rows : (i + 1) * rows] for i in range(count)]
        return blocks

    def put(full, blocks):
        for j, block in blocks.items():
            full = lax.dynamic_update_index_in_dim(full, block, chip ^ j, 0)
        return full

    half_n = n_chip // 2

    def block_of(panel, j):
        return lax.dynamic_index_in_dim(panel.reshape(n_chip, pair, hid), chip ^ j, 0, False)

    def blocks_own(panel):
        return {j: block_of(panel, j) for j in range(n_chip // 2)}

    def blocks_far(panel):
        return {j: block_of(panel, j ^ (n_chip // 2)) for j in range(n_chip // 2)}

    def add(blocks, got):
        return {
            j: (blocks[j].astype(F32) + got[i * pair : (i + 1) * pair].astype(F32)).astype(BF16)
            for i, j in enumerate(blocks)
        }

    def first_send(blocks):
        bit = mids[-1] // 2
        gone = [blocks[j] for j in blocks if j & bit]
        return (
            cat(*gone) if len(gone) > 1 else gone[0],
            *(blocks[j] for j in blocks if not j & bit),
        )

    def shrink(send, *kept):
        got = swap(send, "dp", mids[-1])
        for bit in mids[:-1][::-1]:
            blocks = add(dict(enumerate(kept)), got)
            count = len(blocks) // 2
            got = swap(cat(*(blocks[j + count] for j in range(count))), "dp", bit)
            kept = tuple(blocks[j] for j in range(count))
        return kept[0], got

    def done(kept, got):
        return (kept.astype(F32) + got.astype(F32)).astype(BF16)

    def part(w, u, c):
        return lax.dynamic_slice_in_dim(w, (u * 2 + c) * hid, hid, 1)

    def to_sibling(w):
        return beside(part(w, upper, 1 - core), part(w, 1 - upper, 1 - core))

    def by_core(mine, got):
        return jnp.where(core == 0, cat(mine, got), cat(got, mine))

    def pair_rows(w, got):
        mine = by_core(part(w, upper, core), got[:, :hid])
        other = by_core(part(w, 1 - upper, core), got[:, hid:])
        return mine, other

    gate_0 = lax.dynamic_slice_in_dim(w_gate, upper * 2 * hid, 2 * hid, 1)
    gate_4 = z_far(lax.dynamic_slice_in_dim(w_gate, (1 - upper) * 2 * hid, 2 * hid, 1))
    gate_own = grow(gate_0)
    match, row_weight = select_rows(assign, combine, row_limit)
    hot = match.astype(BF16)
    rows_in = mm(hot, tokens).astype(BF16)
    rows_grad = mm(hot, cotangent).astype(BF16)
    out_grad = (row_weight[:, None] * rows_grad.astype(F32)).astype(BF16)
    quarter = cat(
        *(lax.dynamic_slice_in_dim(v, me_t * width, width, 1) for v in (rows_in, out_grad))
    )
    send = cat(to_sibling(w_up), to_sibling(w_down_t))
    gate_4, quarter, rows_in, out_grad, send, *gate_own = fence(
        gate_4, quarter, rows_in, out_grad, send, *gate_own
    )

    quarter = z_far(quarter)
    gate_far = grow(gate_4)
    in_sib, out_sib = across(rows_in), across(out_grad)
    got = across(send)
    up_0, up_1 = pair_rows(w_up, got[:rows_w])
    down_0, down_1 = pair_rows(w_down_t, got[rows_w:])
    own = beside(up_0, down_0)
    quarter, in_sib, out_sib, own, up_1, down_1, *gate_far = fence(
        quarter, in_sib, out_sib, own, up_1, down_1, *gate_far
    )

    up_4 = z_far(up_1)
    own = grow(own)
    quarters = [quarter] + [swap(quarter, "tensor", k) for k in range(1, n_tensor)]
    gate_all = jnp.stack(gate_own + gate_far)
    gate_mine = lax.dynamic_slice_in_dim(gate_all, core * hid, hid, 2)
    gate_send = lax.dynamic_slice_in_dim(gate_all, (1 - core) * hid, hid, 2)
    empty = jnp.zeros((n_chip, pair, hid), BF16)
    up = put(empty, {0: own[0][:, :hid]})
    down = put(empty, {0: own[0][:, hid:]})
    up_4, gate_mine, gate_send, down_1, up, down, *rest = fence(
        up_4, gate_mine, gate_send, down_1, up, down, *quarters, *own
    )
    quarters, own = rest[: len(quarters)], rest[len(quarters) :]
    up_own, down_own = [b[:, :hid] for b in own], [b[:, hid:] for b in own]

    up_far = grow(up_4)
    down_4 = z_far(down_1)
    gate_got, *quarters = fence(across(gate_send), *quarters)
    gate = jnp.zeros((n_chip, 2, rows_w, hid), BF16)
    for j in range(n_chip):
        gate = lax.dynamic_update_slice(gate, gate_mine[j][None, None], (chip ^ j, core, 0, 0))
        gate = lax.dynamic_update_slice(gate, gate_got[j][None, None], (chip ^ j, 1 - core, 0, 0))
    up = put(up, {j: up_own[j] for j in range(1, half_n)})
    up = put(up, {half_n: up_4})
    down = put(down, {j: down_own[j] for j in range(1, half_n)})
    gate = gate.reshape(depth, hid)

    def true_rows(first):
        return beside(*by_bits([q[first : first + row_limit] for q in quarters], me_t))

    in_away, out_away = true_rows(0), true_rows(row_limit)
    in_away_sib, out_away_sib = across(in_away), across(out_away)
    in_all = cat(rows_in, in_away, in_sib, in_away_sib)
    out_all = cat(out_grad, out_away, out_sib, out_away_sib)
    gate_pre = mm(in_all, gate)
    down_4, in_all, out_all, gate_pre, gate, up, down, *up_far = fence(
        down_4, in_all, out_all, gate_pre, gate, up, down, *up_far
    )

    down_far = grow(down_4)
    up = put(up, {j + half_n: up_far[j] for j in range(1, half_n)}).reshape(depth, hid)
    down = put(down, {half_n: down_4})
    up_pre = mm(in_all, up)
    sigmoid_gate = jax.nn.sigmoid(gate_pre)
    hidden = (gate_pre * sigmoid_gate * up_pre).astype(BF16)
    g_down = mm_first(out_all, hidden).astype(BF16)
    g_down, hidden, up_pre, up, down, *down_far = fence(
        g_down, hidden, up_pre, up, down, *down_far
    )

    table = 2 * row_limit
    g_down_4 = first_send(blocks_far(g_down))
    n_kept = len(g_down_4)
    g_down_4 = shrink(*g_down_4)
    own_send = first_send(blocks_own(g_down))
    down = put(down, {j + half_n: down_far[j] for j in range(1, half_n)}).reshape(depth, hid)
    hidden_grad = mm(out_all, down)
    gate_grad = (
        hidden_grad * up_pre * sigmoid_gate * (1.0 + gate_pre * (1.0 - sigmoid_gate))
    ).astype(BF16)
    up_grad = (hidden_grad * gate_pre * sigmoid_gate).astype(BF16)
    gate_grad, up_grad, *rest = fence(gate_grad, up_grad, *g_down_4, *own_send)
    g_down_4, own_send = done(*rest[:2]), rest[2:]
    g_down_own = shrink(*own_send)
    g_gate = mm_first(in_all, gate_grad).astype(BF16)
    expert_got = across(mm_last(hidden[table:], down).astype(BF16))

    def input_part(rows):
        return mm_last(gate_grad[rows], gate) + mm_last(up_grad[rows], up)

    input_sib = input_part(slice(table, None)).astype(BF16)
    down, gate_grad, up_grad, g_gate, expert_got, input_sib, g_down_4, *g_down_own = fence(
        down, gate_grad, up_grad, g_gate, expert_got, input_sib, g_down_4, *g_down_own
    )
    g_gate_4, g_gate_own = first_send(blocks_far(g_gate)), first_send(blocks_own(g_gate))

    g_down_far = z_far(g_down_4)
    g_gate_4 = shrink(*g_gate_4)
    input_got = across(input_sib)
    g_up = mm_first(in_all, up_grad).astype(BF16)
    expert_sum = (mm_last(hidden[:table], down) + expert_got.astype(F32)).astype(BF16)
    input_sum = (input_part(slice(None, table)) + input_got.astype(F32)).astype(BF16)

    def split_parts(value):
        return {
            k: lax.dynamic_slice_in_dim(value, (me_t ^ k) * width, width, 1)
            for k in range(n_tensor)
        }

    def gone(parts, bit):
        return beside(*(parts[k] for k in parts if k & bit))

    def kept(parts, bit, got):
        keep = [k for k in parts if not k & bit]
        return {
            k: (parts[k].astype(F32) + got[:, i * width : (i + 1) * width].astype(F32)).astype(BF16)
            for i, k in enumerate(keep)
        }

    def step(parts, bit):
        return kept(parts, bit, swap(gone(parts, bit), "tensor", bit))

    def split_rows(value):
        return split_parts(value[:row_limit]), split_parts(value[row_limit:])

    def flat(parts):
        return [parts[k] for k in parts]

    low, high = t_bits[0], t_bits[-1]
    expert_mine, expert_other = split_rows(expert_sum)
    send_low, send_high = gone(expert_mine, low), gone(expert_other, high)
    g_up_4, g_up_own = first_send(blocks_far(g_up)), first_send(blocks_own(g_up))
    g_down_far, input_sum, send_low, send_high, *rest = fence(
        g_down_far, input_sum, send_low, send_high, *g_gate_4, *g_up_4, *g_up_own
    )
    g_up_own = rest[2 + n_kept :]
    g_gate_4, send_low, send_high, input_sum, *g_up_4 = fence(
        done(*rest[:2]), send_low, send_high, input_sum, *rest[2 : 2 + n_kept]
    )

    def halves_of(own, other):
        both = beside(own, other)
        mine = lax.dynamic_slice_in_dim(both, core * rows_w, rows_w, 0)
        return mine, lax.dynamic_slice_in_dim(both, (1 - core) * rows_w, rows_w, 0)

    def panel(mine, got):
        whole = jnp.zeros((rows_w, 4 * hid), BF16)
        for block, u, c in (
            (mine[:, :hid], upper, core),
            (mine[:, hid:], 1 - upper, core),
            (got[:, :hid], upper, 1 - core),
            (got[:, hid:], 1 - upper, 1 - core),
        ):
            whole = lax.dynamic_update_slice(whole, block, (0, (u * 2 + c) * hid))
        return whole

    g_gate_far = z_far(g_gate_4)
    g_up_4 = shrink(*g_up_4)
    expert_mine = kept(expert_mine, low, swap(send_low, "tensor", low))
    expert_other = kept(expert_other, high, swap(send_high, "tensor", high))
    input_mine, input_other = split_rows(input_sum)
    merged = len(t_bits) == 2
    if merged:
        send_high = beside(gone(expert_mine, high), gone(input_other, high))
        send_low = beside(gone(expert_other, low), gone(input_mine, low))
    else:
        send_high, send_low = gone(input_other, high), gone(input_mine, low)
    g_gate_far, expert_mine, expert_other, input_mine, input_other, send_low, send_high, *rest = (
        fence(
            g_gate_far, expert_mine, expert_other, input_mine, input_other, send_low, send_high,
            *g_up_4, *g_gate_own
        )
    )
    g_up_4, send_low, send_high, *g_gate_own = fence(
        done(*rest[:2]), send_low, send_high, *rest[2:]
    )

    g_up_far = z_far(g_up_4)
    g_gate_own = shrink(*g_gate_own)
    got_high, got_low = swap(send_high, "tensor", high), swap(send_low, "tensor", low)
    if merged:
        expert_mine = kept(expert_mine, high, got_high[:, :width])
        expert_other = kept(expert_other, low, got_low[:, :width])
        got_high, got_low = got_high[:, width:], got_low[:, width:]
    else:
        for bit in t_bits[1:]:
            expert_mine = step(expert_mine, bit)
        for bit in t_bits[:-1][::-1]:
            expert_other = step(expert_other, bit)
    input_other = kept(input_other, high, got_high)
    input_mine = kept(input_mine, low, got_low)
    g_up_far, expert_mine, expert_other, input_mine, input_other, g_down_far, g_gate_far, *rest = fence(
        g_up_far, expert_mine[0], expert_other[0], input_mine, input_other, g_down_far, g_gate_far,
        *g_gate_own, *g_down_own, *g_up_own
    )
    g_gate_own, g_down_own, g_up_own = rest[:2], rest[2:4], rest[4:]

    g_up_own = shrink(*g_up_own)
    expert_got = z_far(expert_other)
    for bit in t_bits[1:]:
        input_mine = step(input_mine, bit)
    for bit in t_bits[:-1][::-1]:
        input_other = step(input_other, bit)
    input_mine, input_other, g_down_far, g_gate_far, *rest = fence(
        input_mine[0], input_other[0], g_down_far, g_gate_far, *g_down_own, *g_gate_own
    )
    down_mine, down_send = halves_of(done(*rest[:2]), g_down_far)
    gate_mine, gate_send = halves_of(done(*rest[2:]), g_gate_far)
    got = across(cat(down_send, gate_send))
    down_out, gate_out = panel(down_mine, got[:rows_w]), panel(gate_mine, got[rows_w:])
    up_mine, up_send = halves_of(done(*g_up_own), g_up_far)
    up_out = panel(up_mine, across(up_send))
    input_got = z_far(input_other)
    expert_cols = expert_mine.astype(F32) + expert_got.astype(F32)
    grad_cols = lax.dynamic_slice_in_dim(rows_grad, me_t * width, width, 1)
    weight_rows = jnp.sum(grad_cols.astype(F32) * expert_cols, axis=1)
    for bit in t_bits:
        weight_rows = weight_rows + swap(weight_rows, "tensor", bit)
    weight_grad = jnp.sum(jnp.where(match, weight_rows[:, None], 0.0), axis=0)
    mixed = mm_first(hot, (row_weight[:, None] * expert_cols).astype(BF16)).astype(BF16)
    input_cols = (input_mine.astype(F32) + input_got.astype(F32)).astype(BF16)
    input_grad = mm_first(hot, input_cols).astype(BF16)
    return (mixed, input_grad, weight_grad, gate_out, up_out, down_out)


def solution(mesh):
    return jax.shard_map(
        local,
        mesh=mesh,
        in_specs=(
            P("dp", None),
            P("dp", None),
            P("dp", None),
            P("dp", None),
            P("dp", "tensor"),
            P("dp", "tensor"),
            P("dp", "tensor"),
        ),
        out_specs=(
            P("dp", "tensor"),
            P("dp", "tensor"),
            P("dp"),
            P("dp", "tensor"),
            P("dp", "tensor"),
            P("dp", "tensor"),
        ),
        check_vma=False,
    )
```

```python
import jax
import jax.numpy as jnp
from jax import lax
from jax.sharding import PartitionSpec as P

BF16 = jnp.bfloat16
F32 = jnp.float32


def dot(left, right, dims):
    return lax.dot_general(left, right, (dims, ((), ())), preferred_element_type=F32)


def mm(left, right):
    return dot(left, right, ((1,), (0,)))


def mm_last(left, right):
    return dot(left, right, ((1,), (1,)))


def mm_first(left, right):
    return dot(left, right, ((0,), (0,)))


def swap(value, axis, distance):
    size = lax.axis_size(axis)
    return lax.ppermute(value, axis, [(i, i ^ distance) for i in range(size)])


def fence(*values):
    return lax.optimization_barrier(values)


def select_rows(assign_block, combine_block, row_limit):
    expert_hit = assign_block == 0
    routed = jnp.any(expert_hit, axis=1)
    weight = jnp.sum(
        jnp.where(expert_hit, combine_block, jnp.zeros((), combine_block.dtype)), axis=1
    )
    place = jnp.cumsum(routed.astype(jnp.int32)) - 1
    match = routed[None, :] & (place[None, :] == jnp.arange(row_limit, dtype=jnp.int32)[:, None])
    row_weight = jnp.sum(jnp.where(match, weight[None, :], 0.0), axis=1)
    return (match, row_weight)


def cat(*values):
    return jnp.concatenate(values, axis=0)


def beside(*values):
    return jnp.concatenate(values, axis=1)


def by_bits(blocks, index):
    bit = 1
    while bit < len(blocks):
        flag = (index & bit) != 0
        blocks = [jnp.where(flag, blocks[p ^ bit], blocks[p]) for p in range(len(blocks))]
        bit *= 2
    return blocks


def local(tokens, assign, combine, cotangent, w_gate, w_up, w_down_t):
    token_total, depth = tokens.shape
    row_limit = token_total // 2
    n_dp = lax.axis_size("dp")
    n_tensor = lax.axis_size("tensor")
    me = lax.axis_index("dp")
    me_t = lax.axis_index("tensor")
    chip, core = me // 2, me % 2
    far = n_dp // 2
    upper = me // far
    rows_w = w_gate.shape[0]
    pair = 2 * rows_w
    n_chip = n_dp // 2
    hid = w_gate.shape[1] // 4
    width = depth // n_tensor
    mids = [1 << i for i in range(1, far.bit_length() - 1)]
    t_bits = [1 << i for i in range(n_tensor.bit_length() - 1)]

    def z_far(block):
        return swap(block, "dp", far)

    def across(block):
        return swap(block, "dp", 1)

    def grow(block):
        blocks = [block]
        for bit in mids:
            count, rows = len(blocks), block.shape[0]
            got = swap(cat(*blocks) if count > 1 else block, "dp", bit)
            blocks = blocks + [got[i * rows : (i + 1) * rows] for i in range(count)]
        return blocks

    def put(full, blocks):
        for j, block in blocks.items():
            full = lax.dynamic_update_index_in_dim(full, block, chip ^ j, 0)
        return full

    half_n = n_chip // 2

    def block_of(panel, j):
        return lax.dynamic_index_in_dim(panel.reshape(n_chip, pair, hid), chip ^ j, 0, False)

    def blocks_own(panel):
        return {j: block_of(panel, j) for j in range(n_chip // 2)}

    def blocks_far(panel):
        return {j: block_of(panel, j ^ (n_chip // 2)) for j in range(n_chip // 2)}

    def add(blocks, got):
        return {
            j: (blocks[j].astype(F32) + got[i * pair : (i + 1) * pair].astype(F32)).astype(BF16)
            for i, j in enumerate(blocks)
        }

    def first_send(blocks):
        bit = mids[-1] // 2
        gone = [blocks[j] for j in blocks if j & bit]
        return (
            cat(*gone) if len(gone) > 1 else gone[0],
            *(blocks[j] for j in blocks if not j & bit),
        )

    def shrink(send, *kept):
        got = swap(send, "dp", mids[-1])
        for bit in mids[:-1][::-1]:
            blocks = add(dict(enumerate(kept)), got)
            count = len(blocks) // 2
            got = swap(cat(*(blocks[j + count] for j in range(count))), "dp", bit)
            kept = tuple(blocks[j] for j in range(count))
        return kept[0], got

    def done(kept, got):
        return (kept.astype(F32) + got.astype(F32)).astype(BF16)

    def part(w, u, c):
        return lax.dynamic_slice_in_dim(w, (u * 2 + c) * hid, hid, 1)

    def to_sibling(w):
        return beside(part(w, upper, 1 - core), part(w, 1 - upper, 1 - core))

    def by_core(mine, got):
        return jnp.where(core == 0, cat(mine, got), cat(got, mine))

    def pair_rows(w, got):
        mine = by_core(part(w, upper, core), got[:, :hid])
        other = by_core(part(w, 1 - upper, core), got[:, hid:])
        return mine, other

    gate_0 = lax.dynamic_slice_in_dim(w_gate, upper * 2 * hid, 2 * hid, 1)
    gate_4 = z_far(lax.dynamic_slice_in_dim(w_gate, (1 - upper) * 2 * hid, 2 * hid, 1))
    gate_own = grow(gate_0)
    match, row_weight = select_rows(assign, combine, row_limit)
    hot = match.astype(BF16)
    rows_in = mm(hot, tokens).astype(BF16)
    rows_grad = mm(hot, cotangent).astype(BF16)
    out_grad = (row_weight[:, None] * rows_grad.astype(F32)).astype(BF16)
    quarter = cat(
        *(lax.dynamic_slice_in_dim(v, me_t * width, width, 1) for v in (rows_in, out_grad))
    )
    send = cat(to_sibling(w_up), to_sibling(w_down_t))
    gate_4, quarter, rows_in, out_grad, send, *gate_own = fence(
        gate_4, quarter, rows_in, out_grad, send, *gate_own
    )

    quarter = z_far(quarter)
    gate_far = grow(gate_4)
    in_sib, out_sib = across(rows_in), across(out_grad)
    got = across(send)
    up_0, up_1 = pair_rows(w_up, got[:rows_w])
    down_0, down_1 = pair_rows(w_down_t, got[rows_w:])
    own = beside(up_0, down_0)
    quarter, in_sib, out_sib, own, up_1, down_1, *gate_far = fence(
        quarter, in_sib, out_sib, own, up_1, down_1, *gate_far
    )

    up_4 = z_far(up_1)
    own = grow(own)
    quarters = [quarter] + [swap(quarter, "tensor", k) for k in range(1, n_tensor)]
    gate_all = jnp.stack(gate_own + gate_far)
    gate_mine = lax.dynamic_slice_in_dim(gate_all, core * hid, hid, 2)
    gate_send = lax.dynamic_slice_in_dim(gate_all, (1 - core) * hid, hid, 2)
    empty = jnp.zeros((n_chip, pair, hid), BF16)
    up = put(empty, {0: own[0][:, :hid]})
    down = put(empty, {0: own[0][:, hid:]})
    up_4, gate_mine, gate_send, down_1, up, down, *rest = fence(
        up_4, gate_mine, gate_send, down_1, up, down, *quarters, *own
    )
    quarters, own = rest[: len(quarters)], rest[len(quarters) :]
    up_own, down_own = [b[:, :hid] for b in own], [b[:, hid:] for b in own]

    up_far = grow(up_4)
    down_4 = z_far(down_1)
    gate_got, *quarters = fence(across(gate_send), *quarters)
    gate = jnp.zeros((n_chip, 2, rows_w, hid), BF16)
    for j in range(n_chip):
        gate = lax.dynamic_update_slice(gate, gate_mine[j][None, None], (chip ^ j, core, 0, 0))
        gate = lax.dynamic_update_slice(gate, gate_got[j][None, None], (chip ^ j, 1 - core, 0, 0))
    up = put(up, {j: up_own[j] for j in range(1, half_n)})
    up = put(up, {half_n: up_4})
    down = put(down, {j: down_own[j] for j in range(1, half_n)})
    gate = gate.reshape(depth, hid)

    def true_rows(first):
        return beside(*by_bits([q[first : first + row_limit] for q in quarters], me_t))

    in_away, out_away = true_rows(0), true_rows(row_limit)
    in_away_sib, out_away_sib = across(in_away), across(out_away)
    in_all = cat(rows_in, in_away, in_sib, in_away_sib)
    out_all = cat(out_grad, out_away, out_sib, out_away_sib)
    gate_pre = mm(in_all, gate)
    down_4, in_all, out_all, gate_pre, gate, up, down, *up_far = fence(
        down_4, in_all, out_all, gate_pre, gate, up, down, *up_far
    )

    down_far = grow(down_4)
    up = put(up, {j + half_n: up_far[j] for j in range(1, half_n)}).reshape(depth, hid)
    down = put(down, {half_n: down_4})
    up_pre = mm(in_all, up)
    sigmoid_gate = jax.nn.sigmoid(gate_pre)
    hidden = (gate_pre * sigmoid_gate * up_pre).astype(BF16)
    g_down = mm_first(out_all, hidden).astype(BF16)
    g_down, hidden, up_pre, up, down, *down_far = fence(
        g_down, hidden, up_pre, up, down, *down_far
    )

    table = 2 * row_limit
    g_down_4 = first_send(blocks_far(g_down))
    n_kept = len(g_down_4)
    g_down_4 = shrink(*g_down_4)
    own_send = first_send(blocks_own(g_down))
    down = put(down, {j + half_n: down_far[j] for j in range(1, half_n)}).reshape(depth, hid)
    hidden_grad = mm(out_all, down)
    gate_grad = (
        hidden_grad * up_pre * sigmoid_gate * (1.0 + gate_pre * (1.0 - sigmoid_gate))
    ).astype(BF16)
    up_grad = (hidden_grad * gate_pre * sigmoid_gate).astype(BF16)
    gate_grad, up_grad, *rest = fence(gate_grad, up_grad, *g_down_4, *own_send)
    g_down_4, own_send = done(*rest[:2]), rest[2:]
    g_down_own = shrink(*own_send)
    g_down_far = z_far(g_down_4)
    g_gate = mm_first(in_all, gate_grad).astype(BF16)
    expert_got = across(mm_last(hidden[table:], down).astype(BF16))

    def input_part(rows):
        return mm_last(gate_grad[rows], gate) + mm_last(up_grad[rows], up)

    input_sib = input_part(slice(table, None)).astype(BF16)
    g_gate_4, g_gate_own = first_send(blocks_far(g_gate)), first_send(blocks_own(g_gate))

    g_gate_4 = shrink(*g_gate_4)
    input_got = across(input_sib)
    g_up = mm_first(in_all, up_grad).astype(BF16)
    expert_sum = (mm_last(hidden[:table], down) + expert_got.astype(F32)).astype(BF16)
    input_sum = (input_part(slice(None, table)) + input_got.astype(F32)).astype(BF16)

    def split_parts(value):
        return {
            k: lax.dynamic_slice_in_dim(value, (me_t ^ k) * width, width, 1)
            for k in range(n_tensor)
        }

    def gone(parts, bit):
        return beside(*(parts[k] for k in parts if k & bit))

    def kept(parts, bit, got):
        keep = [k for k in parts if not k & bit]
        return {
            k: (parts[k].astype(F32) + got[:, i * width : (i + 1) * width].astype(F32)).astype(BF16)
            for i, k in enumerate(keep)
        }

    def step(parts, bit):
        return kept(parts, bit, swap(gone(parts, bit), "tensor", bit))

    def split_rows(value):
        return split_parts(value[:row_limit]), split_parts(value[row_limit:])

    def flat(parts):
        return [parts[k] for k in parts]

    low, high = t_bits[0], t_bits[-1]
    expert_mine, expert_other = split_rows(expert_sum)
    send_low, send_high = gone(expert_mine, low), gone(expert_other, high)
    g_up_4, g_up_own = first_send(blocks_far(g_up)), first_send(blocks_own(g_up))
    g_down_far, input_sum, send_low, send_high, *rest = fence(
        g_down_far, input_sum, send_low, send_high, *g_down_own, *g_gate_4, *g_up_4, *g_up_own
    )
    g_down_own, rest = rest[:2], rest[2:]
    g_up_own = rest[2 + n_kept :]
    g_gate_4, send_low, send_high, input_sum, *g_up_4 = fence(
        done(*rest[:2]), send_low, send_high, input_sum, *rest[2 : 2 + n_kept]
    )

    def halves_of(own, other):
        both = beside(own, other)
        mine = lax.dynamic_slice_in_dim(both, core * rows_w, rows_w, 0)
        return mine, lax.dynamic_slice_in_dim(both, (1 - core) * rows_w, rows_w, 0)

    def panel(mine, got):
        whole = jnp.zeros((rows_w, 4 * hid), BF16)
        for block, u, c in (
            (mine[:, :hid], upper, core),
            (mine[:, hid:], 1 - upper, core),
            (got[:, :hid], upper, 1 - core),
            (got[:, hid:], 1 - upper, 1 - core),
        ):
            whole = lax.dynamic_update_slice(whole, block, (0, (u * 2 + c) * hid))
        return whole

    g_gate_far = z_far(g_gate_4)
    g_up_4 = shrink(*g_up_4)
    expert_mine = kept(expert_mine, low, swap(send_low, "tensor", low))
    expert_other = kept(expert_other, high, swap(send_high, "tensor", high))
    input_mine, input_other = split_rows(input_sum)
    merged = len(t_bits) == 2
    if merged:
        send_high = beside(gone(expert_mine, high), gone(input_other, high))
        send_low = beside(gone(expert_other, low), gone(input_mine, low))
    else:
        send_high, send_low = gone(input_other, high), gone(input_mine, low)
    g_gate_far, expert_mine, expert_other, input_mine, input_other, send_low, send_high, *rest = (
        fence(
            g_gate_far, expert_mine, expert_other, input_mine, input_other, send_low, send_high,
            *g_up_4, *g_gate_own
        )
    )
    g_up_4, send_low, send_high, *g_gate_own = fence(
        done(*rest[:2]), send_low, send_high, *rest[2:]
    )

    g_up_far = z_far(g_up_4)
    g_gate_own = shrink(*g_gate_own)
    got_high, got_low = swap(send_high, "tensor", high), swap(send_low, "tensor", low)
    if merged:
        expert_mine = kept(expert_mine, high, got_high[:, :width])
        expert_other = kept(expert_other, low, got_low[:, :width])
        got_high, got_low = got_high[:, width:], got_low[:, width:]
    else:
        for bit in t_bits[1:]:
            expert_mine = step(expert_mine, bit)
        for bit in t_bits[:-1][::-1]:
            expert_other = step(expert_other, bit)
    input_other = kept(input_other, high, got_high)
    input_mine = kept(input_mine, low, got_low)
    g_up_far, expert_mine, expert_other, input_mine, input_other, g_down_far, g_gate_far, *rest = fence(
        g_up_far, expert_mine[0], expert_other[0], input_mine, input_other, g_down_far, g_gate_far,
        *g_gate_own, *g_down_own, *g_up_own
    )
    g_gate_own, g_down_own, g_up_own = rest[:2], rest[2:4], rest[4:]

    g_up_own = shrink(*g_up_own)
    expert_got = z_far(expert_other)
    for bit in t_bits[1:]:
        input_mine = step(input_mine, bit)
    for bit in t_bits[:-1][::-1]:
        input_other = step(input_other, bit)
    input_mine, input_other, g_down_far, g_gate_far, *rest = fence(
        input_mine[0], input_other[0], g_down_far, g_gate_far, *g_down_own, *g_gate_own
    )
    down_mine, down_send = halves_of(done(*rest[:2]), g_down_far)
    gate_mine, gate_send = halves_of(done(*rest[2:]), g_gate_far)
    got = across(cat(down_send, gate_send))
    down_out, gate_out = panel(down_mine, got[:rows_w]), panel(gate_mine, got[rows_w:])
    up_mine, up_send = halves_of(done(*g_up_own), g_up_far)
    up_out = panel(up_mine, across(up_send))
    input_got = z_far(input_other)
    expert_cols = expert_mine.astype(F32) + expert_got.astype(F32)
    grad_cols = lax.dynamic_slice_in_dim(rows_grad, me_t * width, width, 1)
    weight_rows = jnp.sum(grad_cols.astype(F32) * expert_cols, axis=1)
    for bit in t_bits:
        weight_rows = weight_rows + swap(weight_rows, "tensor", bit)
    weight_grad = jnp.sum(jnp.where(match, weight_rows[:, None], 0.0), axis=0)
    mixed = mm_first(hot, (row_weight[:, None] * expert_cols).astype(BF16)).astype(BF16)
    input_cols = (input_mine.astype(F32) + input_got.astype(F32)).astype(BF16)
    input_grad = mm_first(hot, input_cols).astype(BF16)
    return (mixed, input_grad, weight_grad, gate_out, up_out, down_out)


def solution(mesh):
    return jax.shard_map(
        local,
        mesh=mesh,
        in_specs=(
            P("dp", None),
            P("dp", None),
            P("dp", None),
            P("dp", None),
            P("dp", "tensor"),
            P("dp", "tensor"),
            P("dp", "tensor"),
        ),
        out_specs=(
            P("dp", "tensor"),
            P("dp", "tensor"),
            P("dp"),
            P("dp", "tensor"),
            P("dp", "tensor"),
            P("dp", "tensor"),
        ),
        check_vma=False,
    )
```

```python
import jax
import jax.numpy as jnp
from jax import lax
from jax.sharding import PartitionSpec as P

BF16 = jnp.bfloat16
F32 = jnp.float32


def dot(left, right, dims):
    return lax.dot_general(left, right, (dims, ((), ())), preferred_element_type=F32)


def mm(left, right):
    return dot(left, right, ((1,), (0,)))


def mm_last(left, right):
    return dot(left, right, ((1,), (1,)))


def mm_first(left, right):
    return dot(left, right, ((0,), (0,)))


def swap(value, axis, distance):
    size = lax.axis_size(axis)
    return lax.ppermute(value, axis, [(i, i ^ distance) for i in range(size)])


def fence(*values):
    return lax.optimization_barrier(values)


def select_rows(assign_block, combine_block, row_limit):
    expert_hit = assign_block == 0
    routed = jnp.any(expert_hit, axis=1)
    weight = jnp.sum(
        jnp.where(expert_hit, combine_block, jnp.zeros((), combine_block.dtype)), axis=1
    )
    place = jnp.cumsum(routed.astype(jnp.int32)) - 1
    match = routed[None, :] & (place[None, :] == jnp.arange(row_limit, dtype=jnp.int32)[:, None])
    row_weight = jnp.sum(jnp.where(match, weight[None, :], 0.0), axis=1)
    return (match, row_weight)


def cat(*values):
    return jnp.concatenate(values, axis=0)


def beside(*values):
    return jnp.concatenate(values, axis=1)


def by_bits(blocks, index):
    bit = 1
    while bit < len(blocks):
        flag = (index & bit) != 0
        blocks = [jnp.where(flag, blocks[p ^ bit], blocks[p]) for p in range(len(blocks))]
        bit *= 2
    return blocks


def local(tokens, assign, combine, cotangent, w_gate, w_up, w_down_t):
    token_total, depth = tokens.shape
    row_limit = token_total // 2
    n_dp = lax.axis_size("dp")
    n_tensor = lax.axis_size("tensor")
    me = lax.axis_index("dp")
    me_t = lax.axis_index("tensor")
    chip, core = me // 2, me % 2
    far = n_dp // 2
    upper = me // far
    rows_w = w_gate.shape[0]
    pair = 2 * rows_w
    n_chip = n_dp // 2
    hid = w_gate.shape[1] // 4
    width = depth // n_tensor
    mids = [1 << i for i in range(1, far.bit_length() - 1)]
    t_bits = [1 << i for i in range(n_tensor.bit_length() - 1)]

    def z_far(block):
        return swap(block, "dp", far)

    def across(block):
        return swap(block, "dp", 1)

    def grow(block):
        blocks = [block]
        for bit in mids:
            count, rows = len(blocks), block.shape[0]
            got = swap(cat(*blocks) if count > 1 else block, "dp", bit)
            blocks = blocks + [got[i * rows : (i + 1) * rows] for i in range(count)]
        return blocks

    def put(full, blocks):
        for j, block in blocks.items():
            full = lax.dynamic_update_index_in_dim(full, block, chip ^ j, 0)
        return full

    half_n = n_chip // 2

    def block_of(panel, j):
        return lax.dynamic_index_in_dim(panel.reshape(n_chip, pair, hid), chip ^ j, 0, False)

    def blocks_own(panel):
        return {j: block_of(panel, j) for j in range(n_chip // 2)}

    def blocks_far(panel):
        return {j: block_of(panel, j ^ (n_chip // 2)) for j in range(n_chip // 2)}

    def add(blocks, got):
        return {
            j: (blocks[j].astype(F32) + got[i * pair : (i + 1) * pair].astype(F32)).astype(BF16)
            for i, j in enumerate(blocks)
        }

    def first_send(blocks):
        bit = mids[-1] // 2
        gone = [blocks[j] for j in blocks if j & bit]
        return (
            cat(*gone) if len(gone) > 1 else gone[0],
            *(blocks[j] for j in blocks if not j & bit),
        )

    def shrink(send, *kept):
        got = swap(send, "dp", mids[-1])
        for bit in mids[:-1][::-1]:
            blocks = add(dict(enumerate(kept)), got)
            count = len(blocks) // 2
            got = swap(cat(*(blocks[j + count] for j in range(count))), "dp", bit)
            kept = tuple(blocks[j] for j in range(count))
        return kept[0], got

    def done(kept, got):
        return (kept.astype(F32) + got.astype(F32)).astype(BF16)

    def part(w, u, c):
        return lax.dynamic_slice_in_dim(w, (u * 2 + c) * hid, hid, 1)

    def to_sibling(w):
        return beside(part(w, upper, 1 - core), part(w, 1 - upper, 1 - core))

    def by_core(mine, got):
        return jnp.where(core == 0, cat(mine, got), cat(got, mine))

    def pair_rows(w, got):
        mine = by_core(part(w, upper, core), got[:, :hid])
        other = by_core(part(w, 1 - upper, core), got[:, hid:])
        return mine, other

    gate_0 = lax.dynamic_slice_in_dim(w_gate, upper * 2 * hid, 2 * hid, 1)
    gate_4 = z_far(lax.dynamic_slice_in_dim(w_gate, (1 - upper) * 2 * hid, 2 * hid, 1))
    gate_own = grow(gate_0)
    match, row_weight = select_rows(assign, combine, row_limit)
    hot = match.astype(BF16)
    rows_in = mm(hot, tokens).astype(BF16)
    rows_grad = mm(hot, cotangent).astype(BF16)
    out_grad = (row_weight[:, None] * rows_grad.astype(F32)).astype(BF16)
    quarter = cat(
        *(lax.dynamic_slice_in_dim(v, me_t * width, width, 1) for v in (rows_in, out_grad))
    )
    send = cat(to_sibling(w_up), to_sibling(w_down_t))
    gate_4, quarter, rows_in, out_grad, send, *gate_own = fence(
        gate_4, quarter, rows_in, out_grad, send, *gate_own
    )

    quarter = z_far(quarter)
    gate_far = grow(gate_4)
    in_sib, out_sib = across(rows_in), across(out_grad)
    got = across(send)
    up_0, up_1 = pair_rows(w_up, got[:rows_w])
    down_0, down_1 = pair_rows(w_down_t, got[rows_w:])
    own = beside(up_0, down_0)
    quarter, in_sib, out_sib, own, up_1, down_1, *gate_far = fence(
        quarter, in_sib, out_sib, own, up_1, down_1, *gate_far
    )

    up_4 = z_far(up_1)
    own = grow(own)
    quarters = [quarter] + [swap(quarter, "tensor", k) for k in range(1, n_tensor)]
    gate_all = jnp.stack(gate_own + gate_far)
    gate_mine = lax.dynamic_slice_in_dim(gate_all, core * hid, hid, 2)
    gate_send = lax.dynamic_slice_in_dim(gate_all, (1 - core) * hid, hid, 2)
    empty = jnp.zeros((n_chip, pair, hid), BF16)
    up = put(empty, {0: own[0][:, :hid]})
    down = put(empty, {0: own[0][:, hid:]})
    up_4, gate_mine, gate_send, down_1, up, down, *rest = fence(
        up_4, gate_mine, gate_send, down_1, up, down, *quarters, *own
    )
    quarters, own = rest[: len(quarters)], rest[len(quarters) :]
    up_own, down_own = [b[:, :hid] for b in own], [b[:, hid:] for b in own]

    up_far = grow(up_4)
    down_4 = z_far(down_1)
    gate_got, *quarters = fence(across(gate_send), *quarters)
    gate = jnp.zeros((n_chip, 2, rows_w, hid), BF16)
    for j in range(n_chip):
        gate = lax.dynamic_update_slice(gate, gate_mine[j][None, None], (chip ^ j, core, 0, 0))
        gate = lax.dynamic_update_slice(gate, gate_got[j][None, None], (chip ^ j, 1 - core, 0, 0))
    up = put(up, {j: up_own[j] for j in range(1, half_n)})
    up = put(up, {half_n: up_4})
    down = put(down, {j: down_own[j] for j in range(1, half_n)})
    gate = gate.reshape(depth, hid)

    def true_rows(first):
        return beside(*by_bits([q[first : first + row_limit] for q in quarters], me_t))

    in_away, out_away = true_rows(0), true_rows(row_limit)
    in_away_sib, out_away_sib = across(in_away), across(out_away)
    in_all = cat(rows_in, in_away, in_sib, in_away_sib)
    out_all = cat(out_grad, out_away, out_sib, out_away_sib)
    gate_pre = mm(in_all, gate)
    down_4, in_all, out_all, gate_pre, gate, up, down, *up_far = fence(
        down_4, in_all, out_all, gate_pre, gate, up, down, *up_far
    )

    down_far = grow(down_4)
    up = put(up, {j + half_n: up_far[j] for j in range(1, half_n)}).reshape(depth, hid)
    down = put(down, {half_n: down_4})
    up_pre = mm(in_all, up)
    sigmoid_gate = jax.nn.sigmoid(gate_pre)
    hidden = (gate_pre * sigmoid_gate * up_pre).astype(BF16)
    g_down = mm_first(out_all, hidden).astype(BF16)
    g_down, hidden, up_pre, up, down, *down_far = fence(
        g_down, hidden, up_pre, up, down, *down_far
    )

    table = 2 * row_limit
    g_down_4 = first_send(blocks_far(g_down))
    n_kept = len(g_down_4)
    g_down_4 = shrink(*g_down_4)
    own_send = first_send(blocks_own(g_down))
    down = put(down, {j + half_n: down_far[j] for j in range(1, half_n)}).reshape(depth, hid)
    hidden_grad = mm(out_all, down)
    gate_grad = (
        hidden_grad * up_pre * sigmoid_gate * (1.0 + gate_pre * (1.0 - sigmoid_gate))
    ).astype(BF16)
    up_grad = (hidden_grad * gate_pre * sigmoid_gate).astype(BF16)
    gate_grad, up_grad, *rest = fence(gate_grad, up_grad, *g_down_4, *own_send)
    g_down_4, own_send = done(*rest[:2]), rest[2:]
    g_down_own = shrink(*own_send)
    g_down_far = z_far(g_down_4)
    g_gate = mm_first(in_all, gate_grad).astype(BF16)
    expert_got = across(mm_last(hidden[table:], down).astype(BF16))

    def input_part(rows):
        return mm_last(gate_grad[rows], gate) + mm_last(up_grad[rows], up)

    input_sib = input_part(slice(table, None)).astype(BF16)
    g_gate_4, g_gate_own = first_send(blocks_far(g_gate)), first_send(blocks_own(g_gate))

    g_gate_4 = shrink(*g_gate_4)
    input_got = across(input_sib)
    g_up = mm_first(in_all, up_grad).astype(BF16)
    expert_sum = (mm_last(hidden[:table], down) + expert_got.astype(F32)).astype(BF16)
    input_sum = (input_part(slice(None, table)) + input_got.astype(F32)).astype(BF16)

    def split_parts(value):
        return {
            k: lax.dynamic_slice_in_dim(value, (me_t ^ k) * width, width, 1)
            for k in range(n_tensor)
        }

    def gone(parts, bit):
        return beside(*(parts[k] for k in parts if k & bit))

    def kept(parts, bit, got):
        keep = [k for k in parts if not k & bit]
        return {
            k: (parts[k].astype(F32) + got[:, i * width : (i + 1) * width].astype(F32)).astype(BF16)
            for i, k in enumerate(keep)
        }

    def step(parts, bit):
        return kept(parts, bit, swap(gone(parts, bit), "tensor", bit))

    def split_rows(value):
        return split_parts(value[:row_limit]), split_parts(value[row_limit:])

    def flat(parts):
        return [parts[k] for k in parts]

    low, high = t_bits[0], t_bits[-1]
    expert_mine, expert_other = split_rows(expert_sum)
    send_low, send_high = gone(expert_mine, low), gone(expert_other, high)
    g_up_4, g_up_own = first_send(blocks_far(g_up)), first_send(blocks_own(g_up))
    got_low, got_high = swap(send_low, "tensor", low), swap(send_high, "tensor", high)
    g_down_far, input_sum, *rest = fence(
        g_down_far, input_sum, *g_down_own, *g_gate_4, *g_up_4, *g_up_own
    )
    g_down_own, rest = rest[:2], rest[2:]
    g_up_own = rest[2 + n_kept :]
    g_gate_4, input_sum, *g_up_4 = fence(done(*rest[:2]), input_sum, *rest[2 : 2 + n_kept])

    def halves_of(own, other):
        both = beside(own, other)
        mine = lax.dynamic_slice_in_dim(both, core * rows_w, rows_w, 0)
        return mine, lax.dynamic_slice_in_dim(both, (1 - core) * rows_w, rows_w, 0)

    def panel(mine, got):
        whole = jnp.zeros((rows_w, 4 * hid), BF16)
        for block, u, c in (
            (mine[:, :hid], upper, core),
            (mine[:, hid:], 1 - upper, core),
            (got[:, :hid], upper, 1 - core),
            (got[:, hid:], 1 - upper, 1 - core),
        ):
            whole = lax.dynamic_update_slice(whole, block, (0, (u * 2 + c) * hid))
        return whole

    g_gate_far = z_far(g_gate_4)
    g_up_4 = shrink(*g_up_4)
    expert_mine = kept(expert_mine, low, got_low)
    expert_other = kept(expert_other, high, got_high)
    input_mine, input_other = split_rows(input_sum)
    merged = len(t_bits) == 2
    if merged:
        send_high = beside(gone(expert_mine, high), gone(input_other, high))
        send_low = beside(gone(expert_other, low), gone(input_mine, low))
    else:
        send_high, send_low = gone(input_other, high), gone(input_mine, low)
    g_gate_far, expert_mine, expert_other, input_mine, input_other, send_low, send_high, *rest = (
        fence(
            g_gate_far, expert_mine, expert_other, input_mine, input_other, send_low, send_high,
            *g_up_4, *g_gate_own
        )
    )
    g_up_4, send_low, send_high, *g_gate_own = fence(
        done(*rest[:2]), send_low, send_high, *rest[2:]
    )

    g_up_far = z_far(g_up_4)
    g_gate_own = shrink(*g_gate_own)
    got_high, got_low = swap(send_high, "tensor", high), swap(send_low, "tensor", low)
    if merged:
        expert_mine = kept(expert_mine, high, got_high[:, :width])
        expert_other = kept(expert_other, low, got_low[:, :width])
        got_high, got_low = got_high[:, width:], got_low[:, width:]
    else:
        for bit in t_bits[1:]:
            expert_mine = step(expert_mine, bit)
        for bit in t_bits[:-1][::-1]:
            expert_other = step(expert_other, bit)
    input_other = kept(input_other, high, got_high)
    input_mine = kept(input_mine, low, got_low)
    g_up_far, expert_mine, expert_other, input_mine, input_other, g_down_far, g_gate_far, *rest = fence(
        g_up_far, expert_mine[0], expert_other[0], input_mine, input_other, g_down_far, g_gate_far,
        *g_gate_own, *g_down_own, *g_up_own
    )
    g_gate_own, g_down_own, g_up_own = rest[:2], rest[2:4], rest[4:]

    g_up_own = shrink(*g_up_own)
    expert_got = z_far(expert_other)
    for bit in t_bits[1:]:
        input_mine = step(input_mine, bit)
    for bit in t_bits[:-1][::-1]:
        input_other = step(input_other, bit)
    input_mine, input_other, g_down_far, g_gate_far, *rest = fence(
        input_mine[0], input_other[0], g_down_far, g_gate_far, *g_down_own, *g_gate_own
    )
    down_mine, down_send = halves_of(done(*rest[:2]), g_down_far)
    gate_mine, gate_send = halves_of(done(*rest[2:]), g_gate_far)
    got = across(cat(down_send, gate_send))
    down_out, gate_out = panel(down_mine, got[:rows_w]), panel(gate_mine, got[rows_w:])
    up_mine, up_send = halves_of(done(*g_up_own), g_up_far)
    up_out = panel(up_mine, across(up_send))
    input_got = z_far(input_other)
    expert_cols = expert_mine.astype(F32) + expert_got.astype(F32)
    grad_cols = lax.dynamic_slice_in_dim(rows_grad, me_t * width, width, 1)
    weight_rows = jnp.sum(grad_cols.astype(F32) * expert_cols, axis=1)
    for bit in t_bits:
        weight_rows = weight_rows + swap(weight_rows, "tensor", bit)
    weight_grad = jnp.sum(jnp.where(match, weight_rows[:, None], 0.0), axis=0)
    mixed = mm_first(hot, (row_weight[:, None] * expert_cols).astype(BF16)).astype(BF16)
    input_cols = (input_mine.astype(F32) + input_got.astype(F32)).astype(BF16)
    input_grad = mm_first(hot, input_cols).astype(BF16)
    return (mixed, input_grad, weight_grad, gate_out, up_out, down_out)


def solution(mesh):
    return jax.shard_map(
        local,
        mesh=mesh,
        in_specs=(
            P("dp", None),
            P("dp", None),
            P("dp", None),
            P("dp", None),
            P("dp", "tensor"),
            P("dp", "tensor"),
            P("dp", "tensor"),
        ),
        out_specs=(
            P("dp", "tensor"),
            P("dp", "tensor"),
            P("dp"),
            P("dp", "tensor"),
            P("dp", "tensor"),
            P("dp", "tensor"),
        ),
        check_vma=False,
    )
```
